128 devices in a mesh: role: 8 (over z_hi, x), tp: 16 (over y, z_lo, core).
Axes of the slice: x: 4, y: 4, z: 4 (z_hi: 2, z_lo: 2; z = z_hi * 2 + z_lo), core: 2. Of those that a mesh axis runs over, the one named last changes fastest.
Arguments:
- text_embed: bfloat16 [8192, 8192], P('role', 'tp')
- vision_rows: bfloat16 [2048, 8192], P('role', 'tp'), may hold values from -6 to 6
- vision_group: int32 [2048], P('role'), may hold values from 0 to 7, as said below
- vision_slot: int32 [2048], P('role'), may hold values from 0 to 1023, as said below
- request_blocks: int32 [8, 8], P('role'), may hold values from 1 to 32, as said below
- ship_page: int32 [512], P('role'), may hold values from 0 to 16383, as said below
- paged_cache: bfloat16 [16384, 16, 2048], P(('role', 'tp')), may hold values from -6 to 6
- block_table: int32 [128, 256], P('role'), may hold values from -1 to 16383, as said below
- cache_len: int32 [128], P('role'), may hold values from 0 to 4096
- step_embed: bfloat16 [4, 128, 8192], P(None, 'role', 'tp')
- norm_gain: bfloat16 [8192], replicated, may hold values from 0.25 to 1.75
- query_weight: bfloat16 [8192, 8192], P(None, 'tp')
- keyvalue_weight: bfloat16 [8192, 2048], P(None, 'tp')
Outputs:
- prefill_out: bfloat16 [8192, 8192], P('role', 'tp')
- decode_out: bfloat16 [4, 128, 8192], P(None, 'role', 'tp')
The draws below stay inside these ranges and needn't reach their ends.
Inputs may be any that keep to these rules, and one draw needn't show every extreme that they name: `vision_group`: of one group's 256 image rows at most 64 go to any one group, and one group receives exactly 64 from every group. `vision_slot`: image rows sent to one group have distinct positions. `request_blocks`: each row sums to 64; each group has one request of exactly 32 pages. `ship_page`: all named pages are distinct. Device number role * 16 + tp holds 128 consecutive pages. All pages of one request go to one group, and the requests of one group go to distinct groups (possibly its own), and of one group's 64 pages at most 2 go to any one device. `block_table`: rows of group h name only pages h * 2048 to (h + 1) * 2048 - 1, each of them exactly once over the group's rows; row r names its pages in order in its first ceil(cache_len[r] / 16) entries and -1 after them.
All inputs are finite; a program needn't handle non-finite values.
Results may differ from the reference program's by a relative error of at most 0.0055.
The reference program's roundings to bfloat16 on the way count: a program that leaves them out, or rounds other values in their place, can miss the bound.
Values may be sent and summed in bfloat16 or wider, within the bound.
No kernel may reach another device: no remote copies, remote signals or barrier semaphores. Data moves between devices by JAX's collectives and lax.ppermute only.
A program may use at most 256 MiB of HBM per device.

```python
import math
import jax
import jax.numpy as jnp
from jax import lax

MODEL_DIM = 8192
QUERY_HEADS = 64
KEYVALUE_HEADS = 8
HEAD_SIZE = 128
GROUP_TOKENS = 1024
VIS = 256
PAGE_TOKENS = 16
DECODE_BATCH = 16
PAGES_DEV = 128
DECODE_STEPS = 4
PREFILL_PAGES = 64
GROUP_PAGE_COUNT = 2048
TABLE_ENTRIES = 256
N_ROLE = 8
N_TP = 16


def spread_scales(scale_key, values):
    row_key, column_key = jax.random.split(scale_key)
    row_scale = jnp.exp(jax.random.uniform(row_key, values.shape[:-1] + (1,), jnp.float32, 0.0, math.log(10.0)))
    column_scale = jnp.exp(jax.random.uniform(column_key, (values.shape[-1],), jnp.float32, 0.0, math.log(10.0)))
    return values * row_scale * column_scale


def draw_text_embed(key, part):
    key = jax.random.fold_in(key, 707)
    value_key, scale_key = jax.random.split(key)
    full_shape = (N_ROLE * GROUP_TOKENS, MODEL_DIM)
    values = jax.random.normal(value_key, full_shape, jnp.float32)
    return spread_scales(scale_key, values).astype(jnp.bfloat16)


def draw_step_embed(key, part):
    key = jax.random.fold_in(key, 808)
    value_key, scale_key = jax.random.split(key)
    full_shape = (DECODE_STEPS, N_ROLE * DECODE_BATCH, MODEL_DIM)
    values = jax.random.normal(value_key, full_shape, jnp.float32)
    return spread_scales(scale_key, values).astype(jnp.bfloat16)


def vision_plan(key):
    base_key = jax.random.fold_in(key, 101)
    full_key, row_key, place_key = jax.random.split(base_key, 3)
    capacity = 2 * VIS // N_ROLE
    slot_count = N_ROLE * capacity
    slot_dest = jnp.arange(slot_count, dtype=jnp.int32) // capacity
    favored = jax.random.randint(full_key, (), 0, N_ROLE, dtype=jnp.int32)

    def one_source(source_key):
        order_key, shuffle_key = jax.random.split(source_key)
        shuffled = jax.random.permutation(order_key, slot_count).astype(jnp.int32)
        priority = jnp.where(slot_dest == favored, shuffled, slot_count + shuffled)
        chosen = jnp.argsort(priority)[:VIS].astype(jnp.int32)
        return jax.random.permutation(shuffle_key, chosen) // capacity
    destinations = jax.vmap(one_source)(jax.random.split(row_key, N_ROLE)).astype(jnp.int32)
    dest_hits = (destinations[:, :, None] == jnp.arange(N_ROLE, dtype=jnp.int32)[None, None, :]).astype(jnp.int32)
    row_ranks = jnp.sum((jnp.cumsum(dest_hits, axis=1) - 1) * dest_hits, axis=2)
    positions = jax.vmap(lambda sub_key: jax.random.permutation(sub_key, GROUP_TOKENS))(jax.random.split(place_key, N_ROLE)).astype(jnp.int32)
    sources = jnp.arange(N_ROLE, dtype=jnp.int32)[:, None]
    target_slot = positions[destinations, sources * capacity + row_ranks]
    return (destinations.reshape(-1), target_slot.reshape(-1).astype(jnp.int32))


def draw_vision_group(key, part):
    return vision_plan(key)[0]


def draw_vision_slot(key, part):
    return vision_plan(key)[1]


def request_plan(key):
    base_key = jax.random.fold_in(key, 202)
    unit_key, page_key = jax.random.split(base_key)
    blocks = GROUP_TOKENS // PAGE_TOKENS
    longest_blocks = blocks // 2
    spare_units = blocks - longest_blocks - (N_ROLE - 1)
    positions = jnp.arange(N_ROLE, dtype=jnp.int32)

    def one_group(group_key):
        pick_key, spread_key, send_key = jax.random.split(group_key, 3)
        longest = jax.random.randint(pick_key, (), 0, N_ROLE, dtype=jnp.int32)
        unit_rows = jax.random.randint(spread_key, (spare_units,), 0, N_ROLE - 1, dtype=jnp.int32)
        others = 1 + jnp.sum((unit_rows[:, None] == jnp.arange(N_ROLE - 1, dtype=jnp.int32)[None, :]).astype(jnp.int32), axis=0)
        other_index = jnp.clip(positions - (positions > longest).astype(jnp.int32), 0, N_ROLE - 2)
        lengths = jnp.where(positions == longest, longest_blocks, others[other_index])
        targets = jax.random.permutation(send_key, N_ROLE).astype(jnp.int32)
        return (lengths.astype(jnp.int32), targets)
    lengths, targets = jax.vmap(one_group)(jax.random.split(unit_key, N_ROLE))
    request_ends = jnp.cumsum(lengths, axis=1)
    starts = request_ends - lengths
    block_ids = jnp.arange(blocks, dtype=jnp.int32)
    request = jnp.sum((block_ids[None, :, None] >= request_ends[:, None, :]).astype(jnp.int32), axis=2)
    block_rank = block_ids[None, :] - jnp.take_along_axis(starts, request, axis=1)
    dest_group = jnp.take_along_axis(targets, request, axis=1)
    column = block_rank % N_TP
    depth_level = block_rank // N_TP
    device = dest_group * N_TP + column
    layouts = jax.vmap(lambda sub_key: jax.random.permutation(sub_key, PAGES_DEV))(jax.random.split(page_key, N_ROLE * N_TP)).astype(jnp.int32)
    capacity = blocks // (2 * N_TP)
    sources = jnp.arange(N_ROLE, dtype=jnp.int32)[:, None]
    local_page = layouts[device, sources * capacity + depth_level]
    page_ids = device * PAGES_DEV + local_page
    return (lengths, page_ids.reshape(-1).astype(jnp.int32))


def draw_request_blocks(key, part):
    return request_plan(key)[0]


def draw_ship_page(key, part):
    return request_plan(key)[1]


def table_plan(key):
    base_key = jax.random.fold_in(key, 303)
    group_pages = PAGES_DEV * N_TP
    mean_pages = group_pages // DECODE_BATCH
    widest = 2 * mean_pages

    def one_group(group_index):
        group_key = jax.random.fold_in(base_key, group_index)
        pair_key, size_key, page_key, trim_key = jax.random.split(group_key, 4)
        row_order = jax.random.permutation(pair_key, DECODE_BATCH).astype(jnp.int32)
        change = jax.random.randint(size_key, (DECODE_BATCH // 2,), 0, mean_pages, dtype=jnp.int32)
        change = change.at[0].set(mean_pages)
        counts = jnp.zeros((DECODE_BATCH,), jnp.int32).at[row_order[0::2]].set(mean_pages + change).at[row_order[1::2]].set(mean_pages - change)
        offsets = jnp.cumsum(counts) - counts
        page_order = jax.random.permutation(page_key, group_pages).astype(jnp.int32)
        entry_ids = jnp.arange(widest, dtype=jnp.int32)
        position = jnp.clip(offsets[:, None] + entry_ids[None, :], 0, group_pages - 1)
        page_table = jnp.where(entry_ids[None, :] < counts[:, None], group_index * group_pages + page_order[position], -1)
        trimmed = jax.random.randint(trim_key, (DECODE_BATCH,), 0, PAGE_TOKENS, dtype=jnp.int32)
        trimmed = jnp.where(counts == widest, 0, trimmed)
        length = jnp.maximum(counts * PAGE_TOKENS - trimmed, 0)
        return (page_table.astype(jnp.int32), length.astype(jnp.int32))
    page_table, length = jax.vmap(one_group)(jnp.arange(N_ROLE, dtype=jnp.int32))
    return (page_table.reshape(N_ROLE * DECODE_BATCH, widest), length.reshape(-1))


def draw_block_table(key, part):
    return table_plan(key)[0]


def draw_cache_len(key, part):
    return table_plan(key)[1]


def draw_query_weight(key, part):
    key = jax.random.fold_in(key, 505)
    blend_weight = jax.random.normal(key, (MODEL_DIM, QUERY_HEADS, HEAD_SIZE), jnp.float32) * MODEL_DIM ** (-0.5)
    return blend_weight.reshape(MODEL_DIM, QUERY_HEADS * HEAD_SIZE).astype(jnp.bfloat16)


def draw_keyvalue_weight(key, part):
    key = jax.random.fold_in(key, 606)
    blend_weight = jax.random.normal(key, (MODEL_DIM, KEYVALUE_HEADS, 2, HEAD_SIZE), jnp.float32) * MODEL_DIM ** (-0.5)
    return blend_weight.reshape(MODEL_DIM, KEYVALUE_HEADS * 2 * HEAD_SIZE).astype(jnp.bfloat16)


def levels(key, shape, cuts, low, top_value):
    loudness = 1.0
    for dim, parts in cuts:
        steps = jax.random.uniform(jax.random.fold_in(jax.random.fold_in(key, 6), dim), (parts,), jnp.float32, low / len(cuts), top_value / len(cuts))
        loudness = loudness * jnp.repeat(jnp.exp(steps), shape[dim] // parts).reshape((-1,) + (1,) * (len(shape) - 1 - dim))
    return loudness


def normal_values(key, shape, scale, reach, cuts=(), held_as=jnp.bfloat16):
    values = scale * jax.random.normal(key, shape, jnp.float32)
    if cuts:
        values = values * levels(key, shape, cuts, -0.22, 0.18)
    return jnp.clip(values, -reach, reach).astype(held_as)


def setup_inputs(seed: int = 0) -> dict:
    streams_of = jax.random.split(jax.random.key(seed), 14)
    return {
        "text_embed": draw_text_embed(jax.random.fold_in(streams_of[13], 71), 0),
        "vision_rows": normal_values(streams_of[1], (N_ROLE * VIS, MODEL_DIM), 1.0, 6.0, ((0, 8), (1, 16))),
        "vision_group": draw_vision_group(jax.random.fold_in(streams_of[13], 71), 0),
        "vision_slot": draw_vision_slot(jax.random.fold_in(streams_of[13], 71), 0),
        "request_blocks": draw_request_blocks(jax.random.fold_in(streams_of[13], 71), 0),
        "ship_page": draw_ship_page(jax.random.fold_in(streams_of[13], 71), 0),
        "paged_cache": normal_values(streams_of[6], (N_ROLE * GROUP_PAGE_COUNT, PAGE_TOKENS, 2 * KEYVALUE_HEADS * HEAD_SIZE), 1.0, 6.0, ((0, 128),)),
        "block_table": draw_block_table(jax.random.fold_in(streams_of[13], 71), 0),
        "cache_len": draw_cache_len(jax.random.fold_in(streams_of[13], 71), 0),
        "step_embed": draw_step_embed(jax.random.fold_in(streams_of[13], 71), 0),
        "norm_gain": jnp.clip(1.0 + 0.15 * jax.random.normal(streams_of[10], (MODEL_DIM,), jnp.float32), 0.25, 1.75).astype(jnp.bfloat16),
        "query_weight": draw_query_weight(jax.random.fold_in(streams_of[13], 71), 0),
        "keyvalue_weight": draw_keyvalue_weight(jax.random.fold_in(streams_of[13], 71), 0),
    }


epsilon = 1e-06
masked_score = -1e+30

def rms_rows(row_block, norm_gain):
    widened = row_block.astype(jnp.float32)
    mean_square = lax.optimization_barrier(jnp.mean(widened * widened, axis=-1, keepdims=True))
    return (widened * lax.rsqrt(mean_square + epsilon) * norm_gain.astype(jnp.float32)).astype(jnp.bfloat16)

def reference(text_embed, vision_rows, vision_group, vision_slot, request_blocks, ship_page, paged_cache, block_table, cache_len, step_embed, norm_gain, query_weight, keyvalue_weight):
    score_scale = HEAD_SIZE ** (-0.5)
    group_extent = QUERY_HEADS // KEYVALUE_HEADS
    target_rows = (vision_group * GROUP_TOKENS + vision_slot).astype(jnp.int32)
    merged = text_embed.at[target_rows].set(vision_rows)
    group_rows = merged.reshape(N_ROLE, GROUP_TOKENS, MODEL_DIM)
    request_ends = jnp.cumsum(request_blocks * PAGE_TOKENS, axis=1).astype(jnp.int32)

    def prefill_group(packed):
        row_block, group_ends = packed
        normed = rms_rows(row_block, norm_gain)
        query_block = jnp.dot(normed, query_weight, preferred_element_type=jnp.float32).astype(jnp.bfloat16)
        keyvalue_pairs = jnp.dot(normed, keyvalue_weight, preferred_element_type=jnp.float32).astype(jnp.bfloat16)
        positions = jnp.arange(GROUP_TOKENS, dtype=jnp.int32)
        segment = lax.optimization_barrier(jnp.sum((positions[:, None] >= group_ends[None, :]).astype(jnp.int32), axis=1))
        allowed = (segment[:, None] == segment[None, :]) & (positions[None, :] <= positions[:, None])
        query_head_rows = query_block.reshape(GROUP_TOKENS, KEYVALUE_HEADS, group_extent, HEAD_SIZE).transpose(1, 2, 0, 3)
        keyvalue_heads = keyvalue_pairs.reshape(GROUP_TOKENS, KEYVALUE_HEADS, 2, HEAD_SIZE).transpose(1, 2, 0, 3)

        def one_head(head_pair):
            query_heads, pair_rows = head_pair
            scores = jnp.einsum('gcd,ud->gcu', query_heads.astype(jnp.float32), pair_rows[0].astype(jnp.float32)) * score_scale
            scores = jnp.where(allowed[None], scores, masked_score)
            row_top = lax.optimization_barrier(jnp.max(scores, axis=-1, keepdims=True))
            weights = jnp.exp(scores - row_top)
            weights = (weights / lax.optimization_barrier(jnp.sum(weights, axis=-1, keepdims=True))).astype(jnp.bfloat16)
            attended = jnp.einsum('gcu,ud->cgd', weights.astype(jnp.float32), pair_rows[1].astype(jnp.float32))
            return attended.astype(jnp.bfloat16)
        head_outputs = lax.map(one_head, (query_head_rows, keyvalue_heads))
        return (head_outputs.transpose(1, 0, 2, 3).reshape(GROUP_TOKENS, QUERY_HEADS * HEAD_SIZE), keyvalue_pairs)
    prefill_rows, group_keyvalue = lax.map(prefill_group, (group_rows, request_ends))
    prefill_out = prefill_rows.reshape(N_ROLE * GROUP_TOKENS, QUERY_HEADS * HEAD_SIZE)
    sent_pages = group_keyvalue.reshape(N_ROLE * PREFILL_PAGES, PAGE_TOKENS, 2 * KEYVALUE_HEADS * HEAD_SIZE)
    cache_store = paged_cache.at[ship_page].set(sent_pages)
    step_normed = rms_rows(step_embed, norm_gain).reshape(DECODE_STEPS * N_ROLE * DECODE_BATCH, MODEL_DIM)
    step_query_rows = jnp.dot(step_normed, query_weight, preferred_element_type=jnp.float32).astype(jnp.bfloat16)
    step_keyvalue = jnp.dot(step_normed, keyvalue_weight, preferred_element_type=jnp.float32).astype(jnp.bfloat16)
    step_query_rows = step_query_rows.reshape(DECODE_STEPS, N_ROLE * DECODE_BATCH, KEYVALUE_HEADS, group_extent, HEAD_SIZE).transpose(1, 0, 2, 3, 4)
    step_keyvalue = step_keyvalue.reshape(DECODE_STEPS, N_ROLE * DECODE_BATCH, KEYVALUE_HEADS, 2, HEAD_SIZE).transpose(1, 0, 2, 3, 4)

    def decode_row(packed):
        table_row, length, row_queries, new_pairs = packed
        cache_reads = cache_store[jnp.maximum(table_row, 0)].reshape(TABLE_ENTRIES * PAGE_TOKENS, KEYVALUE_HEADS, 2, HEAD_SIZE)
        all_pairs = jnp.concatenate([cache_reads, new_pairs], axis=0)
        cache_positions = jnp.arange(TABLE_ENTRIES * PAGE_TOKENS, dtype=jnp.int32)
        live_cache = jnp.broadcast_to((cache_positions < length)[None, :], (DECODE_STEPS, TABLE_ENTRIES * PAGE_TOKENS))
        step_ids = jnp.arange(DECODE_STEPS, dtype=jnp.int32)
        live_new = step_ids[None, :] <= step_ids[:, None]
        live_tokens = jnp.concatenate([live_cache, live_new], axis=1)
        scores = jnp.einsum('skgd,tkd->skgt', row_queries.astype(jnp.float32), all_pairs[:, :, 0].astype(jnp.float32)) * score_scale
        scores = jnp.where(live_tokens[:, None, None, :], scores, masked_score)
        row_top = lax.optimization_barrier(jnp.max(scores, axis=-1, keepdims=True))
        decode_exp = jnp.where(live_tokens[:, None, None, :], jnp.exp(scores - row_top), 0.0)
        denominator = lax.optimization_barrier(jnp.sum(decode_exp, axis=-1))
        attended = jnp.einsum('skgt,tkd->skgd', decode_exp.astype(jnp.bfloat16).astype(jnp.float32), all_pairs[:, :, 1].astype(jnp.float32))
        return (attended / denominator[..., None]).astype(jnp.bfloat16).reshape(DECODE_STEPS, QUERY_HEADS * HEAD_SIZE)
    decode_rows = lax.map(decode_row, (block_table, cache_len, step_query_rows, step_keyvalue))
    decode_out = decode_rows.transpose(1, 0, 2)
    return (prefill_out, decode_out)
```

```python
import jax
import jax.numpy as jnp
from jax import lax
from jax.experimental import pallas as pl
from jax.experimental.pallas import tpu as pltpu
from jax.sharding import PartitionSpec as P

HEAD_SIZE = 128
KV_HEADS = 8
PAGE_TOKENS = 16
EPS = 1e-06
LOW = -1e30
SCALE = HEAD_SIZE ** (-0.5)
BF = jnp.bfloat16
F32 = jnp.float32
VMEM_LIMIT = 56 * 2**20
TP = 16
ROLE = 8
STAT_ROWS = 16

CORE = 1
ZLO = 2
Y1 = 4
Y3 = 12


def params(**more):
    return pltpu.CompilerParams(vmem_limit_bytes=VMEM_LIMIT, **more)


def vmem():
    return pl.BlockSpec(memory_space=pltpu.VMEM)


def smem():
    return pl.BlockSpec(memory_space=pltpu.SMEM)


def hbm():
    return pl.BlockSpec(memory_space=pl.ANY)


def swap(x, axis, mask):
    size = TP if axis == "tp" else ROLE
    return lax.ppermute(x, axis, [(i, i ^ mask) for i in range(size)])


def ring_y(x):
    return lax.ppermute(
        x, "tp", [(i, (i + 4) % TP if i % 2 == 0 else (i - 4) % TP) for i in range(TP)]
    )


def doubling(x, axis, masks):
    held = x[None]
    for mask in masks:
        held = jnp.concatenate([held, swap(held, axis, mask)], axis=0)
    return held


def offsets(masks):
    table = [0]
    for mask in masks:
        table = table + [v ^ mask for v in table]
    return table


TP_MASKS = (CORE, ZLO, Y1, Y3)
ROLE_MASKS = (4, 1, 3)
TP_OFFSETS = offsets(TP_MASKS)
ROLE_OFFSETS = offsets(ROLE_MASKS)


def nt_dot(a, b):
    return lax.dot_general(a, b, (((1,), (1,)), ((), ())), preferred_element_type=F32)


def nn_dot(a, b):
    return jnp.dot(a, b, preferred_element_type=F32)


def eye(n):
    return lax.broadcasted_iota(jnp.int32, (n, n), 0) == lax.broadcasted_iota(
        jnp.int32, (n, n), 1
    )


def to_row(column):
    n = column.shape[0]
    return jnp.sum(jnp.where(eye(n), column, 0.0), axis=0, keepdims=True)


def to_column(row):
    n = row.shape[1]
    return jnp.sum(jnp.where(eye(n), row, 0.0), axis=1, keepdims=True)


def split3(x):
    high = x.astype(BF)
    rest = x - high.astype(F32)
    middle = rest.astype(BF)
    low = (rest - middle.astype(F32)).astype(BF)
    return high, middle, low


def stat_block(lse_column):
    row = to_row(lse_column)
    parts = jnp.concatenate(
        [row[:, :128], row[:, 128:], jnp.zeros((6, 128), F32)], axis=0
    )
    high, middle, low = split3(parts)
    return jnp.concatenate(
        [
            high[:2].astype(F32),
            middle[:2].astype(F32),
            low[:2].astype(F32),
            jnp.zeros((10, 128), F32),
        ],
        axis=0,
    ).astype(BF)


def stat_column(block):
    wide = block.astype(F32)
    rows = wide[0:2] + wide[2:4] + wide[4:6]
    return jnp.concatenate([to_column(rows[0:1]), to_column(rows[1:2])], axis=0)


def step_kernel(order, xs, gain, wq, wa, wb, q_out, a_out, b_out, scale, acc):
    i = pl.program_id(0)

    @pl.when(i == 0)
    def _():
        total = jnp.zeros((xs.shape[1], 1), F32)
        for k in range(TP):
            wide = xs[k].astype(F32)
            total = total + jnp.sum(wide * wide, axis=1, keepdims=True)
        scale[...] = jnp.broadcast_to(
            lax.rsqrt(total / (TP * xs.shape[2]) + EPS), scale.shape
        )
        acc[...] = jnp.zeros_like(acc)

    normed = (xs[i].astype(F32) * scale[:, :1] * gain[0].astype(F32)).astype(BF)
    acc[:, :512] += nn_dot(normed, wq[...])
    acc[:, 512:640] += nn_dot(normed, wa[...])
    acc[:, 640:768] += nn_dot(normed, wb[...])

    @pl.when(i == TP - 1)
    def _():
        q_out[...] = acc[:, :512].astype(BF)
        a_out[...] = acc[:, 512:640].astype(BF)
        b_out[...] = acc[:, 640:768].astype(BF)


def step_project(order, xs, gain, wq, wa, wb):
    rows = xs.shape[1]
    return pl.pallas_call(
        step_kernel,
        grid_spec=pltpu.PrefetchScalarGridSpec(
            num_scalar_prefetch=1,
            grid=(TP,),
            in_specs=[
                pl.BlockSpec(xs.shape, lambda i, o: (0, 0, 0)),
                pl.BlockSpec((1, 1, 512), lambda i, o: (o[i], 0, 0)),
                pl.BlockSpec((512, 512), lambda i, o: (o[i], 0)),
                pl.BlockSpec((512, 128), lambda i, o: (o[i], 0)),
                pl.BlockSpec((512, 128), lambda i, o: (o[i], 0)),
            ],
            out_specs=[
                pl.BlockSpec((rows, 512), lambda i, o: (0, 0)),
                pl.BlockSpec((rows, 128), lambda i, o: (0, 0)),
                pl.BlockSpec((rows, 128), lambda i, o: (0, 0)),
            ],
            scratch_shapes=[pltpu.VMEM((rows, 128), F32), pltpu.VMEM((rows, 768), F32)],
        ),
        out_shape=[
            jax.ShapeDtypeStruct((rows, 512), BF),
            jax.ShapeDtypeStruct((rows, 128), BF),
            jax.ShapeDtypeStruct((rows, 128), BF),
        ],
        compiler_params=params(),
        cost_estimate=pl.CostEstimate(
            flops=2 * rows * 8192 * 768, bytes_accessed=14 * 2**20, transcendentals=0
        ),
        name="step_project",
    )(order, xs, gain.reshape(TP, 1, 512), wq, wa, wb)


def project_kernel(first, last, counts, *refs):
    blocks = sum(counts)
    refs = list(refs)
    index = refs.pop(0)
    core = refs.pop(0)
    tops = [refs.pop(0) for _ in counts]
    lows = [refs.pop(0) for _ in counts]
    ssq, gain, wq, wa, wb = [refs.pop(0) for _ in range(5)]
    acc_in = None if first else refs.pop(0)
    if last:
        q_out, k_out, v_out = [refs.pop(0) for _ in range(3)]
    else:
        acc_out = refs.pop(0)
    xbuf, wbuf, acc, scale, xsem, wsem, asem = refs
    half = xbuf.shape[2]

    copies = []
    place = 0
    for top, low, count in zip(tops, lows, counts):
        for n in range(count):
            start = pl.multiple_of(index[place] * 512, 512)
            rows = pl.ds(start, 512)
            here = [
                pltpu.make_async_copy(top.at[n], xbuf.at[place, 0], xsem.at[place, 0]),
                pltpu.make_async_copy(low.at[n], xbuf.at[place, 1], xsem.at[place, 1]),
                pltpu.make_async_copy(
                    wq.at[rows], wbuf.at[place, :, pl.ds(0, 512)], wsem.at[place, 0]
                ),
                pltpu.make_async_copy(
                    wa.at[rows], wbuf.at[place, :, pl.ds(512, 128)], wsem.at[place, 1]
                ),
                pltpu.make_async_copy(
                    wb.at[rows], wbuf.at[place, :, pl.ds(640, 128)], wsem.at[place, 2]
                ),
            ]
            for copy in here:
                copy.start()
            copies.append(here)
            place += 1
    if not first:
        load = pltpu.make_async_copy(acc_in, acc, asem.at[0])
        load.start()

    total = jnp.zeros((8, 128), F32)
    for k in range(TP):
        wide = ssq[k].astype(F32)
        total = total + (wide[0:8] + wide[8:16] + wide[16:24])
    factor = lax.rsqrt(total / (TP * 512) + EPS)
    for n in range(8):
        scale[n * 128 : (n + 1) * 128, :] = jnp.broadcast_to(
            to_column(factor[n : n + 1]), (128, 128)
        )
    if not first:
        load.wait()

    for place in range(blocks):
        for copy in copies[place]:
            copy.wait()
        gain_row = gain[index[place]].astype(F32)
        weights = wbuf.at[place]

        def tile(n, carry, place=place, gain_row=gain_row, weights=weights):
            part = n // (half // 256)
            at = pl.multiple_of((n % (half // 256)) * 256, 256)
            row = pl.multiple_of(n * 256, 256)
            x = xbuf[place, part, pl.ds(at, 256), :].astype(F32)
            normed = (x * scale[pl.ds(row, 256), :1] * gain_row).astype(BF)
            product = nn_dot(normed, weights[...])
            if first and place == 0:
                acc[pl.ds(row, 256), :] = product
            else:
                acc[pl.ds(row, 256), :] += product
            return carry

        lax.fori_loop(0, 2 * half // 256, tile, 0)

    if last:
        q_out[...] = acc[:, :512].astype(BF)
        own = acc[:, 512:640]
        other = acc[:, 640:768]
        k_out[...] = jnp.where(core[0] == 0, own, other).astype(BF)
        v_out[...] = jnp.where(core[0] == 0, other, own).astype(BF)
    else:
        store = pltpu.make_async_copy(acc, acc_out, asem.at[0])
        store.start()
        store.wait()


def project(index, core, tops, lows, ssq, gain, wq, wa, wb, acc, last):
    first = acc is None
    counts = tuple(a.shape[0] for a in tops)
    blocks = sum(counts)
    half = tops[0].shape[1]
    rows = 2 * half
    args = [index, core, *tops, *lows, ssq, gain.reshape(TP, 1, 512), wq, wa, wb]
    specs = [smem(), smem()] + [hbm()] * (2 * len(counts)) + [vmem(), vmem()] + [hbm()] * 3
    if not first:
        args.append(acc)
        specs.append(hbm())
    if last:
        shapes = [
            jax.ShapeDtypeStruct((rows, 512), BF),
            jax.ShapeDtypeStruct((rows, 128), BF),
            jax.ShapeDtypeStruct((rows, 128), BF),
        ]
        out_specs = [vmem()] * 3
    else:
        shapes = jax.ShapeDtypeStruct((rows, 768), F32)
        out_specs = hbm()

    def body(*refs):
        project_kernel(first, last, counts, *refs)

    return pl.pallas_call(
        body,
        in_specs=specs,
        out_specs=out_specs,
        out_shape=shapes,
        scratch_shapes=[
            pltpu.VMEM((blocks, 2, half, 512), BF),
            pltpu.VMEM((blocks, 512, 768), BF),
            pltpu.VMEM((rows, 768), F32),
            pltpu.VMEM((rows, 128), F32),
            pltpu.SemaphoreType.DMA((blocks, 2)),
            pltpu.SemaphoreType.DMA((blocks, 3)),
            pltpu.SemaphoreType.DMA((1,)),
        ],
        compiler_params=params(),
        cost_estimate=pl.CostEstimate(
            flops=2 * rows * 512 * blocks * 768,
            bytes_accessed=blocks * 2 * 2**20,
            transcendentals=0,
        ),
        name="prefill_project",
    )(*args)


def paged_kernel(first_chunk, slot_page, slot_live, where, q, cache, out, kv, top, total, acc, lse):
    lane = lax.broadcasted_iota(jnp.int32, (1, 128), 1)

    def one_row(r, carry):
        top[...] = jnp.full_like(top, LOW)
        total[...] = jnp.zeros_like(total)
        acc[...] = jnp.zeros_like(acc)
        at = pl.multiple_of(r * 16, 16)

        def one_chunk(i, inner):
            live = jnp.zeros((1, 128), jnp.int32)
            for j in range(8):
                slot = i * 8 + j
                kv[j * 16 : (j + 1) * 16, :] = cache[slot_page[slot]]
                live = jnp.where(lane // PAGE_TOKENS == j, slot_live[slot], live)
            valid = lane % PAGE_TOKENS < live
            for k in range(KV_HEADS):
                keys = kv[:, k * 256 : k * 256 + 128]
                values = kv[:, k * 256 + 128 : k * 256 + 256]
                queries = jnp.concatenate(
                    [
                        q[where[2 * k], pl.ds(at, 16), :],
                        q[where[2 * k + 1], pl.ds(at, 16), :],
                    ],
                    axis=0,
                )
                rows = slice(k * 32, (k + 1) * 32)
                scores = jnp.where(valid, nt_dot(queries, keys) * SCALE, LOW)
                old = top[rows, :]
                new = jnp.maximum(old, jnp.max(scores, axis=1, keepdims=True))
                weights = jnp.where(valid, jnp.exp(scores - new), 0.0)
                fade = jnp.exp(old - new)
                top[rows, :] = new
                total[rows, :] = total[rows, :] * fade + jnp.sum(weights, axis=1, keepdims=True)
                acc[rows, :] = acc[rows, :] * fade + nn_dot(weights.astype(BF), values)
            return inner

        lax.fori_loop(first_chunk[r], first_chunk[r + 1], one_chunk, 0)
        some = total[...] > 0.0
        divisor = jnp.where(some, total[...], 1.0)
        result = (acc[...] / divisor).astype(BF)
        level = jnp.where(some, top[...] + jnp.log(divisor), LOW)
        for t in range(TP):
            out[t, pl.ds(at, 16), :] = result[t * 16 : (t + 1) * 16]
            lse[t, pl.ds(at, 16), :] = level[t * 16 : (t + 1) * 16]
        return carry

    lax.fori_loop(0, 16, one_row, 0)

    def one_target(t, carry):
        out[t, 256:272, :] = stat_block(lse[t][:, :1])
        return carry

    lax.fori_loop(0, TP, one_target, 0)


def paged_attention(first_chunk, slot_page, slot_live, where, q, cache):
    return pl.pallas_call(
        paged_kernel,
        in_specs=[smem()] * 4 + [vmem()] * 2,
        out_specs=vmem(),
        out_shape=jax.ShapeDtypeStruct((TP, 256 + STAT_ROWS, 128), BF),
        scratch_shapes=[
            pltpu.VMEM((128, 2048), BF),
            pltpu.VMEM((256, 128), F32),
            pltpu.VMEM((256, 128), F32),
            pltpu.VMEM((256, 128), F32),
            pltpu.VMEM((TP, 256, 128), F32),
        ],
        compiler_params=params(),
        cost_estimate=pl.CostEstimate(
            flops=2 * 10**9, bytes_accessed=12 * 2**20, transcendentals=2**20
        ),
        name="paged_attention",
    )(first_chunk, slot_page, slot_live, where, q, cache)


def fresh_kernel(group, q, keys, values, token_row, out):
    def one_group(i, carry):
        queries = q[i]
        row = lax.broadcasted_iota(jnp.int32, (256, 1), 0) // 16 + i * 16
        valid = token_row[...] == row
        scores = jnp.where(valid, nt_dot(queries, keys[...]) * SCALE, LOW)
        top = jnp.max(scores, axis=1, keepdims=True)
        weights = jnp.where(valid, jnp.exp(scores - top), 0.0)
        total = jnp.sum(weights, axis=1, keepdims=True)
        acc = nn_dot(weights.astype(BF), values[...])
        some = total > 0.0
        divisor = jnp.where(some, total, 1.0)
        target = group[i]
        out[target, :256, :] = (acc / divisor).astype(BF)
        out[target, 256:272, :] = stat_block(jnp.where(some, top + jnp.log(divisor), LOW))
        return carry

    lax.fori_loop(0, ROLE, one_group, 0)


def fresh_attention(group, q, keys, values, token_row):
    return pl.pallas_call(
        fresh_kernel,
        in_specs=[smem()] + [vmem()] * 4,
        out_specs=vmem(),
        out_shape=jax.ShapeDtypeStruct((ROLE, 256 + STAT_ROWS, 128), BF),
        compiler_params=params(),
        cost_estimate=pl.CostEstimate(
            flops=10**9, bytes_accessed=2 * 2**20, transcendentals=2**21
        ),
        name="fresh_attention",
    )(group, q, keys, values, token_row)


def prefill_kernel(q, keys, values, seg_row, out):
    rows = q.shape[0]
    for tile in range(rows // 256):
        high = (tile + 1) * 256
        low = max(0, (tile * 256 - 511) // 256 * 256)
        span = high - low
        seg_keys = seg_row[:, low:high]
        seg_queries = to_column(seg_row[:, tile * 256 : high])
        row = lax.broadcasted_iota(jnp.int32, (256, span), 0) + tile * 256
        column = lax.broadcasted_iota(jnp.int32, (256, span), 1) + low
        valid = (seg_keys == seg_queries) & (column <= row)
        for h in range(4):
            lanes = slice(h * 128, (h + 1) * 128)
            scores = nt_dot(q[tile * 256 : high, lanes], keys[low:high, :]) * SCALE
            scores = jnp.where(valid, scores, LOW)
            top = jnp.max(scores, axis=1, keepdims=True)
            weights = jnp.exp(scores - top)
            total = jnp.sum(weights, axis=1, keepdims=True)
            weights = (weights * (1.0 / total)).astype(BF)
            out[tile * 256 : high, lanes] = nn_dot(weights, values[low:high, :]).astype(BF)


def prefill_attention(q, keys, values, seg_row):
    return pl.pallas_call(
        prefill_kernel,
        in_specs=[vmem()] * 4,
        out_specs=vmem(),
        out_shape=jax.ShapeDtypeStruct(q.shape, BF),
        compiler_params=params(),
        cost_estimate=pl.CostEstimate(
            flops=3 * 10**9, bytes_accessed=3 * 2**20, transcendentals=3 * 2**20
        ),
        name="prefill_attention",
    )(q, keys, values, seg_row)


def merge_kernel(held, fresh, q, new_keys, new_values, out):
    queries = q[...]
    row = lax.broadcasted_iota(jnp.int32, (256, 64), 0)
    key = lax.broadcasted_iota(jnp.int32, (256, 64), 1)
    valid = (row // 16 == key % 16) & (key // 16 <= row % 16 // 4)
    scores = jnp.where(valid, nt_dot(queries, new_keys[...]) * SCALE, LOW)
    top = jnp.max(scores, axis=1, keepdims=True)
    levels = []
    for source, count in ((held, TP), (fresh, ROLE)):
        for n in range(count):
            levels.append(stat_column(source[n, 256:272, :]))
    for level in levels:
        top = jnp.maximum(top, level)
    weights = jnp.where(valid, jnp.exp(scores - top), 0.0)
    total = jnp.sum(weights, axis=1, keepdims=True)
    acc = nn_dot(weights.astype(BF), new_values[...])
    place = 0
    for source, count in ((held, TP), (fresh, ROLE)):
        for n in range(count):
            factor = jnp.exp(levels[place] - top)
            total = total + factor
            acc = acc + source[n, :256, :].astype(F32) * factor
            place += 1
    out[...] = (acc / total).astype(BF)


def merge(held, fresh, q, new_keys, new_values):
    return pl.pallas_call(
        merge_kernel,
        in_specs=[vmem()] * 5,
        out_specs=vmem(),
        out_shape=jax.ShapeDtypeStruct((256, 128), BF),
        compiler_params=params(),
        cost_estimate=pl.CostEstimate(
            flops=10**7, bytes_accessed=2 * 2**20, transcendentals=2**16
        ),
        name="decode_merge",
    )(held, fresh, q, new_keys, new_values)


def page_tables(block_table, cache_len, ships, first_page):
    pages = 128
    page_ids = jnp.arange(pages, dtype=jnp.int32)
    rows, entries = block_table.shape
    code_of = (
        jnp.arange(rows, dtype=jnp.int32)[:, None] * entries
        + jnp.arange(entries, dtype=jnp.int32)[None, :]
    )
    match = block_table[None] == (first_page + page_ids)[:, None, None]
    code = jnp.max(jnp.where(match, code_of[None], -1), axis=(1, 2))
    replaced = jnp.any(ships.reshape(1, -1) == (first_page + page_ids)[:, None], axis=1)
    row = jnp.where(replaced | (code < 0), rows, code // entries)
    onehot = row[:, None] == jnp.arange(rows, dtype=jnp.int32)[None, :]
    length = jnp.sum(jnp.where(onehot, cache_len[None, :], 0), axis=1)
    live = jnp.clip(length - (code % entries) * PAGE_TOKENS, 0, PAGE_TOKENS)
    count = jnp.sum(onehot.astype(jnp.int32), axis=0)
    chunks = (count + 7) // 8
    ids17 = jnp.arange(rows + 1, dtype=jnp.int32)
    ids16 = jnp.arange(rows, dtype=jnp.int32)
    first_chunk = jnp.sum(
        jnp.where(ids16[None, :] < ids17[:, None], chunks[None, :], 0), axis=1
    )
    rank = jnp.sum(
        ((row[None, :] == row[:, None]) & (page_ids[None, :] < page_ids[:, None])).astype(jnp.int32),
        axis=1,
    )
    base = jnp.sum(jnp.where(onehot, first_chunk[None, :rows], 0), axis=1)
    slot = jnp.where(row < rows, base * 8 + rank, -1)
    hit = slot[None, :] == jnp.arange(256, dtype=jnp.int32)[:, None]
    slot_page = jnp.sum(jnp.where(hit, page_ids[None, :], 0), axis=1)
    slot_live = jnp.sum(jnp.where(hit, live[None, :], 0), axis=1)
    return first_chunk, slot_page, slot_live


def token_rows(tables, lengths, ship_page):
    rows, entries = tables.shape
    code_of = (
        jnp.arange(rows, dtype=jnp.int32)[:, None] * entries
        + jnp.arange(entries, dtype=jnp.int32)[None, :]
    )
    match = tables[None] == ship_page[:, None, None]
    code = jnp.max(jnp.where(match, code_of[None], -1), axis=(1, 2))
    row = code // entries
    onehot = row[:, None] == jnp.arange(rows, dtype=jnp.int32)[None, :]
    length = jnp.sum(jnp.where(onehot, lengths[None, :], 0), axis=1)
    live = jnp.where(code >= 0, length - (code % entries) * PAGE_TOKENS, 0)
    token = jnp.arange(PAGE_TOKENS, dtype=jnp.int32)[None, :]
    return jnp.where(token < live[:, None], row[:, None], -1).reshape(1, -1)


def per_device(
    text_embed,
    vision_rows,
    vision_group,
    vision_slot,
    request_blocks,
    ship_page,
    paged_cache,
    block_table,
    cache_len,
    step_embed,
    norm_gain,
    query_weight,
    keyvalue_weight,
):
    column = lax.axis_index("tp")
    role = lax.axis_index("role")
    core = column % 2
    group_rows, width = text_embed.shape
    half = group_rows // 2
    steps, rows, _ = step_embed.shape

    meta = jnp.concatenate(
        [
            block_table.reshape(-1),
            cache_len,
            ship_page,
            jnp.zeros((48,), jnp.int32),
        ]
    ).reshape(33, 128)
    metas = doubling(meta, "role", ROLE_MASKS).reshape(ROLE, -1)
    tables = metas[:, :4096].reshape(ROLE * rows, -1)
    lengths = metas[:, 4096 : 4096 + rows].reshape(-1)
    ships = metas[:, 4112 : 4112 + 64]

    image_count = vision_rows.shape[0]
    capacity = 2 * image_count // ROLE
    dest_hits = vision_group[:, None] == jnp.arange(ROLE, dtype=jnp.int32)[None, :]
    running = jnp.cumsum(dest_hits.astype(jnp.int32), axis=0) - 1
    rank_of = jnp.sum(jnp.where(dest_hits, running, 0), axis=1)
    slot_ids = jnp.arange(ROLE * capacity, dtype=jnp.int32)
    picked = (vision_group * capacity + rank_of)[None, :] == slot_ids[:, None]
    outgoing = nn_dot(picked.astype(BF), vision_rows).astype(BF)
    out_slots = jnp.sum(jnp.where(picked, vision_slot[None, :] + 1, 0), axis=1) - 1
    slot_rows = jnp.stack([out_slots // 32, out_slots % 32], axis=0).astype(BF)
    slot_rows = jnp.broadcast_to(
        jnp.concatenate([slot_rows, jnp.zeros((14, ROLE * capacity), BF)], axis=0)[None],
        (ROLE, 16, ROLE * capacity),
    )
    message = jnp.concatenate([outgoing.reshape(ROLE, capacity, width), slot_rows], axis=1)
    arrived = lax.all_to_all(message, "role", split_axis=0, concat_axis=0, tiled=True)
    slot_parts = lax.dynamic_slice_in_dim(
        arrived[:, capacity : capacity + 2, :], role * capacity, capacity, 2
    ).astype(jnp.int32)
    arrived_slots = (slot_parts[:, 0] * 32 + slot_parts[:, 1]).reshape(1, -1)
    arrived_rows = arrived[:, :capacity, :].reshape(ROLE * capacity, width)
    positions = jnp.arange(group_rows, dtype=jnp.int32)

    def merged_rows(low, high):
        landing = positions[low:high, None] == arrived_slots
        placed = nn_dot(landing.astype(BF), arrived_rows).astype(BF)
        return jnp.where(jnp.any(landing, axis=1)[:, None], placed, text_embed[low:high])

    top_own = merged_rows(0, half)
    low_own = merged_rows(half, group_rows)

    def partial_squares(block):
        wide = block.astype(F32)
        return jnp.sum(wide * wide, axis=1)

    other_weight = swap(keyvalue_weight, "tp", CORE)
    tp_order = column ^ jnp.array(TP_OFFSETS, jnp.int32)
    steps_all = doubling(step_embed.reshape(steps * rows, width), "tp", TP_MASKS)
    step_q, step_a, step_b = step_project(
        tp_order, steps_all, norm_gain, query_weight, keyvalue_weight, other_weight
    )
    new_keys = jnp.where(core == 0, step_a, step_b)
    new_values = jnp.where(core == 0, step_b, step_a)
    own_queries = (
        step_q.reshape(steps, rows, 4, HEAD_SIZE).transpose(1, 0, 2, 3).reshape(rows * 16, HEAD_SIZE)
    )

    def plus(a):
        return swap(a, "tp", CORE)

    top_pair = jnp.stack([top_own, plus(top_own)])
    low_pair = jnp.stack([low_own, plus(low_own)])
    top_z_own = swap(top_own, "tp", ZLO)
    low_y = ring_y(low_pair)
    top_y = ring_y(top_pair)
    low_z_own = swap(low_own, "tp", ZLO)
    top_z = jnp.stack([top_z_own, plus(top_z_own)])
    low_z = jnp.stack([low_z_own, plus(low_z_own)])
    top_zy = ring_y(top_z)
    low_zy = swap(low_y, "tp", ZLO)
    far = ring_y(jnp.stack([low_y[0], top_y[0]]))
    top_zf_own = ring_y(top_zy[0])
    low_zf_own = swap(far[0], "tp", ZLO)
    far_other = plus(far)

    squares = jnp.concatenate([partial_squares(top_own), partial_squares(low_own)]).reshape(8, 128)
    reduced = lax.reduce_precision(squares, 8, 7)
    rest = squares - reduced
    reduced2 = lax.reduce_precision(rest, 8, 7)
    square_parts = jnp.concatenate(
        [reduced, reduced2, rest - reduced2, jnp.zeros((8, 128), F32)], axis=0
    ).astype(BF)
    query_message = jnp.concatenate([own_queries, square_parts], axis=0)
    query_all = doubling(query_message, "tp", TP_MASKS)
    ssq = query_all[:, 256:288, :]
    queries_role = doubling(own_queries, "role", ROLE_MASKS)

    y = column // 4
    low_bits = column % 4

    def at(dy, bits):
        return ((y + dy) % 4) * 4 + (low_bits ^ bits)

    toward = jnp.where(core == 0, -1, 1)
    index_1 = jnp.stack(
        [
            at(0, 0),
            at(0, 1),
            at(0, 2),
            at(0, 3),
            at(toward, 0),
            at(toward, 1),
            at(-toward, 1),
            at(-toward, 0),
        ]
    )
    index_2 = jnp.stack(
        [at(toward, 2), at(toward, 3), at(-toward, 3), at(-toward, 2), at(2, 0), at(2, 1)]
    )
    index_3 = jnp.stack([at(2, 2), at(2, 3)])
    core_id = core.reshape(1)
    weights = (norm_gain, query_weight, keyvalue_weight, other_weight)
    acc = project(
        index_1,
        core_id,
        [top_pair, top_z, top_y, plus(top_y)],
        [low_pair, low_z, low_y, plus(low_y)],
        ssq,
        *weights,
        None,
        False,
    )
    acc = project(
        index_2,
        core_id,
        [top_zy, plus(top_zy), far[1:], far_other[1:]],
        [low_zy, plus(low_zy), far[:1], far_other[:1]],
        ssq,
        *weights,
        acc,
        False,
    )
    q_rows, keys, values = project(
        index_3,
        core_id,
        [top_zf_own[None], plus(top_zf_own)[None]],
        [low_zf_own[None], plus(low_zf_own)[None]],
        ssq,
        *weights,
        acc,
        True,
    )

    first_page = (role * TP + column) * 128
    first_chunk, slot_page, slot_live = page_tables(block_table, cache_len, ships, first_page)
    difference = column ^ jnp.arange(TP, dtype=jnp.int32)
    far_bit = difference // 8
    near_bit = (difference // 4) % 2 ^ far_bit
    where = difference % 4 + 4 * near_bit + 8 * far_bit
    held = paged_attention(
        first_chunk, slot_page, slot_live, where, query_all[:, :256, :], paged_cache
    )
    held_parts = lax.all_to_all(held, "tp", split_axis=0, concat_axis=0, tiled=True)

    token_row = token_rows(tables, lengths, ship_page)
    role_order = role ^ jnp.array(ROLE_OFFSETS, jnp.int32)
    fresh = fresh_attention(role_order, queries_role, keys, values, token_row)
    fresh_parts = lax.all_to_all(fresh, "role", split_axis=0, concat_axis=0, tiled=True)

    request_ends = jnp.cumsum(request_blocks[0] * PAGE_TOKENS)
    segment = jnp.sum((positions[:, None] >= request_ends[None, :]).astype(F32), axis=1)
    prefill_out = prefill_attention(q_rows, keys, values, segment.reshape(1, -1))

    decode = merge(held_parts, fresh_parts, own_queries, new_keys, new_values)
    decode_out = (
        decode.reshape(rows, steps, 4, HEAD_SIZE).transpose(1, 0, 2, 3).reshape(steps, rows, 512)
    )
    return (prefill_out, decode_out)


def solution(mesh):
    in_specs = (
        P("role", "tp"),
        P("role", "tp"),
        P("role"),
        P("role"),
        P("role", None),
        P("role"),
        P(("role", "tp"), None, None),
        P("role", None),
        P("role"),
        P(None, "role", "tp"),
        P(),
        P(None, "tp"),
        P(None, "tp"),
    )
    out_specs = (P("role", "tp"), P(None, "role", "tp"))
    return jax.shard_map(
        per_device, mesh=mesh, in_specs=in_specs, out_specs=out_specs, check_vma=False
    )
```

```python
import jax
import jax.numpy as jnp
from jax import lax
from jax.experimental import pallas as pl
from jax.experimental.pallas import tpu as pltpu
from jax.sharding import PartitionSpec as P

HEAD_SIZE = 128
KV_HEADS = 8
PAGE_TOKENS = 16
EPS = 1e-06
LOW = -1e30
SCALE = HEAD_SIZE ** (-0.5)
BF = jnp.bfloat16
F32 = jnp.float32
EXP2_SCALE = SCALE * 1.4426950408889634
LN2 = 0.6931471805599453
TP = 16
ROLE = 8
STAT_ROWS = 16

CORE = 1
ZLO = 2
Y1 = 4
Y3 = 12


def params(mebibytes):
    return pltpu.CompilerParams(vmem_limit_bytes=mebibytes * 2**20)


def vmem():
    return pl.BlockSpec(memory_space=pltpu.VMEM)


def smem():
    return pl.BlockSpec(memory_space=pltpu.SMEM)


def hbm():
    return pl.BlockSpec(memory_space=pl.ANY)


def swap(x, axis, mask):
    size = TP if axis == "tp" else ROLE
    return lax.ppermute(x, axis, [(i, i ^ mask) for i in range(size)])


def ring_y(x):
    return lax.ppermute(
        x, "tp", [(i, (i + 4) % TP if i % 2 == 0 else (i - 4) % TP) for i in range(TP)]
    )


def doubling(x, axis, masks):
    held = x[None]
    for mask in masks:
        held = jnp.concatenate([held, swap(held, axis, mask)], axis=0)
    return held


def offsets(masks):
    table = [0]
    for mask in masks:
        table = table + [v ^ mask for v in table]
    return table


TP_MASKS = (ZLO, Y1, Y3, CORE)
ROLE_MASKS = (4, 1, 3)
TP_OFFSETS = offsets(TP_MASKS)
ROLE_OFFSETS = offsets(ROLE_MASKS)


def nt_dot(a, b):
    return lax.dot_general(a, b, (((1,), (1,)), ((), ())), preferred_element_type=F32)


def nn_dot(a, b):
    return jnp.dot(a, b, preferred_element_type=F32)


def eye(n):
    return lax.broadcasted_iota(jnp.int32, (n, n), 0) == lax.broadcasted_iota(
        jnp.int32, (n, n), 1
    )


def to_row(column):
    n = column.shape[0]
    return jnp.sum(jnp.where(eye(n), column, 0.0), axis=0, keepdims=True)


def to_column(row):
    n = row.shape[1]
    return jnp.sum(jnp.where(eye(n), row, 0.0), axis=1, keepdims=True)


def split3(x):
    high = x.astype(BF)
    rest = x - high.astype(F32)
    middle = rest.astype(BF)
    low = (rest - middle.astype(F32)).astype(BF)
    return high, middle, low


def stat_block(level):
    parts = jnp.concatenate(
        [to_row(level[:128]), to_row(level[128:]), jnp.zeros((6, 128), F32)], axis=0
    )
    high, middle, low = split3(parts)
    return jnp.concatenate(
        [
            high[:2].astype(F32),
            middle[:2].astype(F32),
            low[:2].astype(F32),
            jnp.zeros((10, 128), F32),
        ],
        axis=0,
    ).astype(BF)


def stat_rows(block):
    wide = block.astype(F32)
    return wide[0:2] + wide[2:4] + wide[4:6]


def pick_kernel(group, slot, rows, out):
    count = group.shape[1]
    capacity = 2 * count // ROLE
    onehot = group[...] == lax.broadcasted_iota(jnp.int32, (ROLE, 1), 0)
    before = lax.broadcasted_iota(jnp.int32, (count, count), 0) < lax.broadcasted_iota(
        jnp.int32, (count, count), 1
    )
    rank = nn_dot(onehot.astype(F32).astype(BF), before.astype(F32).astype(BF))
    rank = jnp.sum(jnp.where(onehot, rank, 0.0), axis=0, keepdims=True).astype(jnp.int32)
    place = group[...] * capacity + rank
    picked = place == lax.broadcasted_iota(jnp.int32, (ROLE * capacity, 1), 0)
    picked = picked.astype(F32).astype(BF)
    chosen = nn_dot(picked, rows[...]).astype(BF)
    code = slot[...] + 1
    line = lax.broadcasted_iota(jnp.int32, (16, 1), 0)
    codes = jnp.where(line == 0, code // 32, jnp.where(line == 1, code % 32, 0))
    codes = nt_dot(codes.astype(F32).astype(BF), picked).astype(BF)
    for g in range(ROLE):
        out[g, :capacity, :] = chosen[g * capacity : (g + 1) * capacity]
        out[g, capacity:, :] = codes


def pick_rows(group, slot, rows):
    count, width = rows.shape
    capacity = 2 * count // ROLE
    return pl.pallas_call(
        pick_kernel,
        in_specs=[vmem()] * 3,
        out_specs=vmem(),
        out_shape=jax.ShapeDtypeStruct((ROLE, capacity + 16, width), BF),
        compiler_params=params(16),
        cost_estimate=pl.CostEstimate(flops=2 * 10**8, bytes_accessed=2**20, transcendentals=0),
        name="pick_rows",
    )(group.reshape(1, count), slot.reshape(1, count), rows)


def land_kernel(role, own, other, text_own, text_other, top, low, squares):
    capacity = own.shape[1] - 16
    total = ROLE * capacity
    lane = lax.broadcasted_iota(jnp.int32, (1, total), 1)
    slots = jnp.zeros((1, total), F32)
    for s in range(ROLE):
        codes = own[s, capacity:, :].astype(F32)
        code = jnp.broadcast_to(codes[0:1] * 32.0 + codes[1:2], (8, total))
        shift = ((s + ROLE - role[0]) % ROLE) * capacity
        slots = jnp.where(lane // capacity == s, pltpu.roll(code, shift, 1)[0:1], slots)
    slots = slots.astype(jnp.int32) - 1
    sums = []
    for n in range(text_own.shape[0] // 256):
        row = lax.broadcasted_iota(jnp.int32, (256, 1), 0) + n * 256
        landing = jnp.where(row == slots, 1.0, 0.0)
        hit = jnp.sum(landing, axis=1, keepdims=True) > 0.0
        landing = landing.astype(BF)
        out, at = (top, n * 256) if n < 2 else (low, (n - 2) * 256)
        for place, (rows, text) in enumerate(((own, text_own), (other, text_other))):
            arrived = rows[:, :capacity, :].reshape(total, rows.shape[2])
            block = jnp.where(
                hit, nn_dot(landing, arrived), text[n * 256 : (n + 1) * 256, :].astype(F32)
            )
            out[place, at : at + 256, :] = block.astype(BF)
            if place == 0:
                sums.append(jnp.sum(block * block, axis=1, keepdims=True))
    lines = []
    for column in sums:
        wide = jnp.broadcast_to(column, (256, 128))
        lines += [to_row(wide[:128]), to_row(wide[128:])]
    high, middle, rest = split3(jnp.concatenate(lines, axis=0))
    squares[...] = jnp.concatenate(
        [high.astype(F32), middle.astype(F32), rest.astype(F32), jnp.zeros((8, 128), F32)], axis=0
    ).astype(BF)


def land_rows(role, own, other, text_own, text_other):
    rows, width = text_own.shape
    pair = jax.ShapeDtypeStruct((2, rows // 2, width), BF)
    return pl.pallas_call(
        land_kernel,
        in_specs=[smem()] + [vmem()] * 4,
        out_specs=[vmem()] * 3,
        out_shape=[pair, pair, jax.ShapeDtypeStruct((32, 128), BF)],
        compiler_params=params(24),
        cost_estimate=pl.CostEstimate(flops=10**9, bytes_accessed=6 * 2**20, transcendentals=0),
        name="land_rows",
    )(role, own, other, text_own, text_other)


def step_kernel(order, low, xs, gain, wq, wa, wb, q_out, a_out, b_out, scale, acc):
    i = pl.program_id(0)

    @pl.when(i == 0)
    def _():
        total = jnp.zeros((xs.shape[1], 512), F32)
        for k in range(TP):
            wide = xs[k].astype(F32)
            total = total + wide * wide
        total = jnp.sum(total, axis=1, keepdims=True)
        scale[...] = jnp.broadcast_to(
            lax.rsqrt(total / (TP * xs.shape[2]) + EPS), scale.shape
        )
        acc[...] = jnp.zeros_like(acc)

    factor = jnp.broadcast_to(scale[:, :1], (xs.shape[1], 512))
    total_q = acc[:, :512]
    total_a = acc[:, 512:640]
    total_b = acc[:, 640:768]
    for j in range(4):
        place = low[0] ^ j
        block = j // 2 + 2 * i + 8 * (j % 2)
        rows = pl.ds(pl.multiple_of(place * 512, 512), 512)
        normed = (xs[block].astype(F32) * factor * gain[0, place].astype(F32)).astype(BF)
        total_q = total_q + nn_dot(normed, wq[rows, :])
        total_a = total_a + nn_dot(normed, wa[rows, :])
        total_b = total_b + nn_dot(normed, wb[rows, :])
    acc[:, :512] = total_q
    acc[:, 512:640] = total_a
    acc[:, 640:768] = total_b

    @pl.when(i == 3)
    def _():
        q_out[...] = acc[:, :512].astype(BF)
        a_out[...] = acc[:, 512:640].astype(BF)
        b_out[...] = acc[:, 640:768].astype(BF)


def step_project(order, low, xs, gain, wq, wa, wb):
    rows = xs.shape[1]
    return pl.pallas_call(
        step_kernel,
        grid_spec=pltpu.PrefetchScalarGridSpec(
            num_scalar_prefetch=2,
            grid=(4,),
            in_specs=[
                pl.BlockSpec(xs.shape, lambda i, o, l: (0, 0, 0)),
                pl.BlockSpec((1, 4, 1, 512), lambda i, o, l: (o[i], 0, 0, 0)),
                pl.BlockSpec((2048, 512), lambda i, o, l: (o[i], 0)),
                pl.BlockSpec((2048, 128), lambda i, o, l: (o[i], 0)),
                pl.BlockSpec((2048, 128), lambda i, o, l: (o[i], 0)),
            ],
            out_specs=[
                pl.BlockSpec((rows, 512), lambda i, o, l: (0, 0)),
                pl.BlockSpec((rows, 128), lambda i, o, l: (0, 0)),
                pl.BlockSpec((rows, 128), lambda i, o, l: (0, 0)),
            ],
            scratch_shapes=[pltpu.VMEM((rows, 128), F32), pltpu.VMEM((rows, 768), F32)],
        ),
        out_shape=[
            jax.ShapeDtypeStruct((rows, 512), BF),
            jax.ShapeDtypeStruct((rows, 128), BF),
            jax.ShapeDtypeStruct((rows, 128), BF),
        ],
        compiler_params=params(24),
        cost_estimate=pl.CostEstimate(
            flops=2 * rows * 8192 * 768, bytes_accessed=14 * 2**20, transcendentals=0
        ),
        name="step_project",
    )(order, low, xs, gain.reshape(4, 4, 1, 512), wq, wa, wb)


def start_copies(index, tops, lows, weights, xbuf, wbuf, xsem, wsem):
    copies = []
    place = 0
    for top, low in zip(tops, lows):
        for n in range(top.shape[0]):
            rows = pl.ds(pl.multiple_of(index[place] * 512, 512), 512)
            here = [
                pltpu.make_async_copy(top.at[n], xbuf.at[place, 0], xsem.at[place, 0]),
                pltpu.make_async_copy(low.at[n], xbuf.at[place, 1], xsem.at[place, 1]),
            ]
            at = 0
            for k, weight in enumerate(weights):
                width = weight.shape[1]
                here.append(
                    pltpu.make_async_copy(
                        weight.at[rows], wbuf.at[place, :, pl.ds(at, width)], wsem.at[place, k]
                    )
                )
                at += width
            for copy in here:
                copy.start()
            copies.append(here)
            place += 1
    return copies


def row_factors(ssq, scale):
    total = jnp.zeros((8, 128), F32)
    for k in range(TP):
        wide = ssq[k].astype(F32)
        total = total + (wide[0:8] + wide[8:16] + wide[16:24])
    factor = lax.rsqrt(total / (TP * 512) + EPS)
    for n in range(8):
        scale[n * 128 : (n + 1) * 128, :] = jnp.broadcast_to(
            to_column(factor[n : n + 1]), (128, 128)
        )


def products(copies, index, gain, scale, xbuf, wbuf, add):
    half = xbuf.shape[2]
    for place, here in enumerate(copies):
        for copy in here:
            copy.wait()
        gain_row = gain[index[place]].astype(F32)
        for n in range(2 * half // 256):
            part, at = divmod(n * 256, half)
            rows = slice(n * 256, (n + 1) * 256)
            x = xbuf[place, part, at : at + 256, :].astype(F32)
            normed = (x * scale[rows, :1] * gain_row).astype(BF)
            add(place, rows, nn_dot(normed, wbuf[place]))


def block_scratch(blocks, half, width):
    return [
        pltpu.VMEM((blocks, 2, half, 512), BF),
        pltpu.VMEM((blocks, 512, width), BF),
        pltpu.VMEM((2 * half, 128), F32),
        pltpu.SemaphoreType.DMA((blocks, 2)),
        pltpu.SemaphoreType.DMA((blocks, 3)),
    ]


def project(index, tops, lows, ssq, gain, weights, held):
    parts = len(tops)
    blocks = sum(a.shape[0] for a in tops)
    half = tops[0].shape[1]
    rows = 2 * half
    kinds = len(weights)

    def body(*refs):
        refs = list(refs)
        index_ref = refs.pop(0)
        top_refs = [refs.pop(0) for _ in range(parts)]
        low_refs = [refs.pop(0) for _ in range(parts)]
        ssq_ref, gain_ref = refs.pop(0), refs.pop(0)
        weight_refs = [refs.pop(0) for _ in range(kinds)]
        held_q, held_kv = (refs.pop(0), refs.pop(0)) if held else (None, None)
        q, kv, xbuf, wbuf, scale, xsem, wsem = refs
        copies = start_copies(index_ref, top_refs, low_refs, weight_refs, xbuf, wbuf, xsem, wsem)
        row_factors(ssq_ref, scale)

        def add(place, at, product):
            if place > 0:
                q[at, :] += product[:, :512]
                kv[at, :] += product[:, 512:]
            elif held:
                q[at, :] = held_q[at, :] + product[:, :512]
                kv[at, :] = held_kv[at, :] + product[:, 512:]
            else:
                q[at, :] = product[:, :512]
                kv[at, :] = product[:, 512:]

        products(copies, index_ref, gain_ref, scale, xbuf, wbuf, add)

    return pl.pallas_call(
        body,
        in_specs=[smem()]
        + [hbm()] * (2 * parts)
        + [vmem()] * 2
        + [hbm()] * kinds
        + [vmem()] * (2 if held else 0),
        out_specs=[vmem()] * 2,
        out_shape=[
            jax.ShapeDtypeStruct((rows, 512), F32),
            jax.ShapeDtypeStruct((rows, 256), F32),
        ],
        scratch_shapes=block_scratch(blocks, half, 768),
        compiler_params=params(32),
        cost_estimate=pl.CostEstimate(
            flops=2 * rows * 512 * blocks * 768,
            bytes_accessed=blocks * 2 * 2**20,
            transcendentals=0,
        ),
        name="prefill_project",
    )(index, *tops, *lows, ssq, gain.reshape(TP, 1, 512), *weights, *(held or ()))


def finish_keys(index, core, start, tops, lows, ssq, gain, weights, held, q, group, token_row):
    parts = len(tops)
    blocks = sum(a.shape[0] for a in tops)
    half = tops[0].shape[1]
    rows = 2 * half

    def body(*refs):
        refs = list(refs)
        index_ref, core_ref, start_ref, group_ref = [refs.pop(0) for _ in range(4)]
        top_refs = [refs.pop(0) for _ in range(parts)]
        low_refs = [refs.pop(0) for _ in range(parts)]
        ssq_ref, gain_ref = refs.pop(0), refs.pop(0)
        weight_refs = [refs.pop(0) for _ in range(2)]
        held_ref, q_ref, row_ref = [refs.pop(0) for _ in range(3)]
        keys, values, out, xbuf, wbuf, scale, xsem, wsem, acc = refs
        copies = start_copies(index_ref, top_refs, low_refs, weight_refs, xbuf, wbuf, xsem, wsem)
        row_factors(ssq_ref, scale)

        def add(place, at, product):
            if place < blocks - 1:
                acc[at, :] = (held_ref if place == 0 else acc)[at, :] + product
                return
            total = (held_ref if place == 0 else acc)[at, :] + product
            own, other = total[:, :128], total[:, 128:]
            keys[at, :] = jnp.where(core_ref[0] == 0, own, other).astype(BF)
            values[at, :] = jnp.where(core_ref[0] == 0, other, own).astype(BF)

        products(copies, index_ref, gain_ref, scale, xbuf, wbuf, add)
        fresh_groups(group_ref, start_ref, q_ref, keys, values, row_ref, out)

    return pl.pallas_call(
        body,
        in_specs=[smem()] * 4 + [hbm()] * (2 * parts) + [vmem()] * 2 + [hbm()] * 2 + [vmem()] * 3,
        out_specs=[vmem()] * 3,
        out_shape=[
            jax.ShapeDtypeStruct((rows, 128), BF),
            jax.ShapeDtypeStruct((rows, 128), BF),
            jax.ShapeDtypeStruct((ROLE, 256 + STAT_ROWS, 128), BF),
        ],
        scratch_shapes=block_scratch(blocks, half, 256) + [pltpu.VMEM((rows, 256), F32)],
        compiler_params=params(32),
        cost_estimate=pl.CostEstimate(
            flops=3 * 10**9, bytes_accessed=6 * 2**20, transcendentals=2**20
        ),
        name="keys_and_fresh_pages",
    )(
        index, core, start, group, *tops, *lows, ssq, gain.reshape(TP, 1, 512), *weights,
        held, q, token_row,
    )


def finish_queries(index, tops, lows, ssq, gain, weight, held, keys, values, seg_row):
    parts = len(tops)
    blocks = sum(a.shape[0] for a in tops)
    half = tops[0].shape[1]
    rows = 2 * half

    def body(*refs):
        refs = list(refs)
        index_ref = refs.pop(0)
        top_refs = [refs.pop(0) for _ in range(parts)]
        low_refs = [refs.pop(0) for _ in range(parts)]
        ssq_ref, gain_ref, weight_ref = [refs.pop(0) for _ in range(3)]
        held_ref, key_ref, value_ref, seg_ref = [refs.pop(0) for _ in range(4)]
        out, xbuf, wbuf, scale, xsem, wsem, acc, q = refs
        copies = start_copies(index_ref, top_refs, low_refs, [weight_ref], xbuf, wbuf, xsem, wsem)
        row_factors(ssq_ref, scale)

        def add(place, at, product):
            total = (held_ref if place == 0 else acc)[at, :] + product
            if place < blocks - 1:
                acc[at, :] = total
            else:
                q[at, :] = total.astype(BF)

        products(copies, index_ref, gain_ref, scale, xbuf, wbuf, add)
        prefill_kernel(q, key_ref, value_ref, seg_ref, out)

    return pl.pallas_call(
        body,
        in_specs=[smem()] + [hbm()] * (2 * parts) + [vmem()] * 2 + [hbm()] + [vmem()] * 4,
        out_specs=vmem(),
        out_shape=jax.ShapeDtypeStruct((rows, 512), BF),
        scratch_shapes=block_scratch(blocks, half, 512)
        + [pltpu.VMEM((rows, 512), F32), pltpu.VMEM((rows, 512), BF)],
        compiler_params=params(32),
        cost_estimate=pl.CostEstimate(
            flops=4 * 10**9, bytes_accessed=6 * 2**20, transcendentals=3 * 2**20
        ),
        name="queries_and_prefill",
    )(
        index, *tops, *lows, ssq, gain.reshape(TP, 1, 512), weight, held, keys, values, seg_row
    )


def paged_kernel(first_chunk, slot_page, slot_live, where, q, cache, out, top, total, acc, lse):
    lane = lax.broadcasted_iota(jnp.int32, (1, 128), 1)
    heads = range(KV_HEADS)

    def one_row(r, carry):
        top[...] = jnp.full_like(top, LOW)
        total[...] = jnp.zeros_like(total)
        acc[...] = jnp.zeros_like(acc)
        at = pl.multiple_of(r * 16, 16)
        queries = [
            jnp.concatenate(
                [q[where[2 * k], pl.ds(at, 16), :], q[where[2 * k + 1], pl.ds(at, 16), :]], axis=0
            )
            for k in heads
        ]

        def one_chunk(i, inner):
            live = jnp.zeros((1, 128), jnp.int32)
            pages = []
            for j in range(8):
                slot = i * 8 + j
                pages.append(slot_page[slot])
                live = jnp.where(lane // PAGE_TOKENS == j, slot_live[slot], live)
            valid = lane % PAGE_TOKENS < live

            def part(column):
                return jnp.concatenate(
                    [cache[page, :, column * 128 : (column + 1) * 128] for page in pages], axis=0
                )

            scores = [jnp.where(valid, nt_dot(queries[k], part(2 * k)), LOW) for k in heads]
            old = [top[k * 32 : (k + 1) * 32, :] for k in heads]
            new = [jnp.maximum(old[k], jnp.max(scores[k], axis=1, keepdims=True)) for k in heads]
            weights = [
                jnp.where(valid, jnp.exp2((scores[k] - new[k]) * EXP2_SCALE), 0.0) for k in heads
            ]
            products = [nn_dot(weights[k].astype(BF), part(2 * k + 1)) for k in heads]
            for k in heads:
                rows = slice(k * 32, (k + 1) * 32)
                fade = jnp.exp2((old[k] - new[k]) * EXP2_SCALE)
                top[rows, :] = new[k]
                total[rows, :] = total[rows, :] * fade + jnp.sum(weights[k], axis=1, keepdims=True)
                acc[rows, :] = acc[rows, :] * fade + products[k]
            return inner

        lax.fori_loop(first_chunk[r], first_chunk[r + 1], one_chunk, 0)
        some = total[...] > 0.0
        divisor = jnp.where(some, total[...], 1.0)
        result = (acc[...] * (1.0 / divisor)).astype(BF)
        level = jnp.where(some, top[...] * SCALE + jnp.log(divisor), LOW)
        for t in range(TP):
            out[t, pl.ds(at, 16), :] = result[t * 16 : (t + 1) * 16]
            lse[t, pl.ds(at, 16), :] = level[t * 16 : (t + 1) * 16]
        return carry

    lax.fori_loop(0, 16, one_row, 0)

    def one_target(t, carry):
        out[t, 256:272, :] = stat_block(lse[t])
        return carry

    lax.fori_loop(0, TP, one_target, 0)


def paged_attention(first_chunk, slot_page, slot_live, where, q, cache):
    return pl.pallas_call(
        paged_kernel,
        in_specs=[smem()] * 4 + [vmem()] * 2,
        out_specs=vmem(),
        out_shape=jax.ShapeDtypeStruct((TP, 256 + STAT_ROWS, 128), BF),
        scratch_shapes=[
            pltpu.VMEM((256, 128), F32),
            pltpu.VMEM((256, 128), F32),
            pltpu.VMEM((256, 128), F32),
            pltpu.VMEM((TP, 256, 128), F32),
        ],
        compiler_params=params(24),
        cost_estimate=pl.CostEstimate(
            flops=2 * 10**9, bytes_accessed=12 * 2**20, transcendentals=2**20
        ),
        name="paged_attention",
    )(first_chunk, slot_page, slot_live, where, q, cache)


def fresh_groups(group, start, q, keys, values, token_row, out):
    span = token_row.shape[1]
    for i in range(ROLE):
        rows = pl.ds(pl.multiple_of(start[i] * PAGE_TOKENS, PAGE_TOKENS), span)
        row = lax.broadcasted_iota(jnp.int32, (256, 1), 0) // 16
        valid = token_row[i : i + 1, :] == row
        scores = jnp.where(valid, nt_dot(q[i], keys[rows, :]), LOW)
        top = jnp.maximum(jnp.max(scores, axis=1, keepdims=True), 0.5 * LOW)
        weights = jnp.exp2((scores - top) * EXP2_SCALE)
        total = jnp.sum(weights, axis=1, keepdims=True)
        acc = nn_dot(weights.astype(BF), values[rows, :])
        some = total > 0.0
        divisor = jnp.where(some, total, 1.0)
        target = group[i]
        out[target, :256, :] = (acc * (1.0 / divisor)).astype(BF)
        out[target, 256:272, :] = stat_block(
            jnp.where(some, top * SCALE + jnp.log(divisor), LOW)
        )


def prefill_kernel(q, keys, values, seg_row, out):
    rows = q.shape[0]
    for tile in range(rows // 256):
        high = (tile + 1) * 256
        low = max(0, (tile * 256 - 511) // 256 * 256)
        span = high - low
        seg_keys = seg_row[:, low:high]
        seg_queries = to_column(seg_row[:, tile * 256 : high])
        row = lax.broadcasted_iota(jnp.int32, (256, span), 0) + tile * 256
        column = lax.broadcasted_iota(jnp.int32, (256, span), 1) + low
        valid = (seg_keys == seg_queries) & (column <= row)
        for h in range(4):
            lanes = slice(h * 128, (h + 1) * 128)
            scores = nt_dot(q[tile * 256 : high, lanes], keys[low:high, :])
            scores = jnp.where(valid, scores, LOW)
            top = jnp.max(scores, axis=1, keepdims=True)
            weights = jnp.exp2((scores - top) * EXP2_SCALE)
            total = jnp.sum(weights, axis=1, keepdims=True)
            weights = (weights * (1.0 / total)).astype(BF)
            out[tile * 256 : high, lanes] = nn_dot(weights, values[low:high, :]).astype(BF)


def stat_columns(parts):
    rows = [stat_rows(parts[n, 256:272, :]) for n in range(parts.shape[0])]
    rows.append(jnp.zeros((128 - 2 * len(rows), 128), F32))
    columns = jnp.concatenate(rows, axis=0).T
    return [
        jnp.concatenate([columns[:, 2 * n : 2 * n + 1], columns[:, 2 * n + 1 : 2 * n + 2]], axis=0)
        for n in range(parts.shape[0])
    ]


def held_kernel(held, q, new_keys, new_values, out, top_out, total_out):
    row = lax.broadcasted_iota(jnp.int32, (256, 64), 0)
    key = lax.broadcasted_iota(jnp.int32, (256, 64), 1)
    valid = (row // 16 == key % 16) & (key // 16 <= row % 16 // 4)
    scores = jnp.where(valid, nt_dot(q[...], new_keys[...]) * SCALE, LOW)
    top = jnp.max(scores, axis=1, keepdims=True)
    levels = stat_columns(held)
    for level in levels:
        top = jnp.maximum(top, level)
    weights = jnp.where(valid, jnp.exp(scores - top), 0.0)
    total = jnp.sum(weights, axis=1, keepdims=True)
    acc = nn_dot(weights.astype(BF), new_values[...])
    for n, level in enumerate(levels):
        factor = jnp.exp(level - top)
        total = total + factor
        acc = acc + held[n, :256, :].astype(F32) * factor
    out[...] = acc
    top_out[...] = jnp.broadcast_to(top, top_out.shape)
    total_out[...] = jnp.broadcast_to(total, total_out.shape)


def merge_held(held, q, new_keys, new_values):
    state = jax.ShapeDtypeStruct((256, 128), F32)
    return pl.pallas_call(
        held_kernel,
        in_specs=[vmem()] * 4,
        out_specs=[vmem()] * 3,
        out_shape=[state] * 3,
        compiler_params=params(16),
        cost_estimate=pl.CostEstimate(
            flops=10**7, bytes_accessed=2 * 2**20, transcendentals=2**16
        ),
        name="merge_held_pages",
    )(held, q, new_keys, new_values)


def merge_kernel(fresh, held_acc, held_top, held_total, out):
    top = held_top[:, :1]
    levels = stat_columns(fresh)
    for level in levels:
        top = jnp.maximum(top, level)
    factor = jnp.exp(held_top[:, :1] - top)
    total = held_total[:, :1] * factor
    acc = held_acc[...] * factor
    for n, level in enumerate(levels):
        factor = jnp.exp(level - top)
        total = total + factor
        acc = acc + fresh[n, :256, :].astype(F32) * factor
    out[...] = (acc * (1.0 / total)).astype(BF)


def merge(fresh, state):
    return pl.pallas_call(
        merge_kernel,
        in_specs=[vmem()] * 4,
        out_specs=vmem(),
        out_shape=jax.ShapeDtypeStruct((256, 128), BF),
        compiler_params=params(16),
        cost_estimate=pl.CostEstimate(
            flops=10**7, bytes_accessed=2 * 2**20, transcendentals=2**16
        ),
        name="decode_merge",
    )(fresh, *state)


def page_tables(block_table, cache_len, ships, first_page):
    pages = 128
    page_ids = jnp.arange(pages, dtype=jnp.int32)
    rows, entries = block_table.shape
    code_of = (
        jnp.arange(rows, dtype=jnp.int32)[:, None] * entries
        + jnp.arange(entries, dtype=jnp.int32)[None, :]
    )
    match = block_table[None] == (first_page + page_ids)[:, None, None]
    code = jnp.max(jnp.where(match, code_of[None], -1), axis=(1, 2))
    replaced = jnp.any(ships.reshape(1, -1) == (first_page + page_ids)[:, None], axis=1)
    row = jnp.where(replaced | (code < 0), rows, code // entries)
    onehot = row[:, None] == jnp.arange(rows, dtype=jnp.int32)[None, :]
    length = jnp.sum(jnp.where(onehot, cache_len[None, :], 0), axis=1)
    live = jnp.clip(length - (code % entries) * PAGE_TOKENS, 0, PAGE_TOKENS)
    count = jnp.sum(onehot.astype(jnp.int32), axis=0)
    chunks = (count + 7) // 8
    ids17 = jnp.arange(rows + 1, dtype=jnp.int32)
    ids16 = jnp.arange(rows, dtype=jnp.int32)
    first_chunk = jnp.sum(
        jnp.where(ids16[None, :] < ids17[:, None], chunks[None, :], 0), axis=1
    )
    rank = jnp.sum(
        ((row[None, :] == row[:, None]) & (page_ids[None, :] < page_ids[:, None])).astype(jnp.int32),
        axis=1,
    )
    base = jnp.sum(jnp.where(onehot, first_chunk[None, :rows], 0), axis=1)
    slot = jnp.where(row < rows, base * 8 + rank, -1)
    hit = slot[None, :] == jnp.arange(256, dtype=jnp.int32)[:, None]
    slot_page = jnp.sum(jnp.where(hit, page_ids[None, :], 0), axis=1)
    slot_live = jnp.sum(jnp.where(hit, live[None, :], 0), axis=1)
    return first_chunk, slot_page, slot_live


def token_rows(tables, lengths, ship_page, group):
    rows, entries = tables.shape
    pages = ship_page.shape[0]
    window = pages // 2
    code_of = (
        jnp.arange(rows, dtype=jnp.int32)[:, None] * entries
        + jnp.arange(entries, dtype=jnp.int32)[None, :]
    )
    match = tables[None] == ship_page[:, None, None]
    code = jnp.max(jnp.where(match, code_of[None], -1), axis=(1, 2))
    row = jnp.where(code >= 0, code // entries, -1)
    onehot = row[:, None] == jnp.arange(rows, dtype=jnp.int32)[None, :]
    length = jnp.sum(jnp.where(onehot, lengths[None, :], 0), axis=1)
    live = jnp.clip(length - (code % entries) * PAGE_TOKENS, 0, PAGE_TOKENS)
    live = jnp.where(code >= 0, live, 0)
    page_ids = jnp.arange(pages, dtype=jnp.int32)
    ours = (ship_page // 2048)[None, :] == group[:, None]
    start = jnp.min(jnp.where(ours, page_ids[None, :], window), axis=1)
    start = jnp.minimum(start, window)
    packed = jnp.where(live > 0, row * 32 + live, 0)
    place = start[:, None] + jnp.arange(window, dtype=jnp.int32)[None, :]
    hit = place[:, :, None] == page_ids[None, None, :]
    here = jnp.sum(jnp.where(hit & ours[:, None, :], packed[None, None, :], 0), axis=2)
    token = jnp.arange(PAGE_TOKENS, dtype=jnp.int32)[None, None, :]
    token_row = jnp.where(token < (here % 32)[:, :, None], (here // 32 % 16)[:, :, None], -1)
    return start, token_row.reshape(ROLE, window * PAGE_TOKENS)


def after(x, *others):
    return lax.optimization_barrier((x, *others))[0]


def per_device(
    text_embed,
    vision_rows,
    vision_group,
    vision_slot,
    request_blocks,
    ship_page,
    paged_cache,
    block_table,
    cache_len,
    step_embed,
    norm_gain,
    query_weight,
    keyvalue_weight,
):
    column = lax.axis_index("tp")
    role = lax.axis_index("role")
    core = column % 2
    group_rows, width = text_embed.shape
    half = group_rows // 2
    steps, rows, _ = step_embed.shape

    role_id = role.reshape(1)

    other_text = swap(text_embed, "tp", CORE)
    other_weight = swap(keyvalue_weight, "tp", CORE)
    message = pick_rows(vision_group, vision_slot, vision_rows)
    arrived = lax.all_to_all(message, "role", split_axis=0, concat_axis=0, tiled=True)
    other_arrived = swap(arrived, "tp", CORE)
    top_pair, low_pair, square_parts = land_rows(
        role_id, arrived, other_arrived, text_embed, other_text
    )

    def plus(a):
        return swap(a, "tp", CORE)

    top_z_own = swap(top_pair[0], "tp", ZLO)
    low_y = ring_y(low_pair)
    top_y = ring_y(top_pair)
    low_z_own = swap(low_pair[0], "tp", ZLO)
    top_z = jnp.stack([top_z_own, plus(top_z_own)])
    low_z_other = plus(low_z_own)
    top_zy = ring_y(top_z)
    low_zy = swap(low_y, "tp", ZLO)
    far = ring_y(jnp.stack([low_y[0], top_y[0]]))
    top_zf_own = ring_y(top_zy[0])
    low_zf_own = swap(far[0], "tp", ZLO)
    far_other = plus(far)

    steps_all = doubling(step_embed.reshape(steps * rows, width), "tp", TP_MASKS)
    step_q, step_a, step_b = step_project(
        (column // 4) ^ jnp.array([0, 1, 3, 2], jnp.int32),
        (column % 4).reshape(1),
        steps_all,
        norm_gain,
        query_weight,
        keyvalue_weight,
        other_weight,
    )
    new_keys = jnp.where(core == 0, step_a, step_b)
    new_values = jnp.where(core == 0, step_b, step_a)
    own_queries = (
        step_q.reshape(steps, rows, 4, HEAD_SIZE).transpose(1, 0, 2, 3).reshape(rows * 16, HEAD_SIZE)
    )
    query_message = jnp.concatenate([own_queries, square_parts], axis=0)
    query_all = doubling(query_message, "tp", TP_MASKS)
    ssq = query_all[:, 256:288, :]
    queries_role = doubling(own_queries, "role", ROLE_MASKS)

    meta = jnp.concatenate(
        [block_table.reshape(-1), cache_len, ship_page, jnp.zeros((48,), jnp.int32)]
    ).reshape(33, 128)
    meta = after(meta, square_parts)
    metas = doubling(meta, "role", ROLE_MASKS).reshape(ROLE, -1)
    tables = metas[:, :4096].reshape(ROLE * rows, -1)
    lengths = metas[:, 4096 : 4096 + rows].reshape(-1)
    ships = metas[:, 4112 : 4112 + 64]
    role_order = role ^ jnp.array(ROLE_OFFSETS, jnp.int32)
    first_page = (role * TP + column) * 128
    first_chunk, slot_page, slot_live = page_tables(block_table, cache_len, ships, first_page)
    start, token_row = token_rows(tables, lengths, ship_page, role_order)

    difference = column ^ jnp.arange(TP, dtype=jnp.int32)
    far_bit = difference // 8
    near_bit = (difference // 4) % 2 ^ far_bit
    where = difference // 2 % 2 + 2 * near_bit + 4 * far_bit + 8 * (difference % 2)
    held = paged_attention(
        first_chunk, slot_page, slot_live, where, query_all[:, :256, :], paged_cache
    )
    held_parts = lax.all_to_all(held, "tp", split_axis=0, concat_axis=0, tiled=True)
    state = merge_held(held_parts, own_queries, new_keys, new_values)

    y = column // 4
    low_bits = column % 4

    def at(dy, bits):
        return ((y + dy) % 4) * 4 + (low_bits ^ bits)

    toward = jnp.where(core == 0, -1, 1)
    index_1 = jnp.stack(
        [
            at(0, 0),
            at(0, 1),
            at(0, 2),
            at(0, 3),
            at(toward, 0),
            at(toward, 1),
            at(-toward, 1),
            at(-toward, 0),
        ]
    )
    index_2 = jnp.stack(
        [at(toward, 2), at(toward, 3), at(-toward, 3), at(-toward, 2), at(2, 0), at(2, 1)]
    )
    index_3 = jnp.stack([at(2, 2), at(2, 3)])
    weights = (query_weight, keyvalue_weight, other_weight)
    sums = project(
        index_1,
        [top_pair, top_z[:1], top_z[1:], top_y, plus(top_y)],
        [low_pair, low_z_own[None], low_z_other[None], low_y, plus(low_y)],
        ssq,
        norm_gain,
        weights,
        None,
    )
    q_sum, kv_sum = project(
        index_2,
        [top_zy, plus(top_zy), far[1:], far_other[1:]],
        [low_zy, plus(low_zy), far[:1], far_other[:1]],
        ssq,
        norm_gain,
        weights,
        sums,
    )
    last_top = [top_zf_own[None], plus(top_zf_own)[None]]
    last_low = [low_zf_own[None], plus(low_zf_own)[None]]

    keys, values, fresh = finish_keys(
        index_3,
        core.reshape(1),
        start,
        last_top,
        last_low,
        ssq,
        norm_gain,
        weights[1:],
        kv_sum,
        queries_role,
        role_order,
        token_row,
    )
    fresh_parts = lax.all_to_all(fresh, "role", split_axis=0, concat_axis=0, tiled=True)

    positions = jnp.arange(group_rows, dtype=jnp.int32)
    request_ends = jnp.cumsum(request_blocks[0] * PAGE_TOKENS)
    segment = jnp.sum((positions[:, None] >= request_ends[None, :]).astype(F32), axis=1)
    prefill_out = finish_queries(
        index_3,
        last_top,
        last_low,
        ssq,
        norm_gain,
        query_weight,
        q_sum,
        keys,
        values,
        segment.reshape(1, -1),
    )

    decode = merge(fresh_parts, state)
    decode_out = (
        decode.reshape(rows, steps, 4, HEAD_SIZE).transpose(1, 0, 2, 3).reshape(steps, rows, 512)
    )
    return (prefill_out, decode_out)


def solution(mesh):
    in_specs = (
        P("role", "tp"),
        P("role", "tp"),
        P("role"),
        P("role"),
        P("role", None),
        P("role"),
        P(("role", "tp"), None, None),
        P("role", None),
        P("role"),
        P(None, "role", "tp"),
        P(),
        P(None, "tp"),
        P(None, "tp"),
    )
    out_specs = (P("role", "tp"), P(None, "role", "tp"))
    return jax.shard_map(
        per_device, mesh=mesh, in_specs=in_specs, out_specs=out_specs, check_vma=False
    )
```

```python
import jax
import jax.numpy as jnp
from jax import lax
from jax.experimental import pallas as pl
from jax.experimental.pallas import tpu as pltpu
from jax.sharding import PartitionSpec as P

HEAD_SIZE = 128
KV_HEADS = 8
PAGE_TOKENS = 16
EPS = 1e-06
LOW = -1e30
SCALE = HEAD_SIZE ** (-0.5)
BF = jnp.bfloat16
F32 = jnp.float32
EXP2_SCALE = SCALE * 1.4426950408889634
LN2 = 0.6931471805599453
TP = 16
ROLE = 8
STAT_ROWS = 16

CORE = 1


def params(mebibytes):
    return pltpu.CompilerParams(vmem_limit_bytes=mebibytes * 2**20)


def vmem():
    return pl.BlockSpec(memory_space=pltpu.VMEM)


def smem():
    return pl.BlockSpec(memory_space=pltpu.SMEM)


def hbm():
    return pl.BlockSpec(memory_space=pl.ANY)


def swap(x, axis, mask):
    size = TP if axis == "tp" else ROLE
    return lax.ppermute(x, axis, [(i, i ^ mask) for i in range(size)])


def over_chips(x):
    return [x] + [swap(x, "tp", 2 * i) for i in range(1, 8)]


def more(held, axis, mask):
    return jnp.concatenate([held, swap(held, axis, mask)], axis=0)


def doubling(x, axis, masks):
    held = x[None]
    for mask in masks:
        held = more(held, axis, mask)
    return held


def offsets(masks):
    table = [0]
    for mask in masks:
        table = table + [v ^ mask for v in table]
    return table


ROLE_MASKS = (4, 1, 3)
ROLE_OFFSETS = offsets(ROLE_MASKS)


def nt_dot(a, b):
    return lax.dot_general(a, b, (((1,), (1,)), ((), ())), preferred_element_type=F32)


def nn_dot(a, b):
    return jnp.dot(a, b, preferred_element_type=F32)


def eye(n):
    return lax.broadcasted_iota(jnp.int32, (n, n), 0) == lax.broadcasted_iota(
        jnp.int32, (n, n), 1
    )


def to_row(column):
    n = column.shape[0]
    return jnp.sum(jnp.where(eye(n), column, 0.0), axis=0, keepdims=True)


def to_column(row):
    n = row.shape[1]
    return jnp.sum(jnp.where(eye(n), row, 0.0), axis=1, keepdims=True)


def split3(x):
    high = x.astype(BF)
    rest = x - high.astype(F32)
    middle = rest.astype(BF)
    low = (rest - middle.astype(F32)).astype(BF)
    return high, middle, low


def stat_block(level):
    parts = jnp.concatenate(
        [to_row(level[:128]), to_row(level[128:]), jnp.zeros((6, 128), F32)], axis=0
    )
    high, middle, low = split3(parts)
    return jnp.concatenate(
        [
            high[:2].astype(F32),
            middle[:2].astype(F32),
            low[:2].astype(F32),
            jnp.zeros((10, 128), F32),
        ],
        axis=0,
    ).astype(BF)


def stat_rows(block):
    wide = block.astype(F32)
    return wide[0:2] + wide[2:4] + wide[4:6]


def pick_kernel(group, slot, rows, out):
    count = group.shape[1]
    capacity = 2 * count // ROLE
    onehot = group[...] == lax.broadcasted_iota(jnp.int32, (ROLE, 1), 0)
    before = lax.broadcasted_iota(jnp.int32, (count, count), 0) < lax.broadcasted_iota(
        jnp.int32, (count, count), 1
    )
    rank = nn_dot(onehot.astype(F32).astype(BF), before.astype(F32).astype(BF))
    rank = jnp.sum(jnp.where(onehot, rank, 0.0), axis=0, keepdims=True).astype(jnp.int32)
    place = group[...] * capacity + rank
    picked = place == lax.broadcasted_iota(jnp.int32, (ROLE * capacity, 1), 0)
    picked = picked.astype(F32).astype(BF)
    chosen = nn_dot(picked, rows[...]).astype(BF)
    code = slot[...] + 1
    line = lax.broadcasted_iota(jnp.int32, (16, 1), 0)
    codes = jnp.where(line == 0, code // 32, jnp.where(line == 1, code % 32, 0))
    codes = nt_dot(codes.astype(F32).astype(BF), picked).astype(BF)
    for g in range(ROLE):
        out[g, :capacity, :] = chosen[g * capacity : (g + 1) * capacity]
        out[g, capacity:, :] = codes


def pick_rows(group, slot, rows):
    count, width = rows.shape
    capacity = 2 * count // ROLE
    return pl.pallas_call(
        pick_kernel,
        in_specs=[vmem()] * 3,
        out_specs=vmem(),
        out_shape=jax.ShapeDtypeStruct((ROLE, capacity + 16, width), BF),
        compiler_params=params(16),
        cost_estimate=pl.CostEstimate(flops=2 * 10**8, bytes_accessed=2**20, transcendentals=0),
        name="pick_rows",
    )(group.reshape(1, count), slot.reshape(1, count), rows)


def land_kernel(role, arrived, text, merged, squares):
    capacity = arrived.shape[1] - 16
    total = ROLE * capacity
    lane = lax.broadcasted_iota(jnp.int32, (1, total), 1)
    slots = jnp.zeros((1, total), F32)
    for s in range(ROLE):
        codes = arrived[s, capacity:, :].astype(F32)
        code = jnp.broadcast_to(codes[0:1] * 32.0 + codes[1:2], (8, total))
        shift = ((s + ROLE - role[0]) % ROLE) * capacity
        slots = jnp.where(lane // capacity == s, pltpu.roll(code, shift, 1)[0:1], slots)
    slots = slots.astype(jnp.int32) - 1
    rows = arrived[:, :capacity, :].reshape(total, arrived.shape[2])
    lines = []
    for n in range(text.shape[0] // 256):
        at = slice(n * 256, (n + 1) * 256)
        row = lax.broadcasted_iota(jnp.int32, (256, 1), 0) + n * 256
        landing = jnp.where(row == slots, 1.0, 0.0)
        hit = jnp.sum(landing, axis=1, keepdims=True) > 0.0
        block = jnp.where(hit, nn_dot(landing.astype(BF), rows), text[at, :].astype(F32))
        merged[at, :] = block.astype(BF)
        square = jnp.broadcast_to(jnp.sum(block * block, axis=1, keepdims=True), (256, 128))
        lines += [to_row(square[:128]), to_row(square[128:])]
    high, middle, rest = split3(jnp.concatenate(lines, axis=0))
    squares[...] = jnp.concatenate(
        [high.astype(F32), middle.astype(F32), rest.astype(F32), jnp.zeros((8, 128), F32)], axis=0
    ).astype(BF)


def land_rows(role, arrived, text):
    return pl.pallas_call(
        land_kernel,
        in_specs=[smem()] + [vmem()] * 2,
        out_specs=[vmem()] * 2,
        out_shape=[
            jax.ShapeDtypeStruct(text.shape, BF),
            jax.ShapeDtypeStruct((32, 128), BF),
        ],
        compiler_params=params(24),
        cost_estimate=pl.CostEstimate(flops=10**9, bytes_accessed=6 * 2**20, transcendentals=0),
        name="land_rows",
    )(role, arrived, text)


def step_kernel(order, low, xs, gain, wq, wa, wb, q_out, a_out, b_out, scale, acc):
    i = pl.program_id(0)

    @pl.when(i == 0)
    def _():
        total = jnp.zeros((xs.shape[1], 512), F32)
        for k in range(TP):
            wide = xs[k].astype(F32)
            total = total + wide * wide
        total = jnp.sum(total, axis=1, keepdims=True)
        scale[...] = jnp.broadcast_to(
            lax.rsqrt(total / (TP * xs.shape[2]) + EPS), scale.shape
        )
        acc[...] = jnp.zeros_like(acc)

    factor = jnp.broadcast_to(scale[:, :1], (xs.shape[1], 512))
    total_q = acc[:, :512]
    total_a = acc[:, 512:640]
    total_b = acc[:, 640:768]
    for j in range(4):
        place = low[0] ^ j
        block = j // 2 + 2 * i + 8 * (j % 2)
        rows = pl.ds(pl.multiple_of(place * 512, 512), 512)
        normed = (xs[block].astype(F32) * factor * gain[0, place].astype(F32)).astype(BF)
        total_q = total_q + nn_dot(normed, wq[rows, :])
        total_a = total_a + nn_dot(normed, wa[rows, :])
        total_b = total_b + nn_dot(normed, wb[rows, :])
    acc[:, :512] = total_q
    acc[:, 512:640] = total_a
    acc[:, 640:768] = total_b

    @pl.when(i == 3)
    def _():
        q_out[...] = acc[:, :512].astype(BF)
        a_out[...] = acc[:, 512:640].astype(BF)
        b_out[...] = acc[:, 640:768].astype(BF)


def step_project(order, low, xs, gain, wq, wa, wb):
    rows = xs.shape[1]
    return pl.pallas_call(
        step_kernel,
        grid_spec=pltpu.PrefetchScalarGridSpec(
            num_scalar_prefetch=2,
            grid=(4,),
            in_specs=[
                pl.BlockSpec(xs.shape, lambda i, o, l: (0, 0, 0)),
                pl.BlockSpec((1, 4, 1, 512), lambda i, o, l: (o[i], 0, 0, 0)),
                pl.BlockSpec((2048, 512), lambda i, o, l: (o[i], 0)),
                pl.BlockSpec((2048, 128), lambda i, o, l: (o[i], 0)),
                pl.BlockSpec((2048, 128), lambda i, o, l: (o[i], 0)),
            ],
            out_specs=[
                pl.BlockSpec((rows, 512), lambda i, o, l: (0, 0)),
                pl.BlockSpec((rows, 128), lambda i, o, l: (0, 0)),
                pl.BlockSpec((rows, 128), lambda i, o, l: (0, 0)),
            ],
            scratch_shapes=[pltpu.VMEM((rows, 128), F32), pltpu.VMEM((rows, 768), F32)],
        ),
        out_shape=[
            jax.ShapeDtypeStruct((rows, 512), BF),
            jax.ShapeDtypeStruct((rows, 128), BF),
            jax.ShapeDtypeStruct((rows, 128), BF),
        ],
        compiler_params=params(58),
        cost_estimate=pl.CostEstimate(
            flops=2 * rows * 8192 * 768, bytes_accessed=14 * 2**20, transcendentals=0
        ),
        name="step_project",
    )(order, low, xs, gain.reshape(4, 4, 1, 512), wq, wa, wb)


def row_factors(ssq, line, scale):
    factor = lax.rsqrt(ssq[...] / (TP * 512) + EPS)
    for n in range(scale.shape[0] // 128):
        scale[n * 128 : (n + 1) * 128, :] = jnp.broadcast_to(
            to_column(factor[line + n : line + n + 1]), (128, 128)
        )


def all_blocks(text, gain, weights, scale, xbuf, wbuf, xsem, wsem, acc):
    blocks, rows = text.shape[0], text.shape[1]
    for n in range(blocks):
        pltpu.make_async_copy(text.at[n], xbuf.at[n], xsem.at[n]).start()
        at = 0
        for k, weight in enumerate(weights):
            width = weight.shape[1]
            pltpu.make_async_copy(
                weight.at[pl.ds(n * 512, 512)], wbuf.at[n, :, pl.ds(at, width)], wsem.at[n, k]
            ).start()
            at += width

    def wait(n):
        pltpu.make_async_copy(xbuf.at[n], xbuf.at[n], xsem.at[n]).wait()
        at = 0
        for k, weight in enumerate(weights):
            part = wbuf.at[n, :, pl.ds(at, weight.shape[1])]
            pltpu.make_async_copy(part, part, wsem.at[n, k]).wait()
            at += weight.shape[1]

    def pair(i, carry):
        for n in (2 * i, 2 * i + 1):
            wait(n)
        gains = [gain[2 * i].astype(F32), gain[2 * i + 1].astype(F32)]
        for r in range(rows // 256):
            at = slice(r * 256, (r + 1) * 256)
            factor = scale[at, :1]
            product = None
            for k in range(2):
                normed = (xbuf[2 * i + k, at, :].astype(F32) * factor * gains[k]).astype(BF)
                term = nn_dot(normed, wbuf[2 * i + k])
                product = term if product is None else product + term
            acc[at, :] += product
        return carry

    acc[...] = jnp.zeros_like(acc)
    lax.fori_loop(0, blocks // 2, pair, 0)


def all_scratch(blocks, rows, width, kinds):
    return [
        pltpu.VMEM((blocks, rows, 512), BF),
        pltpu.VMEM((blocks, 512, width), BF),
        pltpu.VMEM((rows, 128), F32),
        pltpu.SemaphoreType.DMA((blocks,)),
        pltpu.SemaphoreType.DMA((blocks, kinds)),
        pltpu.VMEM((rows, width), F32),
    ]


def keys_kernel(
    core, start, group, text, ssq, gain, wa, wb, q, token_row,
    keys, values, out, xbuf, wbuf, scale, xsem, wsem, acc,
):
    row_factors(ssq, 0, scale)
    all_blocks(text, gain, (wa, wb), scale, xbuf, wbuf, xsem, wsem, acc)
    for n in range(acc.shape[0] // 256):
        at = slice(n * 256, (n + 1) * 256)
        own, other = acc[at, :128], acc[at, 128:]
        keys[at, :] = jnp.where(core[0] == 0, own, other).astype(BF)
        values[at, :] = jnp.where(core[0] == 0, other, own).astype(BF)
    fresh_groups(group, start, q, keys, values, token_row, out)


def finish_keys(core, start, group, text, ssq, gain, weights, q, token_row):
    blocks, rows, _ = text.shape
    return pl.pallas_call(
        keys_kernel,
        in_specs=[smem()] * 3 + [hbm()] + [vmem()] * 2 + [hbm()] * 2 + [vmem()] * 2,
        out_specs=[vmem()] * 3,
        out_shape=[
            jax.ShapeDtypeStruct((rows, 128), BF),
            jax.ShapeDtypeStruct((rows, 128), BF),
            jax.ShapeDtypeStruct((ROLE, 256 + STAT_ROWS, 128), BF),
        ],
        scratch_shapes=all_scratch(blocks, rows, 256, 2),
        compiler_params=params(58),
        cost_estimate=pl.CostEstimate(
            flops=6 * 10**9, bytes_accessed=20 * 2**20, transcendentals=2**20
        ),
        name="keys_and_fresh_pages",
    )(
        core, start, group, text, ssq, gain.reshape(TP, 1, 512), *weights, q, token_row
    )


def queries_kernel(
    blocks_ref, text, ssq, gain, weight, keys, values,
    out, xbuf, wbuf, scale, xsem, wsem, acc, q,
):
    row_factors(ssq, 0, scale)
    all_blocks(text, gain, (weight,), scale, xbuf, wbuf, xsem, wsem, acc)
    for n in range(acc.shape[0] // 256):
        at = slice(n * 256, (n + 1) * 256)
        q[at, :] = acc[at, :].astype(BF)
    position = lax.broadcasted_iota(jnp.int32, (1, q.shape[0]), 1)
    segment = jnp.zeros((1, q.shape[0]), F32)
    end = 0
    for n in range(blocks_ref.shape[1]):
        end = end + blocks_ref[0, n] * PAGE_TOKENS
        segment = segment + jnp.where(position >= end, 1.0, 0.0)
    prefill_kernel(q, keys, values, segment, out)


def finish_queries(request_blocks, text, ssq, gain, weight, keys, values):
    blocks, rows, _ = text.shape
    return pl.pallas_call(
        queries_kernel,
        in_specs=[smem(), hbm()] + [vmem()] * 2 + [hbm()] + [vmem()] * 2,
        out_specs=vmem(),
        out_shape=jax.ShapeDtypeStruct((rows, 512), BF),
        scratch_shapes=all_scratch(blocks, rows, 512, 1) + [pltpu.VMEM((rows, 512), BF)],
        compiler_params=params(58),
        cost_estimate=pl.CostEstimate(
            flops=12 * 10**9, bytes_accessed=25 * 2**20, transcendentals=3 * 2**20
        ),
        name="queries_and_prefill",
    )(request_blocks, text, ssq, gain.reshape(TP, 1, 512), weight, keys, values)


def paged_kernel(
    first_chunk, slot_page, slot_live, where, q, cache, out, kv, top, total, acc, lse, sem
):
    def fetch(i, carry):
        for j in range(8):
            pltpu.make_async_copy(
                cache.at[slot_page[i * 8 + j]],
                kv.at[i, pl.ds(j * PAGE_TOKENS, PAGE_TOKENS), :],
                sem.at[i],
            ).start()
        return carry

    lax.fori_loop(0, first_chunk[16], fetch, 0)
    lane = lax.broadcasted_iota(jnp.int32, (1, 128), 1)
    heads = range(KV_HEADS)

    def one_row(r, carry):
        top[...] = jnp.full_like(top, LOW)
        total[...] = jnp.zeros_like(total)
        acc[...] = jnp.zeros_like(acc)
        at = pl.multiple_of(r * 16, 16)
        queries = [
            jnp.concatenate(
                [q[where[2 * k], pl.ds(at, 16), :], q[where[2 * k + 1], pl.ds(at, 16), :]], axis=0
            )
            for k in heads
        ]

        def one_chunk(i, inner):
            live = jnp.zeros((1, 128), jnp.int32)
            for j in range(8):
                live = jnp.where(lane // PAGE_TOKENS == j, slot_live[i * 8 + j], live)
            valid = lane % PAGE_TOKENS < live
            pltpu.make_async_copy(kv.at[i], kv.at[i], sem.at[i]).wait()

            def part(column):
                return kv[i, :, column * 128 : (column + 1) * 128]

            scores = [jnp.where(valid, nt_dot(queries[k], part(2 * k)), LOW) for k in heads]
            old = [top[k * 32 : (k + 1) * 32, :] for k in heads]
            new = [jnp.maximum(old[k], jnp.max(scores[k], axis=1, keepdims=True)) for k in heads]
            weights = [
                jnp.where(valid, jnp.exp2((scores[k] - new[k]) * EXP2_SCALE), 0.0) for k in heads
            ]
            products = [nn_dot(weights[k].astype(BF), part(2 * k + 1)) for k in heads]
            for k in heads:
                rows = slice(k * 32, (k + 1) * 32)
                fade = jnp.exp2((old[k] - new[k]) * EXP2_SCALE)
                top[rows, :] = new[k]
                total[rows, :] = total[rows, :] * fade + jnp.sum(weights[k], axis=1, keepdims=True)
                acc[rows, :] = acc[rows, :] * fade + products[k]
            return inner

        lax.fori_loop(first_chunk[r], first_chunk[r + 1], one_chunk, 0)
        some = total[...] > 0.0
        divisor = jnp.where(some, total[...], 1.0)
        result = (acc[...] * (1.0 / divisor)).astype(BF)
        level = jnp.where(some, top[...] * SCALE + jnp.log(divisor), LOW)
        for t in range(TP):
            out[t, pl.ds(at, 16), :] = result[t * 16 : (t + 1) * 16]
            lse[t, pl.ds(at, 16), :] = level[t * 16 : (t + 1) * 16]
        return carry

    lax.fori_loop(0, 16, one_row, 0)

    def one_target(t, carry):
        out[t, 256:272, :] = stat_block(lse[t])
        return carry

    lax.fori_loop(0, TP, one_target, 0)


def paged_attention(first_chunk, slot_page, slot_live, where, q, cache):
    return pl.pallas_call(
        paged_kernel,
        in_specs=[smem()] * 4 + [vmem(), hbm()],
        out_specs=vmem(),
        out_shape=jax.ShapeDtypeStruct((TP, 256 + STAT_ROWS, 128), BF),
        scratch_shapes=[
            pltpu.VMEM((32, 128, 2048), BF),
            pltpu.VMEM((256, 128), F32),
            pltpu.VMEM((256, 128), F32),
            pltpu.VMEM((256, 128), F32),
            pltpu.VMEM((TP, 256, 128), F32),
            pltpu.SemaphoreType.DMA((32,)),
        ],
        compiler_params=params(58),
        cost_estimate=pl.CostEstimate(
            flops=2 * 10**9, bytes_accessed=12 * 2**20, transcendentals=2**20
        ),
        name="paged_attention",
    )(first_chunk, slot_page, slot_live, where, q, cache)


def fresh_groups(group, start, q, keys, values, token_row, out):
    span = token_row.shape[1]
    for i in range(ROLE):
        rows = pl.ds(pl.multiple_of(start[i] * PAGE_TOKENS, PAGE_TOKENS), span)
        row = lax.broadcasted_iota(jnp.int32, (256, 1), 0) // 16
        valid = token_row[i : i + 1, :] == row
        scores = jnp.where(valid, nt_dot(q[i], keys[rows, :]), LOW)
        top = jnp.maximum(jnp.max(scores, axis=1, keepdims=True), 0.5 * LOW)
        weights = jnp.exp2((scores - top) * EXP2_SCALE)
        total = jnp.sum(weights, axis=1, keepdims=True)
        acc = nn_dot(weights.astype(BF), values[rows, :])
        some = total > 0.0
        divisor = jnp.where(some, total, 1.0)
        target = group[i]
        out[target, :256, :] = (acc * (1.0 / divisor)).astype(BF)
        out[target, 256:272, :] = stat_block(
            jnp.where(some, top * SCALE + jnp.log(divisor), LOW)
        )


def prefill_kernel(q, keys, values, seg_row, out):
    rows = q.shape[0]
    for tile in range(rows // 256):
        high = (tile + 1) * 256
        low = max(0, (tile * 256 - 511) // 256 * 256)
        span = high - low
        seg_keys = seg_row[:, low:high]
        seg_queries = to_column(seg_row[:, tile * 256 : high])
        row = lax.broadcasted_iota(jnp.int32, (256, span), 0) + tile * 256
        column = lax.broadcasted_iota(jnp.int32, (256, span), 1) + low
        valid = (seg_keys == seg_queries) & (column <= row)
        for h in range(4):
            lanes = slice(h * 128, (h + 1) * 128)
            scores = nt_dot(q[tile * 256 : high, lanes], keys[low:high, :])
            scores = jnp.where(valid, scores, LOW)
            top = jnp.max(scores, axis=1, keepdims=True)
            weights = jnp.exp2((scores - top) * EXP2_SCALE)
            total = jnp.sum(weights, axis=1, keepdims=True)
            weights = (weights * (1.0 / total)).astype(BF)
            out[tile * 256 : high, lanes] = nn_dot(weights, values[low:high, :]).astype(BF)


def stat_columns(parts):
    rows = [stat_rows(parts[n, 256:272, :]) for n in range(parts.shape[0])]
    rows.append(jnp.zeros((128 - 2 * len(rows), 128), F32))
    columns = jnp.concatenate(rows, axis=0).T
    return [
        jnp.concatenate([columns[:, 2 * n : 2 * n + 1], columns[:, 2 * n + 1 : 2 * n + 2]], axis=0)
        for n in range(parts.shape[0])
    ]


def held_kernel(held, q, new_keys, new_values, out, top_out, total_out):
    row = lax.broadcasted_iota(jnp.int32, (256, 64), 0)
    key = lax.broadcasted_iota(jnp.int32, (256, 64), 1)
    valid = (row // 16 == key % 16) & (key // 16 <= row % 16 // 4)
    scores = jnp.where(valid, nt_dot(q[...], new_keys[...]) * SCALE, LOW)
    top = jnp.max(scores, axis=1, keepdims=True)
    levels = stat_columns(held)
    for level in levels:
        top = jnp.maximum(top, level)
    weights = jnp.where(valid, jnp.exp(scores - top), 0.0)
    total = jnp.sum(weights, axis=1, keepdims=True)
    acc = nn_dot(weights.astype(BF), new_values[...])
    for n, level in enumerate(levels):
        factor = jnp.exp(level - top)
        total = total + factor
        acc = acc + held[n, :256, :].astype(F32) * factor
    out[...] = acc
    top_out[...] = jnp.broadcast_to(top, top_out.shape)
    total_out[...] = jnp.broadcast_to(total, total_out.shape)


def merge_held(held, q, new_keys, new_values):
    state = jax.ShapeDtypeStruct((256, 128), F32)
    return pl.pallas_call(
        held_kernel,
        in_specs=[vmem()] * 4,
        out_specs=[vmem()] * 3,
        out_shape=[state] * 3,
        compiler_params=params(16),
        cost_estimate=pl.CostEstimate(
            flops=10**7, bytes_accessed=2 * 2**20, transcendentals=2**16
        ),
        name="merge_held_pages",
    )(held, q, new_keys, new_values)


def merge_kernel(fresh, held_acc, held_top, held_total, out):
    top = held_top[:, :1]
    levels = stat_columns(fresh)
    for level in levels:
        top = jnp.maximum(top, level)
    factor = jnp.exp(held_top[:, :1] - top)
    total = held_total[:, :1] * factor
    acc = held_acc[...] * factor
    for n, level in enumerate(levels):
        factor = jnp.exp(level - top)
        total = total + factor
        acc = acc + fresh[n, :256, :].astype(F32) * factor
    out[...] = (acc * (1.0 / total)).astype(BF)


def merge(fresh, state):
    return pl.pallas_call(
        merge_kernel,
        in_specs=[vmem()] * 4,
        out_specs=vmem(),
        out_shape=jax.ShapeDtypeStruct((256, 128), BF),
        compiler_params=params(16),
        cost_estimate=pl.CostEstimate(
            flops=10**7, bytes_accessed=2 * 2**20, transcendentals=2**16
        ),
        name="decode_merge",
    )(fresh, *state)


def page_tables(block_table, cache_len, ships, first_page):
    pages = 128
    page_ids = jnp.arange(pages, dtype=jnp.int32)
    rows, entries = block_table.shape
    code_of = (
        jnp.arange(rows, dtype=jnp.int32)[:, None] * entries
        + jnp.arange(entries, dtype=jnp.int32)[None, :]
    )
    match = block_table[None] == (first_page + page_ids)[:, None, None]
    code = jnp.max(jnp.where(match, code_of[None], -1), axis=(1, 2))
    replaced = jnp.any(ships.reshape(1, -1) == (first_page + page_ids)[:, None], axis=1)
    row = jnp.where(replaced | (code < 0), rows, code // entries)
    onehot = row[:, None] == jnp.arange(rows, dtype=jnp.int32)[None, :]
    length = jnp.sum(jnp.where(onehot, cache_len[None, :], 0), axis=1)
    live = jnp.clip(length - (code % entries) * PAGE_TOKENS, 0, PAGE_TOKENS)
    count = jnp.sum(onehot.astype(jnp.int32), axis=0)
    chunks = (count + 7) // 8
    ids17 = jnp.arange(rows + 1, dtype=jnp.int32)
    ids16 = jnp.arange(rows, dtype=jnp.int32)
    first_chunk = jnp.sum(
        jnp.where(ids16[None, :] < ids17[:, None], chunks[None, :], 0), axis=1
    )
    rank = jnp.sum(
        ((row[None, :] == row[:, None]) & (page_ids[None, :] < page_ids[:, None])).astype(jnp.int32),
        axis=1,
    )
    base = jnp.sum(jnp.where(onehot, first_chunk[None, :rows], 0), axis=1)
    slot = jnp.where(row < rows, base * 8 + rank, -1)
    hit = slot[None, :] == jnp.arange(256, dtype=jnp.int32)[:, None]
    slot_page = jnp.sum(jnp.where(hit, page_ids[None, :], 0), axis=1)
    slot_live = jnp.sum(jnp.where(hit, live[None, :], 0), axis=1)
    return first_chunk, slot_page, slot_live


def token_rows(tables, lengths, ship_page, group):
    rows, entries = tables.shape
    pages = ship_page.shape[0]
    window = pages // 2
    code_of = (
        jnp.arange(rows, dtype=jnp.int32)[:, None] * entries
        + jnp.arange(entries, dtype=jnp.int32)[None, :]
    )
    match = tables[None] == ship_page[:, None, None]
    code = jnp.max(jnp.where(match, code_of[None], -1), axis=(1, 2))
    row = jnp.where(code >= 0, code // entries, -1)
    onehot = row[:, None] == jnp.arange(rows, dtype=jnp.int32)[None, :]
    length = jnp.sum(jnp.where(onehot, lengths[None, :], 0), axis=1)
    live = jnp.clip(length - (code % entries) * PAGE_TOKENS, 0, PAGE_TOKENS)
    live = jnp.where(code >= 0, live, 0)
    page_ids = jnp.arange(pages, dtype=jnp.int32)
    ours = (ship_page // 2048)[None, :] == group[:, None]
    start = jnp.min(jnp.where(ours, page_ids[None, :], window), axis=1)
    start = jnp.minimum(start, window)
    packed = jnp.where(live > 0, row * 32 + live, 0)
    place = start[:, None] + jnp.arange(window, dtype=jnp.int32)[None, :]
    hit = place[:, :, None] == page_ids[None, None, :]
    here = jnp.sum(jnp.where(hit & ours[:, None, :], packed[None, None, :], 0), axis=2)
    token = jnp.arange(PAGE_TOKENS, dtype=jnp.int32)[None, None, :]
    token_row = jnp.where(token < (here % 32)[:, :, None], (here // 32 % 16)[:, :, None], -1)
    return start, token_row.reshape(ROLE, window * PAGE_TOKENS)


def phase(*arrays):
    return lax.optimization_barrier(arrays)


def per_device(
    text_embed,
    vision_rows,
    vision_group,
    vision_slot,
    request_blocks,
    ship_page,
    paged_cache,
    block_table,
    cache_len,
    step_embed,
    norm_gain,
    query_weight,
    keyvalue_weight,
):
    column = lax.axis_index("tp")
    role = lax.axis_index("role")
    core = column % 2
    group_rows, width = text_embed.shape
    steps, rows, _ = step_embed.shape

    role_id = role.reshape(1)

    def plus(a):
        return swap(a, "tp", CORE)

    other_weight = plus(keyvalue_weight)
    weights = (query_weight, keyvalue_weight, other_weight)
    (message,) = phase(pick_rows(vision_group, vision_slot, vision_rows))
    arrived = lax.all_to_all(message, "role", split_axis=0, concat_axis=0, tiled=True)
    merged, squares = land_rows(role_id, arrived, text_embed)
    text_all = lax.all_gather(merged, "tp")

    steps_all = jnp.stack(over_chips(step_embed.reshape(steps * rows, width)))
    meta = jnp.concatenate(
        [block_table.reshape(-1), cache_len, ship_page, jnp.zeros((48,), jnp.int32)]
    ).reshape(33, 128)
    metas = doubling(meta, "role", ROLE_MASKS[:1])
    steps_all, metas = phase(steps_all, metas)
    steps_all = more(steps_all, "tp", CORE)
    step_q, step_a, step_b = step_project(
        (column // 4) ^ jnp.arange(4, dtype=jnp.int32),
        (column % 4).reshape(1),
        steps_all,
        norm_gain,
        *weights,
    )
    new_keys = jnp.where(core == 0, step_a, step_b)
    new_values = jnp.where(core == 0, step_b, step_a)
    own_queries = (
        step_q.reshape(steps, rows, 4, HEAD_SIZE).transpose(1, 0, 2, 3).reshape(rows * 16, HEAD_SIZE)
    )
    metas = more(metas, "role", ROLE_MASKS[1])
    own_queries, metas, squares = phase(own_queries, metas, squares)

    queries = jnp.stack(over_chips(jnp.concatenate([own_queries, squares], axis=0)))
    queries_role = doubling(own_queries, "role", ROLE_MASKS[:1])
    metas = more(metas, "role", ROLE_MASKS[2])
    queries, queries_role, metas = phase(queries, queries_role, metas)

    query_all = more(queries, "tp", CORE)
    parts = jnp.sum(query_all[:, 256:280, :].astype(F32), axis=0)
    ssq = parts[0:8] + parts[8:16] + parts[16:24]
    queries_role = more(queries_role, "role", ROLE_MASKS[1])
    metas = metas.reshape(ROLE, -1)
    tables = metas[:, :4096].reshape(ROLE * rows, -1)
    lengths = metas[:, 4096 : 4096 + rows].reshape(-1)
    ships = metas[:, 4112 : 4112 + 64]
    role_order = role ^ jnp.array(ROLE_OFFSETS, jnp.int32)
    first_page = (role * TP + column) * 128
    first_chunk, slot_page, slot_live = page_tables(block_table, cache_len, ships, first_page)
    difference = column ^ jnp.arange(TP, dtype=jnp.int32)
    where = difference // 2 + 8 * (difference % 2)
    held = paged_attention(first_chunk, slot_page, slot_live, where, query_all, paged_cache)
    held, queries_role, tables = phase(held, queries_role, tables)

    held_parts = lax.all_to_all(held, "tp", split_axis=0, concat_axis=0, tiled=True)
    queries_role = more(queries_role, "role", ROLE_MASKS[2])
    start, token_row = token_rows(tables, lengths, ship_page, role_order)
    state = merge_held(held_parts, own_queries, new_keys, new_values)
    text_all, start, token_row, queries_role, ssq, *state = phase(
        text_all, start, token_row, queries_role, ssq, *state
    )

    keys, values, fresh = finish_keys(
        core.reshape(1),
        start,
        role_order,
        text_all,
        ssq,
        norm_gain,
        weights[1:],
        queries_role,
        token_row,
    )
    fresh_parts = lax.all_to_all(fresh, "role", split_axis=0, concat_axis=0, tiled=True)

    prefill_out = finish_queries(
        request_blocks, text_all, ssq, norm_gain, query_weight, keys, values
    )

    decode = merge(fresh_parts, state)
    decode_out = (
        decode.reshape(rows, steps, 4, HEAD_SIZE).transpose(1, 0, 2, 3).reshape(steps, rows, 512)
    )
    return (prefill_out, decode_out)


def solution(mesh):
    in_specs = (
        P("role", "tp"),
        P("role", "tp"),
        P("role"),
        P("role"),
        P("role", None),
        P("role"),
        P(("role", "tp"), None, None),
        P("role", None),
        P("role"),
        P(None, "role", "tp"),
        P(),
        P(None, "tp"),
        P(None, "tp"),
    )
    out_specs = (P("role", "tp"), P(None, "role", "tp"))
    return jax.shard_map(
        per_device, mesh=mesh, in_specs=in_specs, out_specs=out_specs, check_vma=False
    )
```

```python
import jax
import jax.numpy as jnp
from jax import lax
from jax.experimental import pallas as pl
from jax.experimental.pallas import tpu as pltpu
from jax.sharding import PartitionSpec as P

HEAD_SIZE = 128
KV_HEADS = 8
PAGE_TOKENS = 16
EPS = 1e-06
LOW = -1e30
SCALE = HEAD_SIZE ** (-0.5)
BF = jnp.bfloat16
F32 = jnp.float32
EXP2_SCALE = SCALE * 1.4426950408889634
LN2 = 0.6931471805599453
TP = 16
ROLE = 8
STAT_ROWS = 16

CORE = 1
TP_MASKS = (2, 4, 12, CORE)
ROLE_MASKS = (4, 1, 3)


def params(mebibytes):
    return pltpu.CompilerParams(vmem_limit_bytes=mebibytes * 2**20)


def vmem():
    return pl.BlockSpec(memory_space=pltpu.VMEM)


def smem():
    return pl.BlockSpec(memory_space=pltpu.SMEM)


def hbm():
    return pl.BlockSpec(memory_space=pl.ANY)


def swap(x, axis, mask):
    size = TP if axis == "tp" else ROLE
    return lax.ppermute(x, axis, [(i, i ^ mask) for i in range(size)])


def more(held, axis, mask):
    return jnp.concatenate([held, swap(held, axis, mask)], axis=0)


def doubling(x, axis, masks):
    held = x[None]
    for mask in masks:
        held = more(held, axis, mask)
    return held


def offsets(masks):
    table = [0]
    for mask in masks:
        table = table + [v ^ mask for v in table]
    return table


ROLE_OFFSETS = offsets(ROLE_MASKS)


def nt_dot(a, b):
    return lax.dot_general(a, b, (((1,), (1,)), ((), ())), preferred_element_type=F32)


def nn_dot(a, b):
    return jnp.dot(a, b, preferred_element_type=F32)


def eye(n):
    return lax.broadcasted_iota(jnp.int32, (n, n), 0) == lax.broadcasted_iota(
        jnp.int32, (n, n), 1
    )


def to_row(column):
    n = column.shape[0]
    return jnp.sum(jnp.where(eye(n), column, 0.0), axis=0, keepdims=True)


def to_column(row):
    n = row.shape[1]
    return jnp.sum(jnp.where(eye(n), row, 0.0), axis=1, keepdims=True)


def split3(x):
    high = x.astype(BF)
    rest = x - high.astype(F32)
    middle = rest.astype(BF)
    low = (rest - middle.astype(F32)).astype(BF)
    return high, middle, low


def stat_block(level):
    parts = jnp.concatenate(
        [to_row(level[:128]), to_row(level[128:]), jnp.zeros((6, 128), F32)], axis=0
    )
    high, middle, low = split3(parts)
    return jnp.concatenate(
        [
            high[:2].astype(F32),
            middle[:2].astype(F32),
            low[:2].astype(F32),
            jnp.zeros((10, 128), F32),
        ],
        axis=0,
    ).astype(BF)


def stat_rows(block):
    wide = block.astype(F32)
    return wide[0:2] + wide[2:4] + wide[4:6]


def pick_kernel(group, slot, ships, rows, out):
    count = group.shape[1]
    capacity = 2 * count // ROLE
    onehot = group[...] == lax.broadcasted_iota(jnp.int32, (ROLE, 1), 0)
    before = lax.broadcasted_iota(jnp.int32, (count, count), 0) < lax.broadcasted_iota(
        jnp.int32, (count, count), 1
    )
    rank = nn_dot(onehot.astype(F32).astype(BF), before.astype(F32).astype(BF))
    rank = jnp.sum(jnp.where(onehot, rank, 0.0), axis=0, keepdims=True).astype(jnp.int32)
    place = group[...] * capacity + rank
    picked = place == lax.broadcasted_iota(jnp.int32, (ROLE * capacity, 1), 0)
    picked = picked.astype(F32).astype(BF)
    chosen = nn_dot(picked, rows[...]).astype(BF)
    code = slot[...] + 1
    line = lax.broadcasted_iota(jnp.int32, (16, 1), 0)
    codes = jnp.where(line == 0, code // 32, jnp.where(line == 1, code % 32, 0))
    codes = nt_dot(codes.astype(F32).astype(BF), picked)
    page = jnp.concatenate(
        [ships[...], jnp.zeros((1, ROLE * capacity - ships.shape[1]), jnp.int32)], axis=1
    )
    pages = jnp.where(line == 2, page // 128, jnp.where(line == 3, page % 128, 0))
    codes = (codes + pages.astype(F32)).astype(BF)
    for g in range(ROLE):
        out[g, :capacity, :] = chosen[g * capacity : (g + 1) * capacity]
        out[g, capacity:, :] = codes


def pick_rows(group, slot, ships, rows):
    count, width = rows.shape
    capacity = 2 * count // ROLE
    return pl.pallas_call(
        pick_kernel,
        in_specs=[vmem()] * 4,
        out_specs=vmem(),
        out_shape=jax.ShapeDtypeStruct((ROLE, capacity + 16, width), BF),
        compiler_params=params(16),
        cost_estimate=pl.CostEstimate(flops=2 * 10**8, bytes_accessed=2**20, transcendentals=0),
        name="pick_rows",
    )(group.reshape(1, count), slot.reshape(1, count), ships.reshape(1, -1), rows)


def land_kernel(role, arrived, text, merged, squares):
    capacity = arrived.shape[1] - 16
    total = ROLE * capacity
    lane = lax.broadcasted_iota(jnp.int32, (1, total), 1)
    slots = jnp.zeros((1, total), F32)
    for s in range(ROLE):
        codes = arrived[s, capacity:, :].astype(F32)
        code = jnp.broadcast_to(codes[0:1] * 32.0 + codes[1:2], (8, total))
        shift = ((s + ROLE - role[0]) % ROLE) * capacity
        slots = jnp.where(lane // capacity == s, pltpu.roll(code, shift, 1)[0:1], slots)
    slots = slots.astype(jnp.int32) - 1
    rows = arrived[:, :capacity, :].reshape(total, arrived.shape[2])
    lines = []
    for n in range(text.shape[0] // 256):
        at = slice(n * 256, (n + 1) * 256)
        row = lax.broadcasted_iota(jnp.int32, (256, 1), 0) + n * 256
        landing = jnp.where(row == slots, 1.0, 0.0)
        hit = jnp.sum(landing, axis=1, keepdims=True) > 0.0
        block = jnp.where(hit, nn_dot(landing.astype(BF), rows), text[at, :].astype(F32))
        merged[at, :] = block.astype(BF)
        square = jnp.broadcast_to(jnp.sum(block * block, axis=1, keepdims=True), (256, 128))
        lines += [to_row(square[:128]), to_row(square[128:])]
    high, middle, rest = split3(jnp.concatenate(lines, axis=0))
    squares[...] = jnp.concatenate(
        [high.astype(F32), middle.astype(F32), rest.astype(F32), jnp.zeros((8, 128), F32)], axis=0
    ).astype(BF)


def land_rows(role, arrived, text):
    return pl.pallas_call(
        land_kernel,
        in_specs=[smem()] + [vmem()] * 2,
        out_specs=[vmem()] * 2,
        out_shape=[
            jax.ShapeDtypeStruct(text.shape, BF),
            jax.ShapeDtypeStruct((32, 128), BF),
        ],
        compiler_params=params(24),
        cost_estimate=pl.CostEstimate(flops=10**9, bytes_accessed=6 * 2**20, transcendentals=0),
        name="land_rows",
    )(role, arrived, text)


def step_kernel(order, low, xs, gain, wq, wa, wb, q_out, a_out, b_out, scale, acc):
    i = pl.program_id(0)

    @pl.when(i == 0)
    def _():
        total = jnp.zeros((xs.shape[1], 512), F32)
        for k in range(TP):
            wide = xs[k].astype(F32)
            total = total + wide * wide
        total = jnp.sum(total, axis=1, keepdims=True)
        scale[...] = jnp.broadcast_to(
            lax.rsqrt(total / (TP * xs.shape[2]) + EPS), scale.shape
        )
        acc[...] = jnp.zeros_like(acc)

    factor = jnp.broadcast_to(scale[:, :1], (xs.shape[1], 512))
    total_q = acc[:, :512]
    total_a = acc[:, 512:640]
    total_b = acc[:, 640:768]
    for j in range(4):
        place = low[0] ^ j
        block = j // 2 + 2 * i + 8 * (j % 2)
        rows = pl.ds(pl.multiple_of(place * 512, 512), 512)
        normed = (xs[block].astype(F32) * factor * gain[0, place].astype(F32)).astype(BF)
        total_q = total_q + nn_dot(normed, wq[rows, :])
        total_a = total_a + nn_dot(normed, wa[rows, :])
        total_b = total_b + nn_dot(normed, wb[rows, :])
    acc[:, :512] = total_q
    acc[:, 512:640] = total_a
    acc[:, 640:768] = total_b

    @pl.when(i == 3)
    def _():
        q_out[...] = acc[:, :512].astype(BF)
        a_out[...] = acc[:, 512:640].astype(BF)
        b_out[...] = acc[:, 640:768].astype(BF)


def step_project(order, low, xs, gain, wq, wa, wb):
    rows = xs.shape[1]
    return pl.pallas_call(
        step_kernel,
        grid_spec=pltpu.PrefetchScalarGridSpec(
            num_scalar_prefetch=2,
            grid=(4,),
            in_specs=[
                pl.BlockSpec(xs.shape, lambda i, o, l: (0, 0, 0)),
                pl.BlockSpec((1, 4, 1, 512), lambda i, o, l: (o[i], 0, 0, 0)),
                pl.BlockSpec((2048, 512), lambda i, o, l: (o[i], 0)),
                pl.BlockSpec((2048, 128), lambda i, o, l: (o[i], 0)),
                pl.BlockSpec((2048, 128), lambda i, o, l: (o[i], 0)),
            ],
            out_specs=[
                pl.BlockSpec((rows, 512), lambda i, o, l: (0, 0)),
                pl.BlockSpec((rows, 128), lambda i, o, l: (0, 0)),
                pl.BlockSpec((rows, 128), lambda i, o, l: (0, 0)),
            ],
            scratch_shapes=[pltpu.VMEM((rows, 128), F32), pltpu.VMEM((rows, 768), F32)],
        ),
        out_shape=[
            jax.ShapeDtypeStruct((rows, 512), BF),
            jax.ShapeDtypeStruct((rows, 128), BF),
            jax.ShapeDtypeStruct((rows, 128), BF),
        ],
        compiler_params=params(58),
        cost_estimate=pl.CostEstimate(
            flops=2 * rows * 8192 * 768, bytes_accessed=14 * 2**20, transcendentals=0
        ),
        name="step_project",
    )(order, low, xs, gain.reshape(4, 4, 1, 512), wq, wa, wb)


def row_factors(ssq, line, scale):
    factor = lax.rsqrt(ssq[...] / (TP * 512) + EPS)
    for n in range(scale.shape[0] // 128):
        scale[n * 128 : (n + 1) * 128, :] = jnp.broadcast_to(
            to_column(factor[line + n : line + n + 1]), (128, 128)
        )


def all_blocks(text, gain, weights, scale, xbuf, wbuf, xsem, wsem, acc):
    blocks, rows = text.shape[0], text.shape[1]
    widths = [weight.shape[1] for weight in weights]

    def part(n, k):
        return wbuf.at[n // 4, pl.ds(n % 4 * 512, 512), pl.ds(sum(widths[:k]), widths[k])]

    for n in range(blocks):
        pltpu.make_async_copy(text.at[n], xbuf.at[n], xsem.at[n]).start()
        for k, weight in enumerate(weights):
            pltpu.make_async_copy(weight.at[pl.ds(n * 512, 512)], part(n, k), wsem.at[n, k]).start()

    for i in range(blocks // 4):
        for n in range(4 * i, 4 * i + 4):
            pltpu.make_async_copy(xbuf.at[n], xbuf.at[n], xsem.at[n]).wait()
            for k in range(len(weights)):
                pltpu.make_async_copy(part(n, k), part(n, k), wsem.at[n, k]).wait()
        gains = [gain[4 * i + k].astype(F32) for k in range(4)]
        for r in range(rows // 256):
            at = slice(r * 256, (r + 1) * 256)
            factor = scale[at, :1]
            normed = jnp.concatenate(
                [
                    (xbuf[4 * i + k, at, :].astype(F32) * factor * gains[k]).astype(BF)
                    for k in range(4)
                ],
                axis=1,
            )
            product = nn_dot(normed, wbuf[i])
            if i == 0:
                acc[at, :] = product
            else:
                acc[at, :] += product


def all_scratch(blocks, rows, width, kinds):
    return [
        pltpu.VMEM((blocks, rows, 512), BF),
        pltpu.VMEM((blocks // 4, 2048, width), BF),
        pltpu.VMEM((rows, 128), F32),
        pltpu.SemaphoreType.DMA((blocks,)),
        pltpu.SemaphoreType.DMA((blocks, kinds)),
        pltpu.VMEM((rows, width), F32),
    ]


def keys_kernel(
    core, start, group, text, ssq, gain, wq, wa, wb, q, token_row,
    queries, keys, values, out, xbuf, wbuf, scale, xsem, wsem, acc,
):
    row_factors(ssq, 0, scale)
    all_blocks(text, gain, (wq, wa, wb), scale, xbuf, wbuf, xsem, wsem, acc)
    for n in range(acc.shape[0] // 256):
        at = slice(n * 256, (n + 1) * 256)
        queries[at, :] = acc[at, :512].astype(BF)
        own, other = acc[at, 512:640], acc[at, 640:]
        keys[at, :] = jnp.where(core[0] == 0, own, other).astype(BF)
        values[at, :] = jnp.where(core[0] == 0, other, own).astype(BF)
    fresh_groups(group, start, q, keys, values, token_row, out)


def finish_keys(core, start, group, text, ssq, gain, weights, q, token_row):
    blocks, rows, _ = text.shape
    return pl.pallas_call(
        keys_kernel,
        in_specs=[smem()] * 3 + [hbm()] + [vmem()] * 2 + [hbm()] * 3 + [vmem()] * 2,
        out_specs=[vmem()] * 4,
        out_shape=[
            jax.ShapeDtypeStruct((rows, 512), BF),
            jax.ShapeDtypeStruct((rows, 128), BF),
            jax.ShapeDtypeStruct((rows, 128), BF),
            jax.ShapeDtypeStruct((ROLE, 256 + STAT_ROWS, 128), BF),
        ],
        scratch_shapes=all_scratch(blocks, rows, 768, 3),
        compiler_params=params(58),
        cost_estimate=pl.CostEstimate(
            flops=6 * 10**9, bytes_accessed=20 * 2**20, transcendentals=2**20
        ),
        name="keys_and_fresh_pages",
    )(
        core, start, group, text, ssq, gain.reshape(TP, 1, 512), *weights, q, token_row
    )


def attend_kernel(blocks_ref, q, keys, values, out):
    position = lax.broadcasted_iota(jnp.int32, (1, q.shape[0]), 1)
    segment = jnp.zeros((1, q.shape[0]), F32)
    end = 0
    for n in range(blocks_ref.shape[1]):
        end = end + blocks_ref[0, n] * PAGE_TOKENS
        segment = segment + jnp.where(position >= end, 1.0, 0.0)
    prefill_kernel(q, keys, values, segment, out)


def prefill_attention(request_blocks, q, keys, values):
    return pl.pallas_call(
        attend_kernel,
        in_specs=[smem()] + [vmem()] * 3,
        out_specs=vmem(),
        out_shape=jax.ShapeDtypeStruct(q.shape, BF),
        compiler_params=params(24),
        cost_estimate=pl.CostEstimate(
            flops=3 * 10**9, bytes_accessed=3 * 2**20, transcendentals=3 * 2**20
        ),
        name="prefill_attention",
    )(request_blocks, q, keys, values)


def paged_kernel(
    first_chunk, slot_page, slot_live, where, q, cache, out, kv, top, total, acc, lse, sem
):
    def fetch(i, carry):
        for j in range(8):
            pltpu.make_async_copy(
                cache.at[slot_page[i * 8 + j]],
                kv.at[i, pl.ds(j * PAGE_TOKENS, PAGE_TOKENS), :],
                sem.at[i],
            ).start()
        return carry

    lax.fori_loop(0, first_chunk[16], fetch, 0)
    lane = lax.broadcasted_iota(jnp.int32, (1, 128), 1)
    heads = range(KV_HEADS)

    def one_row(r, carry):
        top[...] = jnp.full_like(top, LOW)
        total[...] = jnp.zeros_like(total)
        acc[...] = jnp.zeros_like(acc)
        at = pl.multiple_of(r * 16, 16)
        queries = [
            jnp.concatenate(
                [q[where[2 * k], pl.ds(at, 16), :], q[where[2 * k + 1], pl.ds(at, 16), :]], axis=0
            )
            for k in heads
        ]

        def one_chunk(i, inner):
            live = jnp.zeros((1, 128), jnp.int32)
            for j in range(8):
                live = jnp.where(lane // PAGE_TOKENS == j, slot_live[i * 8 + j], live)
            valid = lane % PAGE_TOKENS < live
            pltpu.make_async_copy(kv.at[i], kv.at[i], sem.at[i]).wait()

            def part(column):
                return kv[i, :, column * 128 : (column + 1) * 128]

            scores = [jnp.where(valid, nt_dot(queries[k], part(2 * k)), LOW) for k in heads]
            old = [top[k * 32 : (k + 1) * 32, :] for k in heads]
            new = [jnp.maximum(old[k], jnp.max(scores[k], axis=1, keepdims=True)) for k in heads]
            weights = [
                jnp.where(valid, jnp.exp2((scores[k] - new[k]) * EXP2_SCALE), 0.0) for k in heads
            ]
            products = [nn_dot(weights[k].astype(BF), part(2 * k + 1)) for k in heads]
            for k in heads:
                rows = slice(k * 32, (k + 1) * 32)
                fade = jnp.exp2((old[k] - new[k]) * EXP2_SCALE)
                top[rows, :] = new[k]
                total[rows, :] = total[rows, :] * fade + jnp.sum(weights[k], axis=1, keepdims=True)
                acc[rows, :] = acc[rows, :] * fade + products[k]
            return inner

        lax.fori_loop(first_chunk[r], first_chunk[r + 1], one_chunk, 0)
        some = total[...] > 0.0
        divisor = jnp.where(some, total[...], 1.0)
        result = (acc[...] * (1.0 / divisor)).astype(BF)
        level = jnp.where(some, top[...] * SCALE + jnp.log(divisor), LOW)
        for t in range(TP):
            out[t, pl.ds(at, 16), :] = result[t * 16 : (t + 1) * 16]
            lse[t, pl.ds(at, 16), :] = level[t * 16 : (t + 1) * 16]
        return carry

    lax.fori_loop(0, 16, one_row, 0)

    def one_target(t, carry):
        out[t, 256:272, :] = stat_block(lse[t])
        return carry

    lax.fori_loop(0, TP, one_target, 0)


def paged_attention(first_chunk, slot_page, slot_live, where, q, cache):
    return pl.pallas_call(
        paged_kernel,
        in_specs=[smem()] * 4 + [vmem(), hbm()],
        out_specs=vmem(),
        out_shape=jax.ShapeDtypeStruct((TP, 256 + STAT_ROWS, 128), BF),
        scratch_shapes=[
            pltpu.VMEM((32, 128, 2048), BF),
            pltpu.VMEM((256, 128), F32),
            pltpu.VMEM((256, 128), F32),
            pltpu.VMEM((256, 128), F32),
            pltpu.VMEM((TP, 256, 128), F32),
            pltpu.SemaphoreType.DMA((32,)),
        ],
        compiler_params=params(58),
        cost_estimate=pl.CostEstimate(
            flops=2 * 10**9, bytes_accessed=12 * 2**20, transcendentals=2**20
        ),
        name="paged_attention",
    )(first_chunk, slot_page, slot_live, where, q, cache)


def fresh_groups(group, start, q, keys, values, token_row, out):
    span = token_row.shape[1]
    for i in range(ROLE):
        rows = pl.ds(pl.multiple_of(start[i] * PAGE_TOKENS, PAGE_TOKENS), span)
        row = lax.broadcasted_iota(jnp.int32, (256, 1), 0) // 16
        valid = token_row[i : i + 1, :] == row
        scores = jnp.where(valid, nt_dot(q[i, :256, :], keys[rows, :]), LOW)
        top = jnp.maximum(jnp.max(scores, axis=1, keepdims=True), 0.5 * LOW)
        weights = jnp.exp2((scores - top) * EXP2_SCALE)
        total = jnp.sum(weights, axis=1, keepdims=True)
        acc = nn_dot(weights.astype(BF), values[rows, :])
        some = total > 0.0
        divisor = jnp.where(some, total, 1.0)
        target = group[i]
        out[target, :256, :] = (acc * (1.0 / divisor)).astype(BF)
        out[target, 256:272, :] = stat_block(
            jnp.where(some, top * SCALE + jnp.log(divisor), LOW)
        )


def prefill_kernel(q, keys, values, seg_row, out):
    rows = q.shape[0]
    for tile in range(rows // 256):
        high = (tile + 1) * 256
        low = max(0, (tile * 256 - 511) // 256 * 256)
        span = high - low
        seg_keys = seg_row[:, low:high]
        seg_queries = to_column(seg_row[:, tile * 256 : high])
        row = lax.broadcasted_iota(jnp.int32, (256, span), 0) + tile * 256
        column = lax.broadcasted_iota(jnp.int32, (256, span), 1) + low
        valid = (seg_keys == seg_queries) & (column <= row)
        for h in range(4):
            lanes = slice(h * 128, (h + 1) * 128)
            scores = nt_dot(q[tile * 256 : high, lanes], keys[low:high, :])
            scores = jnp.where(valid, scores, LOW)
            top = jnp.max(scores, axis=1, keepdims=True)
            weights = jnp.exp2((scores - top) * EXP2_SCALE)
            total = jnp.sum(weights, axis=1, keepdims=True)
            weights = (weights * (1.0 / total)).astype(BF)
            out[tile * 256 : high, lanes] = nn_dot(weights, values[low:high, :]).astype(BF)


def stat_columns(parts):
    rows = [stat_rows(parts[n, 256:272, :]) for n in range(parts.shape[0])]
    rows.append(jnp.zeros((128 - 2 * len(rows), 128), F32))
    columns = jnp.concatenate(rows, axis=0).T
    return [
        jnp.concatenate([columns[:, 2 * n : 2 * n + 1], columns[:, 2 * n + 1 : 2 * n + 2]], axis=0)
        for n in range(parts.shape[0])
    ]


def held_kernel(held, q, new_keys, new_values, out, top_out, total_out):
    row = lax.broadcasted_iota(jnp.int32, (256, 64), 0)
    key = lax.broadcasted_iota(jnp.int32, (256, 64), 1)
    valid = (row // 16 == key % 16) & (key // 16 <= row % 16 // 4)
    scores = jnp.where(valid, nt_dot(q[...], new_keys[...]) * SCALE, LOW)
    top = jnp.max(scores, axis=1, keepdims=True)
    levels = stat_columns(held)
    for level in levels:
        top = jnp.maximum(top, level)
    weights = jnp.where(valid, jnp.exp(scores - top), 0.0)
    total = jnp.sum(weights, axis=1, keepdims=True)
    acc = nn_dot(weights.astype(BF), new_values[...])
    for n, level in enumerate(levels):
        factor = jnp.exp(level - top)
        total = total + factor
        acc = acc + held[n, :256, :].astype(F32) * factor
    out[...] = acc
    top_out[...] = jnp.broadcast_to(top, top_out.shape)
    total_out[...] = jnp.broadcast_to(total, total_out.shape)


def merge_held(held, q, new_keys, new_values):
    state = jax.ShapeDtypeStruct((256, 128), F32)
    return pl.pallas_call(
        held_kernel,
        in_specs=[vmem()] * 4,
        out_specs=[vmem()] * 3,
        out_shape=[state] * 3,
        compiler_params=params(16),
        cost_estimate=pl.CostEstimate(
            flops=10**7, bytes_accessed=2 * 2**20, transcendentals=2**16
        ),
        name="merge_held_pages",
    )(held, q, new_keys, new_values)


def merge_kernel(fresh, held_acc, held_top, held_total, out):
    top = held_top[:, :1]
    levels = stat_columns(fresh)
    for level in levels:
        top = jnp.maximum(top, level)
    factor = jnp.exp(held_top[:, :1] - top)
    total = held_total[:, :1] * factor
    acc = held_acc[...] * factor
    for n, level in enumerate(levels):
        factor = jnp.exp(level - top)
        total = total + factor
        acc = acc + fresh[n, :256, :].astype(F32) * factor
    out[...] = (acc * (1.0 / total)).astype(BF)


def merge(fresh, state):
    return pl.pallas_call(
        merge_kernel,
        in_specs=[vmem()] * 4,
        out_specs=vmem(),
        out_shape=jax.ShapeDtypeStruct((256, 128), BF),
        compiler_params=params(16),
        cost_estimate=pl.CostEstimate(
            flops=10**7, bytes_accessed=2 * 2**20, transcendentals=2**16
        ),
        name="decode_merge",
    )(fresh, *state)


def find_kernel(table, length, pages, row_out, live_out):
    code = jnp.full(pages.shape, -1.0, F32)
    entry = lax.broadcasted_iota(jnp.int32, (128, 1), 0).astype(F32)
    for r in range(table.shape[0]):
        for n in range(table.shape[1] // 128):
            column = to_column(table[r : r + 1, n * 128 : (n + 1) * 128].astype(F32))
            found = jnp.where(column == pages[...], entry + (r * 256 + n * 128), -1.0)
            code = jnp.maximum(code, jnp.max(found, axis=0, keepdims=True))
    code = code.astype(jnp.int32)
    row = jnp.where(code >= 0, code // 256, -1)
    tokens = jnp.zeros(row.shape, jnp.int32)
    for r in range(table.shape[0]):
        tokens = jnp.where(row == r, length[r], tokens)
    row_out[...] = row
    live_out[...] = jnp.where(row >= 0, jnp.clip(tokens - code % 256 * PAGE_TOKENS, 0, PAGE_TOKENS), 0)


def find_pages(block_table, cache_len, pages):
    count = pages.shape[0]
    line = jax.ShapeDtypeStruct((1, count), jnp.int32)
    row, live = pl.pallas_call(
        find_kernel,
        in_specs=[vmem(), smem(), vmem()],
        out_specs=[vmem()] * 2,
        out_shape=[line] * 2,
        compiler_params=params(16),
        cost_estimate=pl.CostEstimate(flops=10**7, bytes_accessed=2**16, transcendentals=0),
        name="find_pages",
    )(block_table, cache_len, pages.astype(F32).reshape(1, count))
    return row[0], live[0]


def page_tables(row, live, replaced, rows):
    page_ids = jnp.arange(row.shape[0], dtype=jnp.int32)
    row = jnp.where(replaced | (row < 0), rows, row)
    onehot = row[:, None] == jnp.arange(rows, dtype=jnp.int32)[None, :]
    count = jnp.sum(onehot.astype(jnp.int32), axis=0)
    chunks = (count + 7) // 8
    ids17 = jnp.arange(rows + 1, dtype=jnp.int32)
    ids16 = jnp.arange(rows, dtype=jnp.int32)
    first_chunk = jnp.sum(
        jnp.where(ids16[None, :] < ids17[:, None], chunks[None, :], 0), axis=1
    )
    rank = jnp.sum(
        ((row[None, :] == row[:, None]) & (page_ids[None, :] < page_ids[:, None])).astype(jnp.int32),
        axis=1,
    )
    base = jnp.sum(jnp.where(onehot, first_chunk[None, :rows], 0), axis=1)
    slot = jnp.where(row < rows, base * 8 + rank, -1)
    hit = slot[None, :] == jnp.arange(256, dtype=jnp.int32)[:, None]
    slot_page = jnp.sum(jnp.where(hit, page_ids[None, :], 0), axis=1)
    slot_live = jnp.sum(jnp.where(hit, live[None, :], 0), axis=1)
    return first_chunk, slot_page, slot_live


def token_rows(row, live, ship_page, group):
    pages = ship_page.shape[0]
    window = pages // 2
    page_ids = jnp.arange(pages, dtype=jnp.int32)
    ours = (ship_page // 2048)[None, :] == group[:, None]
    start = jnp.min(jnp.where(ours, page_ids[None, :], window), axis=1)
    start = jnp.minimum(start, window)
    packed = jnp.where(ours & (live > 0), row * 32 + live, 0)
    place = start[:, None] + jnp.arange(window, dtype=jnp.int32)[None, :]
    hit = place[:, :, None] == page_ids[None, None, :]
    here = jnp.sum(jnp.where(hit, packed[:, None, :], 0), axis=2)
    token = jnp.arange(PAGE_TOKENS, dtype=jnp.int32)[None, None, :]
    token_row = jnp.where(token < (here % 32)[:, :, None], (here // 32)[:, :, None], -1)
    return start, token_row.reshape(ROLE, window * PAGE_TOKENS)


def phase(*arrays):
    return lax.optimization_barrier(arrays)


def per_device(
    text_embed,
    vision_rows,
    vision_group,
    vision_slot,
    request_blocks,
    ship_page,
    paged_cache,
    block_table,
    cache_len,
    step_embed,
    norm_gain,
    query_weight,
    keyvalue_weight,
):
    column = lax.axis_index("tp")
    role = lax.axis_index("role")
    core = column % 2
    group_rows, width = text_embed.shape
    steps, rows, _ = step_embed.shape

    role_id = role.reshape(1)

    def plus(a):
        return swap(a, "tp", CORE)

    other_weight = plus(keyvalue_weight)
    weights = (query_weight, keyvalue_weight, other_weight)
    (message,) = phase(pick_rows(vision_group, vision_slot, ship_page, vision_rows))
    arrived = lax.all_to_all(message, "role", split_axis=0, concat_axis=0, tiled=True)
    steps_y = doubling(step_embed.reshape(steps * rows, width), "tp", TP_MASKS[:2])
    arrived, steps_y = phase(arrived, steps_y)
    merged, squares = land_rows(role_id, arrived, text_embed)
    text_all = lax.all_gather(merged, "tp")

    first_page = (role * TP + column) * 128
    parts = arrived[:, 64 + 2 : 64 + 4, : ship_page.shape[0]].astype(jnp.int32)
    ships = parts[:, 0] * 128 + parts[:, 1]
    page_ids = first_page + jnp.arange(paged_cache.shape[0], dtype=jnp.int32)
    held_count = page_ids.shape[0]
    row_of, live_of = find_pages(
        block_table, cache_len, jnp.concatenate([page_ids, ships.reshape(-1)])
    )
    codes = jnp.concatenate(
        [
            row_of[held_count:].reshape(4, 128),
            live_of[held_count:].reshape(4, 128),
            jnp.zeros((8, 128), jnp.int32),
        ],
        axis=0,
    ).astype(BF)
    steps_all = more(more(steps_y, "tp", TP_MASKS[2]), "tp", CORE)
    step_q, step_a, step_b = step_project(
        (column // 4) ^ jnp.array([0, 1, 3, 2], jnp.int32),
        (column % 4).reshape(1),
        steps_all,
        norm_gain,
        *weights,
    )
    new_keys = jnp.where(core == 0, step_a, step_b)
    new_values = jnp.where(core == 0, step_b, step_a)
    own_queries = (
        step_q.reshape(steps, rows, 4, HEAD_SIZE).transpose(1, 0, 2, 3).reshape(rows * 16, HEAD_SIZE)
    )
    own_queries, squares, codes = phase(own_queries, squares, codes)

    query_all = doubling(jnp.concatenate([own_queries, squares], axis=0), "tp", TP_MASKS)
    replaced = jnp.any(ships.reshape(1, -1) == page_ids[:, None], axis=1)
    first_chunk, slot_page, slot_live = page_tables(
        row_of[:held_count], live_of[:held_count], replaced, rows
    )
    role_message = jnp.concatenate([own_queries, codes], axis=0)
    queries_role = doubling(role_message, "role", ROLE_MASKS[:1])
    difference = column ^ jnp.arange(TP, dtype=jnp.int32)
    far_bit = difference // 8
    near_bit = (difference // 4) % 2 ^ far_bit
    where = difference // 2 % 2 + 2 * near_bit + 4 * far_bit + 8 * (difference % 2)
    held = paged_attention(first_chunk, slot_page, slot_live, where, query_all, paged_cache)
    held, queries_role = phase(held, queries_role)

    held_parts = lax.all_to_all(held, "tp", split_axis=0, concat_axis=0, tiled=True)
    sums = jnp.sum(query_all[:, 256:280, :].astype(F32), axis=0)
    ssq = sums[0:8] + sums[8:16] + sums[16:24]
    queries_role = more(more(queries_role, "role", ROLE_MASKS[1]), "role", ROLE_MASKS[2])
    role_order = role ^ jnp.array(ROLE_OFFSETS, jnp.int32)
    info = queries_role[:, 256:264, :].reshape(ROLE, 2, ROLE * ship_page.shape[0])
    info = lax.dynamic_slice_in_dim(info, role * ship_page.shape[0], ship_page.shape[0], 2)
    info = info.astype(jnp.int32)
    start, token_row = token_rows(info[:, 0], info[:, 1], ship_page, role_order)
    text_all, start, token_row, queries_role, ssq = phase(
        text_all, start, token_row, queries_role, ssq
    )

    prefill_queries, keys, values, fresh = finish_keys(
        core.reshape(1),
        start,
        role_order,
        text_all,
        ssq,
        norm_gain,
        weights,
        queries_role,
        token_row,
    )
    fresh, held_parts = phase(fresh, held_parts)
    fresh_parts = lax.all_to_all(fresh, "role", split_axis=0, concat_axis=0, tiled=True)

    prefill_out = prefill_attention(request_blocks, prefill_queries, keys, values)
    state = merge_held(held_parts, own_queries, new_keys, new_values)

    decode = merge(fresh_parts, state)
    decode_out = (
        decode.reshape(rows, steps, 4, HEAD_SIZE).transpose(1, 0, 2, 3).reshape(steps, rows, 512)
    )
    return (prefill_out, decode_out)


def solution(mesh):
    in_specs = (
        P("role", "tp"),
        P("role", "tp"),
        P("role"),
        P("role"),
        P("role", None),
        P("role"),
        P(("role", "tp"), None, None),
        P("role", None),
        P("role"),
        P(None, "role", "tp"),
        P(),
        P(None, "tp"),
        P(None, "tp"),
    )
    out_specs = (P("role", "tp"), P(None, "role", "tp"))
    return jax.shard_map(
        per_device, mesh=mesh, in_specs=in_specs, out_specs=out_specs, check_vma=False
    )
```

```python
import jax
import jax.numpy as jnp
from jax import lax
from jax.experimental import pallas as pl
from jax.experimental.pallas import tpu as pltpu
from jax.sharding import PartitionSpec as P

HEAD_SIZE = 128
KV_HEADS = 8
PAGE_TOKENS = 16
EPS = 1e-06
LOW = -1e30
SCALE = HEAD_SIZE ** (-0.5)
BF = jnp.bfloat16
F32 = jnp.float32
EXP2_SCALE = SCALE * 1.4426950408889634
LN2 = 0.6931471805599453
TP = 16
ROLE = 8
STAT_ROWS = 16

CORE = 1
TP_MASKS = (2, 4, 12, CORE)
ROLE_MASKS = (4, 1, 3)


def params(mebibytes):
    return pltpu.CompilerParams(vmem_limit_bytes=mebibytes * 2**20)


def vmem():
    return pl.BlockSpec(memory_space=pltpu.VMEM)


def smem():
    return pl.BlockSpec(memory_space=pltpu.SMEM)


def hbm():
    return pl.BlockSpec(memory_space=pl.ANY)


def swap(x, axis, mask):
    size = TP if axis == "tp" else ROLE
    return lax.ppermute(x, axis, [(i, i ^ mask) for i in range(size)])


def more(held, axis, mask):
    return jnp.concatenate([held, swap(held, axis, mask)], axis=0)


def doubling(x, axis, masks):
    held = x[None]
    for mask in masks:
        held = more(held, axis, mask)
    return held


def offsets(masks):
    table = [0]
    for mask in masks:
        table = table + [v ^ mask for v in table]
    return table


ROLE_OFFSETS = offsets(ROLE_MASKS)


def nt_dot(a, b):
    return lax.dot_general(a, b, (((1,), (1,)), ((), ())), preferred_element_type=F32)


def nn_dot(a, b):
    return jnp.dot(a, b, preferred_element_type=F32)


def eye(n):
    return lax.broadcasted_iota(jnp.int32, (n, n), 0) == lax.broadcasted_iota(
        jnp.int32, (n, n), 1
    )


def to_row(column):
    n = column.shape[0]
    return jnp.sum(jnp.where(eye(n), column, 0.0), axis=0, keepdims=True)


def to_column(row):
    n = row.shape[1]
    return jnp.sum(jnp.where(eye(n), row, 0.0), axis=1, keepdims=True)


def split3(x):
    high = x.astype(BF)
    rest = x - high.astype(F32)
    middle = rest.astype(BF)
    low = (rest - middle.astype(F32)).astype(BF)
    return high, middle, low


def stat_block(level):
    parts = jnp.concatenate(
        [to_row(level[:128]), to_row(level[128:]), jnp.zeros((6, 128), F32)], axis=0
    )
    high, middle, low = split3(parts)
    return jnp.concatenate(
        [
            high[:2].astype(F32),
            middle[:2].astype(F32),
            low[:2].astype(F32),
            jnp.zeros((10, 128), F32),
        ],
        axis=0,
    ).astype(BF)


def stat_rows(block):
    wide = block.astype(F32)
    return wide[0:2] + wide[2:4] + wide[4:6]


def pick_kernel(group_in, slot_in, ships_in, rows_in, out, group, slot, ships, rows, sem):
    pairs = ((group_in, group), (slot_in, slot), (ships_in, ships), (rows_in, rows))
    copies = [pltpu.make_async_copy(a, b, sem.at[n]) for n, (a, b) in enumerate(pairs)]
    for copy in copies:
        copy.start()
    for copy in copies:
        copy.wait()
    count = group.shape[1]
    capacity = 2 * count // ROLE
    onehot = group[...] == lax.broadcasted_iota(jnp.int32, (ROLE, 1), 0)
    before = lax.broadcasted_iota(jnp.int32, (count, count), 0) < lax.broadcasted_iota(
        jnp.int32, (count, count), 1
    )
    rank = nn_dot(onehot.astype(F32).astype(BF), before.astype(F32).astype(BF))
    rank = jnp.sum(jnp.where(onehot, rank, 0.0), axis=0, keepdims=True).astype(jnp.int32)
    place = group[...] * capacity + rank
    picked = place == lax.broadcasted_iota(jnp.int32, (ROLE * capacity, 1), 0)
    picked = picked.astype(F32).astype(BF)
    chosen = nn_dot(picked, rows[...]).astype(BF)
    code = slot[...] + 1
    line = lax.broadcasted_iota(jnp.int32, (16, 1), 0)
    codes = jnp.where(line == 0, code // 32, jnp.where(line == 1, code % 32, 0))
    codes = nt_dot(codes.astype(F32).astype(BF), picked)
    page = jnp.concatenate(
        [ships[...], jnp.zeros((1, ROLE * capacity - ships.shape[1]), jnp.int32)], axis=1
    )
    pages = jnp.where(line == 2, page // 128, jnp.where(line == 3, page % 128, 0))
    codes = (codes + pages.astype(F32)).astype(BF)
    for g in range(ROLE):
        out[g, :capacity, :] = chosen[g * capacity : (g + 1) * capacity]
        out[g, capacity:, :] = codes


def pick_rows(group, slot, ships, rows):
    count, width = rows.shape
    capacity = 2 * count // ROLE
    return pl.pallas_call(
        pick_kernel,
        in_specs=[hbm()] * 4,
        out_specs=vmem(),
        scratch_shapes=[
            pltpu.VMEM((1, count), jnp.int32),
            pltpu.VMEM((1, count), jnp.int32),
            pltpu.VMEM((1, ships.shape[0]), jnp.int32),
            pltpu.VMEM(rows.shape, BF),
            pltpu.SemaphoreType.DMA((4,)),
        ],
        out_shape=jax.ShapeDtypeStruct((ROLE, capacity + 16, width), BF),
        compiler_params=params(58),
        cost_estimate=pl.CostEstimate(flops=2 * 10**8, bytes_accessed=2**20, transcendentals=0),
        name="pick_rows",
    )(group.reshape(1, count), slot.reshape(1, count), ships.reshape(1, -1), rows)


def land_kernel(role, arrived, text, merged, squares):
    capacity = arrived.shape[1] - 16
    total = ROLE * capacity
    lane = lax.broadcasted_iota(jnp.int32, (1, total), 1)
    slots = jnp.zeros((1, total), F32)
    for s in range(ROLE):
        codes = arrived[s, capacity:, :].astype(F32)
        code = jnp.broadcast_to(codes[0:1] * 32.0 + codes[1:2], (8, total))
        shift = ((s + ROLE - role[0]) % ROLE) * capacity
        slots = jnp.where(lane // capacity == s, pltpu.roll(code, shift, 1)[0:1], slots)
    slots = slots.astype(jnp.int32) - 1
    rows = arrived[:, :capacity, :].reshape(total, arrived.shape[2])
    lines = []
    for n in range(text.shape[0] // 256):
        at = slice(n * 256, (n + 1) * 256)
        row = lax.broadcasted_iota(jnp.int32, (256, 1), 0) + n * 256
        landing = jnp.where(row == slots, 1.0, 0.0)
        hit = jnp.sum(landing, axis=1, keepdims=True) > 0.0
        block = jnp.where(hit, nn_dot(landing.astype(BF), rows), text[at, :].astype(F32))
        merged[at, :] = block.astype(BF)
        square = jnp.broadcast_to(jnp.sum(block * block, axis=1, keepdims=True), (256, 128))
        lines += [to_row(square[:128]), to_row(square[128:])]
    high, middle, rest = split3(jnp.concatenate(lines, axis=0))
    squares[...] = jnp.concatenate(
        [high.astype(F32), middle.astype(F32), rest.astype(F32), jnp.zeros((8, 128), F32)], axis=0
    ).astype(BF)


def land_rows(role, arrived, text):
    return pl.pallas_call(
        land_kernel,
        in_specs=[smem()] + [vmem()] * 2,
        out_specs=[vmem()] * 2,
        out_shape=[
            jax.ShapeDtypeStruct(text.shape, BF),
            jax.ShapeDtypeStruct((32, 128), BF),
        ],
        compiler_params=params(24),
        cost_estimate=pl.CostEstimate(flops=10**9, bytes_accessed=6 * 2**20, transcendentals=0),
        name="land_rows",
    )(role, arrived, text)


def step_kernel(order, low, xs, gain, wq, wa, wb, q_out, a_out, b_out, scale, acc):
    i = pl.program_id(0)

    @pl.when(i == 0)
    def _():
        total = jnp.zeros((xs.shape[1], 512), F32)
        for k in range(TP):
            wide = xs[k].astype(F32)
            total = total + wide * wide
        total = jnp.sum(total, axis=1, keepdims=True)
        scale[...] = jnp.broadcast_to(
            lax.rsqrt(total / (TP * xs.shape[2]) + EPS), scale.shape
        )
        acc[...] = jnp.zeros_like(acc)

    factor = jnp.broadcast_to(scale[:, :1], (xs.shape[1], 512))
    total_q = acc[:, :512]
    total_a = acc[:, 512:640]
    total_b = acc[:, 640:768]
    for j in range(4):
        place = low[0] ^ j
        block = j // 2 + 2 * i + 8 * (j % 2)
        rows = pl.ds(pl.multiple_of(place * 512, 512), 512)
        normed = (xs[block].astype(F32) * factor * gain[0, place].astype(F32)).astype(BF)
        total_q = total_q + nn_dot(normed, wq[rows, :])
        total_a = total_a + nn_dot(normed, wa[rows, :])
        total_b = total_b + nn_dot(normed, wb[rows, :])
    acc[:, :512] = total_q
    acc[:, 512:640] = total_a
    acc[:, 640:768] = total_b

    @pl.when(i == 3)
    def _():
        q_out[...] = acc[:, :512].astype(BF)
        a_out[...] = acc[:, 512:640].astype(BF)
        b_out[...] = acc[:, 640:768].astype(BF)


def step_project(order, low, xs, gain, wq, wa, wb):
    rows = xs.shape[1]
    return pl.pallas_call(
        step_kernel,
        grid_spec=pltpu.PrefetchScalarGridSpec(
            num_scalar_prefetch=2,
            grid=(4,),
            in_specs=[
                pl.BlockSpec(xs.shape, lambda i, o, l: (0, 0, 0)),
                pl.BlockSpec((1, 4, 1, 512), lambda i, o, l: (o[i], 0, 0, 0)),
                pl.BlockSpec((2048, 512), lambda i, o, l: (o[i], 0)),
                pl.BlockSpec((2048, 128), lambda i, o, l: (o[i], 0)),
                pl.BlockSpec((2048, 128), lambda i, o, l: (o[i], 0)),
            ],
            out_specs=[
                pl.BlockSpec((rows, 512), lambda i, o, l: (0, 0)),
                pl.BlockSpec((rows, 128), lambda i, o, l: (0, 0)),
                pl.BlockSpec((rows, 128), lambda i, o, l: (0, 0)),
            ],
            scratch_shapes=[pltpu.VMEM((rows, 128), F32), pltpu.VMEM((rows, 768), F32)],
        ),
        out_shape=[
            jax.ShapeDtypeStruct((rows, 512), BF),
            jax.ShapeDtypeStruct((rows, 128), BF),
            jax.ShapeDtypeStruct((rows, 128), BF),
        ],
        compiler_params=params(58),
        cost_estimate=pl.CostEstimate(
            flops=2 * rows * 8192 * 768, bytes_accessed=14 * 2**20, transcendentals=0
        ),
        name="step_project",
    )(order, low, xs, gain.reshape(4, 4, 1, 512), wq, wa, wb)


def row_factors(ssq, line, scale):
    factor = lax.rsqrt(ssq[...] / (TP * 512) + EPS)
    for n in range(scale.shape[0] // 128):
        scale[n * 128 : (n + 1) * 128, :] = jnp.broadcast_to(
            to_column(factor[line + n : line + n + 1]), (128, 128)
        )


def all_blocks(text, gain, weights, scale, xbuf, wbuf, xsem, wsem, acc):
    blocks, rows = text.shape[0], text.shape[1]
    widths = [weight.shape[1] for weight in weights]

    def part(n, k):
        return wbuf.at[n // 4, pl.ds(n % 4 * 512, 512), pl.ds(sum(widths[:k]), widths[k])]

    def fetch(i):
        for n in range(4 * i, 4 * i + 4):
            pltpu.make_async_copy(text.at[n], xbuf.at[n], xsem.at[n]).start()
            for k, weight in enumerate(weights):
                rows_of = weight.at[pl.ds(n * 512, 512)]
                pltpu.make_async_copy(rows_of, part(n, k), wsem.at[n, k]).start()

    fetch(0)
    for i in range(blocks // 4):
        for n in range(4 * i, 4 * i + 4):
            pltpu.make_async_copy(xbuf.at[n], xbuf.at[n], xsem.at[n]).wait()
            for k in range(len(weights)):
                pltpu.make_async_copy(part(n, k), part(n, k), wsem.at[n, k]).wait()
        if i + 1 < blocks // 4:
            fetch(i + 1)
        gains = [gain[4 * i + k].astype(F32) for k in range(4)]
        for r in range(rows // 256):
            at = slice(r * 256, (r + 1) * 256)
            factor = scale[at, :1]
            normed = jnp.concatenate(
                [
                    (xbuf[4 * i + k, at, :].astype(F32) * factor * gains[k]).astype(BF)
                    for k in range(4)
                ],
                axis=1,
            )
            product = nn_dot(normed, wbuf[i])
            if i == 0:
                acc[at, :] = product
            else:
                acc[at, :] += product


def all_scratch(blocks, rows, width, kinds):
    return [
        pltpu.VMEM((blocks, rows, 512), BF),
        pltpu.VMEM((blocks // 4, 2048, width), BF),
        pltpu.VMEM((rows, 128), F32),
        pltpu.SemaphoreType.DMA((blocks,)),
        pltpu.SemaphoreType.DMA((blocks, kinds)),
        pltpu.VMEM((rows, width), F32),
    ]


def keys_kernel(
    core, start, group, text, ssq, gain, wq, wa, wb, q, token_row,
    queries, keys, values, out, xbuf, wbuf, scale, xsem, wsem, acc,
):
    row_factors(ssq, 0, scale)
    all_blocks(text, gain, (wq, wa, wb), scale, xbuf, wbuf, xsem, wsem, acc)
    for n in range(acc.shape[0] // 256):
        at = slice(n * 256, (n + 1) * 256)
        queries[at, :] = acc[at, :512].astype(BF)
        own, other = acc[at, 512:640], acc[at, 640:]
        keys[at, :] = jnp.where(core[0] == 0, own, other).astype(BF)
        values[at, :] = jnp.where(core[0] == 0, other, own).astype(BF)
    fresh_groups(group, start, q, keys, values, token_row, out)


def finish_keys(core, start, group, text, ssq, gain, weights, q, token_row):
    blocks, rows, _ = text.shape
    return pl.pallas_call(
        keys_kernel,
        in_specs=[smem()] * 3 + [hbm()] + [vmem()] * 2 + [hbm()] * 3 + [vmem()] * 2,
        out_specs=[vmem()] * 4,
        out_shape=[
            jax.ShapeDtypeStruct((rows, 512), BF),
            jax.ShapeDtypeStruct((rows, 128), BF),
            jax.ShapeDtypeStruct((rows, 128), BF),
            jax.ShapeDtypeStruct((ROLE, 256 + STAT_ROWS, 128), BF),
        ],
        scratch_shapes=all_scratch(blocks, rows, 768, 3),
        compiler_params=params(58),
        cost_estimate=pl.CostEstimate(
            flops=6 * 10**9, bytes_accessed=20 * 2**20, transcendentals=2**20
        ),
        name="keys_and_fresh_pages",
    )(
        core, start, group, text, ssq, gain.reshape(TP, 1, 512), *weights, q, token_row
    )


def attend_kernel(blocks_ref, q, keys, values, out):
    position = lax.broadcasted_iota(jnp.int32, (1, q.shape[0]), 1)
    segment = jnp.zeros((1, q.shape[0]), F32)
    end = 0
    for n in range(blocks_ref.shape[1]):
        end = end + blocks_ref[0, n] * PAGE_TOKENS
        segment = segment + jnp.where(position >= end, 1.0, 0.0)
    prefill_kernel(q, keys, values, segment, out)


def prefill_attention(request_blocks, q, keys, values):
    return pl.pallas_call(
        attend_kernel,
        in_specs=[smem()] + [vmem()] * 3,
        out_specs=vmem(),
        out_shape=jax.ShapeDtypeStruct(q.shape, BF),
        compiler_params=params(24),
        cost_estimate=pl.CostEstimate(
            flops=3 * 10**9, bytes_accessed=3 * 2**20, transcendentals=3 * 2**20
        ),
        name="prefill_attention",
    )(request_blocks, q, keys, values)


def paged_kernel(
    first_chunk, slot_page, slot_live, where, q, cache, out, kv, top, total, acc, lse, sem
):
    def fetch(i, carry):
        for j in range(8):
            pltpu.make_async_copy(
                cache.at[slot_page[i * 8 + j]],
                kv.at[i, pl.ds(j * PAGE_TOKENS, PAGE_TOKENS), :],
                sem.at[i],
            ).start()
        return carry

    lax.fori_loop(0, first_chunk[16], fetch, 0)
    lane = lax.broadcasted_iota(jnp.int32, (1, 128), 1)
    heads = range(KV_HEADS)

    def one_row(r, carry):
        top[...] = jnp.full_like(top, LOW)
        total[...] = jnp.zeros_like(total)
        acc[...] = jnp.zeros_like(acc)
        at = pl.multiple_of(r * 16, 16)
        queries = [
            jnp.concatenate(
                [q[where[2 * k], pl.ds(at, 16), :], q[where[2 * k + 1], pl.ds(at, 16), :]], axis=0
            )
            for k in heads
        ]

        def one_chunk(i, inner):
            live = jnp.zeros((1, 128), jnp.int32)
            for j in range(8):
                live = jnp.where(lane // PAGE_TOKENS == j, slot_live[i * 8 + j], live)
            valid = lane % PAGE_TOKENS < live
            pltpu.make_async_copy(kv.at[i], kv.at[i], sem.at[i]).wait()

            def part(column):
                return kv[i, :, column * 128 : (column + 1) * 128]

            scores = [jnp.where(valid, nt_dot(queries[k], part(2 * k)), LOW) for k in heads]
            old = [top[k * 32 : (k + 1) * 32, :] for k in heads]
            new = [jnp.maximum(old[k], jnp.max(scores[k], axis=1, keepdims=True)) for k in heads]
            weights = [
                jnp.where(valid, jnp.exp2((scores[k] - new[k]) * EXP2_SCALE), 0.0) for k in heads
            ]
            products = [nn_dot(weights[k].astype(BF), part(2 * k + 1)) for k in heads]
            for k in heads:
                rows = slice(k * 32, (k + 1) * 32)
                fade = jnp.exp2((old[k] - new[k]) * EXP2_SCALE)
                top[rows, :] = new[k]
                total[rows, :] = total[rows, :] * fade + jnp.sum(weights[k], axis=1, keepdims=True)
                acc[rows, :] = acc[rows, :] * fade + products[k]
            return inner

        lax.fori_loop(first_chunk[r], first_chunk[r + 1], one_chunk, 0)
        some = total[...] > 0.0
        divisor = jnp.where(some, total[...], 1.0)
        result = (acc[...] * (1.0 / divisor)).astype(BF)
        level = jnp.where(some, top[...] * SCALE + jnp.log(divisor), LOW)
        for t in range(TP):
            out[t, pl.ds(at, 16), :] = result[t * 16 : (t + 1) * 16]
            lse[t, pl.ds(at, 16), :] = level[t * 16 : (t + 1) * 16]
        return carry

    lax.fori_loop(0, 16, one_row, 0)

    def one_target(t, carry):
        out[t, 256:272, :] = stat_block(lse[t])
        return carry

    lax.fori_loop(0, TP, one_target, 0)


def paged_attention(first_chunk, slot_page, slot_live, where, q, cache):
    return pl.pallas_call(
        paged_kernel,
        in_specs=[smem()] * 4 + [vmem(), hbm()],
        out_specs=vmem(),
        out_shape=jax.ShapeDtypeStruct((TP, 256 + STAT_ROWS, 128), BF),
        scratch_shapes=[
            pltpu.VMEM((32, 128, 2048), BF),
            pltpu.VMEM((256, 128), F32),
            pltpu.VMEM((256, 128), F32),
            pltpu.VMEM((256, 128), F32),
            pltpu.VMEM((TP, 256, 128), F32),
            pltpu.SemaphoreType.DMA((32,)),
        ],
        compiler_params=params(58),
        cost_estimate=pl.CostEstimate(
            flops=2 * 10**9, bytes_accessed=12 * 2**20, transcendentals=2**20
        ),
        name="paged_attention",
    )(first_chunk, slot_page, slot_live, where, q, cache)


def fresh_groups(group, start, q, keys, values, token_row, out):
    span = token_row.shape[1]
    for i in range(ROLE):
        rows = pl.ds(pl.multiple_of(start[i] * PAGE_TOKENS, PAGE_TOKENS), span)
        row = lax.broadcasted_iota(jnp.int32, (256, 1), 0) // 16
        valid = token_row[i : i + 1, :] == row
        scores = jnp.where(valid, nt_dot(q[i, :256, :], keys[rows, :]), LOW)
        top = jnp.maximum(jnp.max(scores, axis=1, keepdims=True), 0.5 * LOW)
        weights = jnp.exp2((scores - top) * EXP2_SCALE)
        total = jnp.sum(weights, axis=1, keepdims=True)
        acc = nn_dot(weights.astype(BF), values[rows, :])
        some = total > 0.0
        divisor = jnp.where(some, total, 1.0)
        target = group[i]
        out[target, :256, :] = (acc * (1.0 / divisor)).astype(BF)
        out[target, 256:272, :] = stat_block(
            jnp.where(some, top * SCALE + jnp.log(divisor), LOW)
        )


def prefill_kernel(q, keys, values, seg_row, out):
    rows = q.shape[0]
    for tile in range(rows // 256):
        high = (tile + 1) * 256
        low = max(0, (tile * 256 - 511) // 256 * 256)
        span = high - low
        seg_keys = seg_row[:, low:high]
        seg_queries = to_column(seg_row[:, tile * 256 : high])
        row = lax.broadcasted_iota(jnp.int32, (256, span), 0) + tile * 256
        column = lax.broadcasted_iota(jnp.int32, (256, span), 1) + low
        valid = (seg_keys == seg_queries) & (column <= row)
        for h in range(4):
            lanes = slice(h * 128, (h + 1) * 128)
            scores = nt_dot(q[tile * 256 : high, lanes], keys[low:high, :])
            scores = jnp.where(valid, scores, LOW)
            top = jnp.max(scores, axis=1, keepdims=True)
            weights = jnp.exp2((scores - top) * EXP2_SCALE)
            total = jnp.sum(weights, axis=1, keepdims=True)
            weights = (weights * (1.0 / total)).astype(BF)
            out[tile * 256 : high, lanes] = nn_dot(weights, values[low:high, :]).astype(BF)


def stat_columns(parts):
    rows = [stat_rows(parts[n, 256:272, :]) for n in range(parts.shape[0])]
    rows.append(jnp.zeros((128 - 2 * len(rows), 128), F32))
    columns = jnp.concatenate(rows, axis=0).T
    return [
        jnp.concatenate([columns[:, 2 * n : 2 * n + 1], columns[:, 2 * n + 1 : 2 * n + 2]], axis=0)
        for n in range(parts.shape[0])
    ]


def held_kernel(held, q, new_keys, new_values, out, top_out, total_out):
    row = lax.broadcasted_iota(jnp.int32, (256, 64), 0)
    key = lax.broadcasted_iota(jnp.int32, (256, 64), 1)
    valid = (row // 16 == key % 16) & (key // 16 <= row % 16 // 4)
    scores = jnp.where(valid, nt_dot(q[...], new_keys[...]) * SCALE, LOW)
    top = jnp.max(scores, axis=1, keepdims=True)
    levels = stat_columns(held)
    for level in levels:
        top = jnp.maximum(top, level)
    weights = jnp.where(valid, jnp.exp(scores - top), 0.0)
    total = jnp.sum(weights, axis=1, keepdims=True)
    acc = nn_dot(weights.astype(BF), new_values[...])
    for n, level in enumerate(levels):
        factor = jnp.exp(level - top)
        total = total + factor
        acc = acc + held[n, :256, :].astype(F32) * factor
    out[...] = acc
    top_out[...] = jnp.broadcast_to(top, top_out.shape)
    total_out[...] = jnp.broadcast_to(total, total_out.shape)


def merge_held(held, q, new_keys, new_values):
    state = jax.ShapeDtypeStruct((256, 128), F32)
    return pl.pallas_call(
        held_kernel,
        in_specs=[vmem()] * 4,
        out_specs=[vmem()] * 3,
        out_shape=[state] * 3,
        compiler_params=params(16),
        cost_estimate=pl.CostEstimate(
            flops=10**7, bytes_accessed=2 * 2**20, transcendentals=2**16
        ),
        name="merge_held_pages",
    )(held, q, new_keys, new_values)


def merge_kernel(fresh, held_acc, held_top, held_total, out):
    top = held_top[:, :1]
    levels = stat_columns(fresh)
    for level in levels:
        top = jnp.maximum(top, level)
    factor = jnp.exp(held_top[:, :1] - top)
    total = held_total[:, :1] * factor
    acc = held_acc[...] * factor
    for n, level in enumerate(levels):
        factor = jnp.exp(level - top)
        total = total + factor
        acc = acc + fresh[n, :256, :].astype(F32) * factor
    out[...] = (acc * (1.0 / total)).astype(BF)


def merge(fresh, state):
    return pl.pallas_call(
        merge_kernel,
        in_specs=[vmem()] * 4,
        out_specs=vmem(),
        out_shape=jax.ShapeDtypeStruct((256, 128), BF),
        compiler_params=params(16),
        cost_estimate=pl.CostEstimate(
            flops=10**7, bytes_accessed=2 * 2**20, transcendentals=2**16
        ),
        name="decode_merge",
    )(fresh, *state)


def find_kernel(table, length, pages, row_out, live_out):
    code = jnp.full(pages.shape, -1.0, F32)
    entry = lax.broadcasted_iota(jnp.int32, (128, 1), 0).astype(F32)
    for r in range(table.shape[0]):
        for n in range(table.shape[1] // 128):
            column = to_column(table[r : r + 1, n * 128 : (n + 1) * 128].astype(F32))
            found = jnp.where(column == pages[...], entry + (r * 256 + n * 128), -1.0)
            code = jnp.maximum(code, jnp.max(found, axis=0, keepdims=True))
    code = code.astype(jnp.int32)
    row = jnp.where(code >= 0, code // 256, -1)
    tokens = jnp.zeros(row.shape, jnp.int32)
    for r in range(table.shape[0]):
        tokens = jnp.where(row == r, length[r], tokens)
    row_out[...] = row
    live_out[...] = jnp.where(row >= 0, jnp.clip(tokens - code % 256 * PAGE_TOKENS, 0, PAGE_TOKENS), 0)


def find_pages(block_table, cache_len, pages):
    count = pages.shape[0]
    line = jax.ShapeDtypeStruct((1, count), jnp.int32)
    row, live = pl.pallas_call(
        find_kernel,
        in_specs=[vmem(), smem(), vmem()],
        out_specs=[vmem()] * 2,
        out_shape=[line] * 2,
        compiler_params=params(16),
        cost_estimate=pl.CostEstimate(flops=10**7, bytes_accessed=2**16, transcendentals=0),
        name="find_pages",
    )(block_table, cache_len, pages.astype(F32).reshape(1, count))
    return row[0], live[0]


def page_tables(row, live, replaced, rows):
    page_ids = jnp.arange(row.shape[0], dtype=jnp.int32)
    row = jnp.where(replaced | (row < 0), rows, row)
    onehot = row[:, None] == jnp.arange(rows, dtype=jnp.int32)[None, :]
    count = jnp.sum(onehot.astype(jnp.int32), axis=0)
    chunks = (count + 7) // 8
    ids17 = jnp.arange(rows + 1, dtype=jnp.int32)
    ids16 = jnp.arange(rows, dtype=jnp.int32)
    first_chunk = jnp.sum(
        jnp.where(ids16[None, :] < ids17[:, None], chunks[None, :], 0), axis=1
    )
    rank = jnp.sum(
        ((row[None, :] == row[:, None]) & (page_ids[None, :] < page_ids[:, None])).astype(jnp.int32),
        axis=1,
    )
    base = jnp.sum(jnp.where(onehot, first_chunk[None, :rows], 0), axis=1)
    slot = jnp.where(row < rows, base * 8 + rank, -1)
    hit = slot[None, :] == jnp.arange(256, dtype=jnp.int32)[:, None]
    slot_page = jnp.sum(jnp.where(hit, page_ids[None, :], 0), axis=1)
    slot_live = jnp.sum(jnp.where(hit, live[None, :], 0), axis=1)
    return first_chunk, slot_page, slot_live


def token_rows(row, live, ship_page, group):
    pages = ship_page.shape[0]
    window = pages // 2
    page_ids = jnp.arange(pages, dtype=jnp.int32)
    ours = (ship_page // 2048)[None, :] == group[:, None]
    start = jnp.min(jnp.where(ours, page_ids[None, :], window), axis=1)
    start = jnp.minimum(start, window)
    packed = jnp.where(ours & (live > 0), row * 32 + live, 0)
    place = start[:, None] + jnp.arange(window, dtype=jnp.int32)[None, :]
    hit = place[:, :, None] == page_ids[None, None, :]
    here = jnp.sum(jnp.where(hit, packed[:, None, :], 0), axis=2)
    token = jnp.arange(PAGE_TOKENS, dtype=jnp.int32)[None, None, :]
    token_row = jnp.where(token < (here % 32)[:, :, None], (here // 32)[:, :, None], -1)
    return start, token_row.reshape(ROLE, window * PAGE_TOKENS)


def phase(*arrays):
    return lax.optimization_barrier(arrays)


def per_device(
    text_embed,
    vision_rows,
    vision_group,
    vision_slot,
    request_blocks,
    ship_page,
    paged_cache,
    block_table,
    cache_len,
    step_embed,
    norm_gain,
    query_weight,
    keyvalue_weight,
):
    column = lax.axis_index("tp")
    role = lax.axis_index("role")
    core = column % 2
    group_rows, width = text_embed.shape
    steps, rows, _ = step_embed.shape

    role_id = role.reshape(1)

    def plus(a):
        return swap(a, "tp", CORE)

    other_weight = plus(keyvalue_weight)
    weights = (query_weight, keyvalue_weight, other_weight)
    (message,) = phase(pick_rows(vision_group, vision_slot, ship_page, vision_rows))
    arrived = lax.all_to_all(message, "role", split_axis=0, concat_axis=0, tiled=True)
    steps_y = doubling(step_embed.reshape(steps * rows, width), "tp", TP_MASKS[:2])
    arrived, steps_y = phase(arrived, steps_y)
    merged, squares = land_rows(role_id, arrived, text_embed)
    text_all = lax.all_gather(merged, "tp")

    first_page = (role * TP + column) * 128
    parts = arrived[:, 64 + 2 : 64 + 4, : ship_page.shape[0]].astype(jnp.int32)
    ships = parts[:, 0] * 128 + parts[:, 1]
    page_ids = first_page + jnp.arange(paged_cache.shape[0], dtype=jnp.int32)
    held_count = page_ids.shape[0]
    row_of, live_of = find_pages(
        block_table, cache_len, jnp.concatenate([page_ids, ships.reshape(-1)])
    )
    codes = jnp.concatenate(
        [
            row_of[held_count:].reshape(4, 128),
            live_of[held_count:].reshape(4, 128),
            jnp.zeros((8, 128), jnp.int32),
        ],
        axis=0,
    ).astype(BF)
    steps_all = more(more(steps_y, "tp", TP_MASKS[2]), "tp", CORE)
    step_q, step_a, step_b = step_project(
        (column // 4) ^ jnp.array([0, 1, 3, 2], jnp.int32),
        (column % 4).reshape(1),
        steps_all,
        norm_gain,
        *weights,
    )
    new_keys = jnp.where(core == 0, step_a, step_b)
    new_values = jnp.where(core == 0, step_b, step_a)
    own_queries = (
        step_q.reshape(steps, rows, 4, HEAD_SIZE).transpose(1, 0, 2, 3).reshape(rows * 16, HEAD_SIZE)
    )
    own_queries, squares, codes = phase(own_queries, squares, codes)

    query_all = doubling(jnp.concatenate([own_queries, squares], axis=0), "tp", TP_MASKS)
    replaced = jnp.any(ships.reshape(1, -1) == page_ids[:, None], axis=1)
    first_chunk, slot_page, slot_live = page_tables(
        row_of[:held_count], live_of[:held_count], replaced, rows
    )
    role_message = jnp.concatenate([own_queries, codes], axis=0)
    queries_role = doubling(role_message, "role", ROLE_MASKS[:1])
    difference = column ^ jnp.arange(TP, dtype=jnp.int32)
    far_bit = difference // 8
    near_bit = (difference // 4) % 2 ^ far_bit
    where = difference // 2 % 2 + 2 * near_bit + 4 * far_bit + 8 * (difference % 2)
    held = paged_attention(first_chunk, slot_page, slot_live, where, query_all, paged_cache)
    held, queries_role = phase(held, queries_role)

    held_parts = lax.all_to_all(held, "tp", split_axis=0, concat_axis=0, tiled=True)
    sums = jnp.sum(query_all[:, 256:280, :].astype(F32), axis=0)
    ssq = sums[0:8] + sums[8:16] + sums[16:24]
    queries_role = more(more(queries_role, "role", ROLE_MASKS[1]), "role", ROLE_MASKS[2])
    role_order = role ^ jnp.array(ROLE_OFFSETS, jnp.int32)
    info = queries_role[:, 256:264, :].reshape(ROLE, 2, ROLE * ship_page.shape[0])
    info = lax.dynamic_slice_in_dim(info, role * ship_page.shape[0], ship_page.shape[0], 2)
    info = info.astype(jnp.int32)
    start, token_row = token_rows(info[:, 0], info[:, 1], ship_page, role_order)
    text_all, start, token_row, queries_role, ssq = phase(
        text_all, start, token_row, queries_role, ssq
    )

    prefill_queries, keys, values, fresh = finish_keys(
        core.reshape(1),
        start,
        role_order,
        text_all,
        ssq,
        norm_gain,
        weights,
        queries_role,
        token_row,
    )
    fresh, held_parts = phase(fresh, held_parts)
    fresh_parts = lax.all_to_all(fresh, "role", split_axis=0, concat_axis=0, tiled=True)

    prefill_out = prefill_attention(request_blocks, prefill_queries, keys, values)
    state = merge_held(held_parts, own_queries, new_keys, new_values)

    decode = merge(fresh_parts, state)
    decode_out = (
        decode.reshape(rows, steps, 4, HEAD_SIZE).transpose(1, 0, 2, 3).reshape(steps, rows, 512)
    )
    return (prefill_out, decode_out)


def solution(mesh):
    in_specs = (
        P("role", "tp"),
        P("role", "tp"),
        P("role"),
        P("role"),
        P("role", None),
        P("role"),
        P(("role", "tp"), None, None),
        P("role", None),
        P("role"),
        P(None, "role", "tp"),
        P(),
        P(None, "tp"),
        P(None, "tp"),
    )
    out_specs = (P("role", "tp"), P(None, "role", "tp"))
    return jax.shard_map(
        per_device, mesh=mesh, in_specs=in_specs, out_specs=out_specs, check_vma=False
    )
```

```python
import jax
import jax.numpy as jnp
from jax import lax
from jax.experimental import pallas as pl
from jax.experimental.pallas import tpu as pltpu
from jax.sharding import PartitionSpec as P

HEAD_SIZE = 128
KV_HEADS = 8
PAGE_TOKENS = 16
EPS = 1e-06
LOW = -1e30
SCALE = HEAD_SIZE ** (-0.5)
BF = jnp.bfloat16
F32 = jnp.float32
EXP2_SCALE = SCALE * 1.4426950408889634
LN2 = 0.6931471805599453
TP = 16
ROLE = 8
STAT_ROWS = 16

CORE = 1
TP_MASKS = (2, 4, 12, CORE)
ROLE_MASKS = (4, 1, 3)


def params(mebibytes):
    return pltpu.CompilerParams(vmem_limit_bytes=mebibytes * 2**20)


def vmem():
    return pl.BlockSpec(memory_space=pltpu.VMEM)


def smem():
    return pl.BlockSpec(memory_space=pltpu.SMEM)


def hbm():
    return pl.BlockSpec(memory_space=pl.ANY)


def swap(x, axis, mask):
    size = TP if axis == "tp" else ROLE
    return lax.ppermute(x, axis, [(i, i ^ mask) for i in range(size)])


def more(held, axis, mask):
    return jnp.concatenate([held, swap(held, axis, mask)], axis=0)


def doubling(x, axis, masks):
    held = x[None]
    for mask in masks:
        held = more(held, axis, mask)
    return held


def offsets(masks):
    table = [0]
    for mask in masks:
        table = table + [v ^ mask for v in table]
    return table


ROLE_OFFSETS = offsets(ROLE_MASKS)


def nt_dot(a, b):
    return lax.dot_general(a, b, (((1,), (1,)), ((), ())), preferred_element_type=F32)


def nn_dot(a, b):
    return jnp.dot(a, b, preferred_element_type=F32)


def eye(n):
    return lax.broadcasted_iota(jnp.int32, (n, n), 0) == lax.broadcasted_iota(
        jnp.int32, (n, n), 1
    )


def to_row(column):
    n = column.shape[0]
    return jnp.sum(jnp.where(eye(n), column, 0.0), axis=0, keepdims=True)


def to_column(row):
    n = row.shape[1]
    return jnp.sum(jnp.where(eye(n), row, 0.0), axis=1, keepdims=True)


def split3(x):
    high = x.astype(BF)
    rest = x - high.astype(F32)
    middle = rest.astype(BF)
    low = (rest - middle.astype(F32)).astype(BF)
    return high, middle, low


def stat_block(level):
    parts = jnp.concatenate(
        [to_row(level[:128]), to_row(level[128:]), jnp.zeros((6, 128), F32)], axis=0
    )
    high, middle, low = split3(parts)
    return jnp.concatenate(
        [
            high[:2].astype(F32),
            middle[:2].astype(F32),
            low[:2].astype(F32),
            jnp.zeros((10, 128), F32),
        ],
        axis=0,
    ).astype(BF)


def stat_rows(block):
    wide = block.astype(F32)
    return wide[0:2] + wide[2:4] + wide[4:6]


def pick_kernel(group_in, slot_in, ships_in, rows_in, out, group, slot, ships, rows, sem):
    pairs = ((group_in, group), (slot_in, slot), (ships_in, ships), (rows_in, rows))
    copies = [pltpu.make_async_copy(a, b, sem.at[n]) for n, (a, b) in enumerate(pairs)]
    for copy in copies:
        copy.start()
    for copy in copies:
        copy.wait()
    count = group.shape[1]
    capacity = 2 * count // ROLE
    onehot = group[...] == lax.broadcasted_iota(jnp.int32, (ROLE, 1), 0)
    before = lax.broadcasted_iota(jnp.int32, (count, count), 0) < lax.broadcasted_iota(
        jnp.int32, (count, count), 1
    )
    rank = nn_dot(onehot.astype(F32).astype(BF), before.astype(F32).astype(BF))
    rank = jnp.sum(jnp.where(onehot, rank, 0.0), axis=0, keepdims=True).astype(jnp.int32)
    place = group[...] * capacity + rank
    picked = place == lax.broadcasted_iota(jnp.int32, (ROLE * capacity, 1), 0)
    picked = picked.astype(F32).astype(BF)
    chosen = nn_dot(picked, rows[...]).astype(BF)
    code = slot[...] + 1
    line = lax.broadcasted_iota(jnp.int32, (16, 1), 0)
    codes = jnp.where(line == 0, code // 32, jnp.where(line == 1, code % 32, 0))
    codes = nt_dot(codes.astype(F32).astype(BF), picked)
    page = jnp.concatenate(
        [ships[...], jnp.zeros((1, ROLE * capacity - ships.shape[1]), jnp.int32)], axis=1
    )
    pages = jnp.where(line == 2, page // 128, jnp.where(line == 3, page % 128, 0))
    codes = (codes + pages.astype(F32)).astype(BF)
    for g in range(ROLE):
        out[g, :capacity, :] = chosen[g * capacity : (g + 1) * capacity]
        out[g, capacity:, :] = codes


def pick_rows(group, slot, ships, rows):
    count, width = rows.shape
    capacity = 2 * count // ROLE
    return pl.pallas_call(
        pick_kernel,
        in_specs=[hbm()] * 4,
        out_specs=vmem(),
        scratch_shapes=[
            pltpu.VMEM((1, count), jnp.int32),
            pltpu.VMEM((1, count), jnp.int32),
            pltpu.VMEM((1, ships.shape[0]), jnp.int32),
            pltpu.VMEM(rows.shape, BF),
            pltpu.SemaphoreType.DMA((4,)),
        ],
        out_shape=jax.ShapeDtypeStruct((ROLE, capacity + 16, width), BF),
        compiler_params=params(58),
        cost_estimate=pl.CostEstimate(flops=2 * 10**8, bytes_accessed=2**20, transcendentals=0),
        name="pick_rows",
    )(group.reshape(1, count), slot.reshape(1, count), ships.reshape(1, -1), rows)


def land_kernel(role, arrived, text, merged, squares):
    capacity = arrived.shape[1] - 16
    total = ROLE * capacity
    lane = lax.broadcasted_iota(jnp.int32, (1, total), 1)
    slots = jnp.zeros((1, total), F32)
    for s in range(ROLE):
        codes = arrived[s, capacity:, :].astype(F32)
        code = jnp.broadcast_to(codes[0:1] * 32.0 + codes[1:2], (8, total))
        shift = ((s + ROLE - role[0]) % ROLE) * capacity
        slots = jnp.where(lane // capacity == s, pltpu.roll(code, shift, 1)[0:1], slots)
    slots = slots.astype(jnp.int32) - 1
    rows = arrived[:, :capacity, :].reshape(total, arrived.shape[2])
    lines = []
    for n in range(text.shape[0] // 256):
        at = slice(n * 256, (n + 1) * 256)
        row = lax.broadcasted_iota(jnp.int32, (256, 1), 0) + n * 256
        landing = jnp.where(row == slots, 1.0, 0.0)
        hit = jnp.sum(landing, axis=1, keepdims=True) > 0.0
        block = jnp.where(hit, nn_dot(landing.astype(BF), rows), text[at, :].astype(F32))
        merged[at, :] = block.astype(BF)
        square = jnp.broadcast_to(jnp.sum(block * block, axis=1, keepdims=True), (256, 128))
        lines += [to_row(square[:128]), to_row(square[128:])]
    high, middle, rest = split3(jnp.concatenate(lines, axis=0))
    squares[...] = jnp.concatenate(
        [high.astype(F32), middle.astype(F32), rest.astype(F32), jnp.zeros((8, 128), F32)], axis=0
    ).astype(BF)


def land_rows(role, arrived, text):
    return pl.pallas_call(
        land_kernel,
        in_specs=[smem()] + [vmem()] * 2,
        out_specs=[vmem()] * 2,
        out_shape=[
            jax.ShapeDtypeStruct(text.shape, BF),
            jax.ShapeDtypeStruct((32, 128), BF),
        ],
        compiler_params=params(24),
        cost_estimate=pl.CostEstimate(flops=10**9, bytes_accessed=6 * 2**20, transcendentals=0),
        name="land_rows",
    )(role, arrived, text)


def step_kernel(order, low, xs, gain, wq, wa, wb, q_out, a_out, b_out, scale, acc):
    i = pl.program_id(0)

    @pl.when(i == 0)
    def _():
        total = jnp.zeros((xs.shape[1], 512), F32)
        for k in range(TP):
            wide = xs[k].astype(F32)
            total = total + wide * wide
        total = jnp.sum(total, axis=1, keepdims=True)
        scale[...] = jnp.broadcast_to(
            lax.rsqrt(total / (TP * xs.shape[2]) + EPS), scale.shape
        )
        acc[...] = jnp.zeros_like(acc)

    factor = jnp.broadcast_to(scale[:, :1], (xs.shape[1], 512))
    total_q = acc[:, :512]
    total_a = acc[:, 512:640]
    total_b = acc[:, 640:768]
    for j in range(4):
        place = low[0] ^ j
        block = j // 2 + 2 * i + 8 * (j % 2)
        rows = pl.ds(pl.multiple_of(place * 512, 512), 512)
        normed = (xs[block].astype(F32) * factor * gain[0, place].astype(F32)).astype(BF)
        total_q = total_q + nn_dot(normed, wq[rows, :])
        total_a = total_a + nn_dot(normed, wa[rows, :])
        total_b = total_b + nn_dot(normed, wb[rows, :])
    acc[:, :512] = total_q
    acc[:, 512:640] = total_a
    acc[:, 640:768] = total_b

    @pl.when(i == 3)
    def _():
        q_out[...] = acc[:, :512].astype(BF)
        a_out[...] = acc[:, 512:640].astype(BF)
        b_out[...] = acc[:, 640:768].astype(BF)


def step_project(order, low, xs, gain, wq, wa, wb):
    rows = xs.shape[1]
    return pl.pallas_call(
        step_kernel,
        grid_spec=pltpu.PrefetchScalarGridSpec(
            num_scalar_prefetch=2,
            grid=(4,),
            in_specs=[
                pl.BlockSpec(xs.shape, lambda i, o, l: (0, 0, 0)),
                pl.BlockSpec((1, 4, 1, 512), lambda i, o, l: (o[i], 0, 0, 0)),
                pl.BlockSpec((2048, 512), lambda i, o, l: (o[i], 0)),
                pl.BlockSpec((2048, 128), lambda i, o, l: (o[i], 0)),
                pl.BlockSpec((2048, 128), lambda i, o, l: (o[i], 0)),
            ],
            out_specs=[
                pl.BlockSpec((rows, 512), lambda i, o, l: (0, 0)),
                pl.BlockSpec((rows, 128), lambda i, o, l: (0, 0)),
                pl.BlockSpec((rows, 128), lambda i, o, l: (0, 0)),
            ],
            scratch_shapes=[pltpu.VMEM((rows, 128), F32), pltpu.VMEM((rows, 768), F32)],
        ),
        out_shape=[
            jax.ShapeDtypeStruct((rows, 512), BF),
            jax.ShapeDtypeStruct((rows, 128), BF),
            jax.ShapeDtypeStruct((rows, 128), BF),
        ],
        compiler_params=params(58),
        cost_estimate=pl.CostEstimate(
            flops=2 * rows * 8192 * 768, bytes_accessed=14 * 2**20, transcendentals=0
        ),
        name="step_project",
    )(order, low, xs, gain.reshape(4, 4, 1, 512), wq, wa, wb)


def row_factors(ssq, line, scale):
    factor = lax.rsqrt(ssq[...] / (TP * 512) + EPS)
    for n in range(scale.shape[0] // 128):
        scale[n * 128 : (n + 1) * 128, :] = jnp.broadcast_to(
            to_column(factor[line + n : line + n + 1]), (128, 128)
        )


def all_blocks(text, ssq, gain, weights, scale, xbuf, wbuf, xsem, wsem, acc):
    blocks, rows = text.shape[0], text.shape[1]
    widths = [weight.shape[1] for weight in weights]

    def part(n, k):
        return wbuf.at[n // 4, pl.ds(n % 4 * 512, 512), pl.ds(sum(widths[:k]), widths[k])]

    def fetch(i):
        for n in range(4 * i, 4 * i + 4):
            pltpu.make_async_copy(text.at[n], xbuf.at[n], xsem.at[n]).start()
            for k, weight in enumerate(weights):
                rows_of = weight.at[pl.ds(n * 512, 512)]
                pltpu.make_async_copy(rows_of, part(n, k), wsem.at[n, k]).start()

    fetch(0)
    fetch(1)
    row_factors(ssq, 0, scale)
    for i in range(blocks // 4):
        for n in range(4 * i, 4 * i + 4):
            pltpu.make_async_copy(xbuf.at[n], xbuf.at[n], xsem.at[n]).wait()
            for k in range(len(weights)):
                pltpu.make_async_copy(part(n, k), part(n, k), wsem.at[n, k]).wait()
        if i + 2 < blocks // 4:
            fetch(i + 2)
        gains = [gain[4 * i + k].astype(F32) for k in range(4)]
        for r in range(rows // 256):
            at = slice(r * 256, (r + 1) * 256)
            factor = scale[at, :1]
            normed = jnp.concatenate(
                [
                    (xbuf[4 * i + k, at, :].astype(F32) * factor * gains[k]).astype(BF)
                    for k in range(4)
                ],
                axis=1,
            )
            product = nn_dot(normed, wbuf[i])
            if i == 0:
                acc[at, :] = product
            else:
                acc[at, :] += product


def all_scratch(blocks, rows, width, kinds):
    return [
        pltpu.VMEM((blocks, rows, 512), BF),
        pltpu.VMEM((blocks // 4, 2048, width), BF),
        pltpu.VMEM((rows, 128), F32),
        pltpu.SemaphoreType.DMA((blocks,)),
        pltpu.SemaphoreType.DMA((blocks, kinds)),
        pltpu.VMEM((rows, width), F32),
    ]


def keys_kernel(
    core, start, group, text, ssq, gain, wq, wa, wb, q, token_row,
    queries, keys, values, out, xbuf, wbuf, scale, xsem, wsem, acc,
):
    all_blocks(text, ssq, gain, (wq, wa, wb), scale, xbuf, wbuf, xsem, wsem, acc)
    for n in range(acc.shape[0] // 256):
        at = slice(n * 256, (n + 1) * 256)
        queries[at, :] = acc[at, :512].astype(BF)
        own, other = acc[at, 512:640], acc[at, 640:]
        keys[at, :] = jnp.where(core[0] == 0, own, other).astype(BF)
        values[at, :] = jnp.where(core[0] == 0, other, own).astype(BF)
    fresh_groups(group, start, q, keys, values, token_row, out)


def finish_keys(core, start, group, text, ssq, gain, weights, q, token_row):
    blocks, rows, _ = text.shape
    return pl.pallas_call(
        keys_kernel,
        in_specs=[smem()] * 3 + [hbm()] + [vmem()] * 2 + [hbm()] * 3 + [vmem()] * 2,
        out_specs=[vmem()] * 4,
        out_shape=[
            jax.ShapeDtypeStruct((rows, 512), BF),
            jax.ShapeDtypeStruct((rows, 128), BF),
            jax.ShapeDtypeStruct((rows, 128), BF),
            jax.ShapeDtypeStruct((ROLE, 256 + STAT_ROWS, 128), BF),
        ],
        scratch_shapes=all_scratch(blocks, rows, 768, 3),
        compiler_params=params(58),
        cost_estimate=pl.CostEstimate(
            flops=6 * 10**9, bytes_accessed=20 * 2**20, transcendentals=2**20
        ),
        name="keys_and_fresh_pages",
    )(
        core, start, group, text, ssq, gain.reshape(TP, 1, 512), *weights, q, token_row
    )


def attend_kernel(blocks_ref, q, keys, values, out):
    position = lax.broadcasted_iota(jnp.int32, (1, q.shape[0]), 1)
    segment = jnp.zeros((1, q.shape[0]), F32)
    end = 0
    for n in range(blocks_ref.shape[1]):
        end = end + blocks_ref[0, n] * PAGE_TOKENS
        segment = segment + jnp.where(position >= end, 1.0, 0.0)
    prefill_kernel(q, keys, values, segment, out)


def prefill_attention(request_blocks, q, keys, values):
    return pl.pallas_call(
        attend_kernel,
        in_specs=[smem()] + [vmem()] * 3,
        out_specs=vmem(),
        out_shape=jax.ShapeDtypeStruct(q.shape, BF),
        compiler_params=params(24),
        cost_estimate=pl.CostEstimate(
            flops=3 * 10**9, bytes_accessed=3 * 2**20, transcendentals=3 * 2**20
        ),
        name="prefill_attention",
    )(request_blocks, q, keys, values)


def paged_kernel(
    first_chunk, slot_page, slot_live, where, q, cache, out, kv, top, total, acc, lse, sem
):
    def fetch(i, carry):
        for j in range(8):
            pltpu.make_async_copy(
                cache.at[slot_page[i * 8 + j]],
                kv.at[i, pl.ds(j * PAGE_TOKENS, PAGE_TOKENS), :],
                sem.at[i],
            ).start()
        return carry

    lax.fori_loop(0, first_chunk[16], fetch, 0)
    lane = lax.broadcasted_iota(jnp.int32, (1, 128), 1)
    heads = range(KV_HEADS)

    def one_row(r, carry):
        top[...] = jnp.full_like(top, LOW)
        total[...] = jnp.zeros_like(total)
        acc[...] = jnp.zeros_like(acc)
        at = pl.multiple_of(r * 16, 16)
        queries = [
            jnp.concatenate(
                [q[where[2 * k], pl.ds(at, 16), :], q[where[2 * k + 1], pl.ds(at, 16), :]], axis=0
            )
            for k in heads
        ]

        def one_chunk(i, inner):
            live = jnp.zeros((1, 128), jnp.int32)
            for j in range(8):
                live = jnp.where(lane // PAGE_TOKENS == j, slot_live[i * 8 + j], live)
            valid = lane % PAGE_TOKENS < live
            pltpu.make_async_copy(kv.at[i], kv.at[i], sem.at[i]).wait()

            def part(column):
                return kv[i, :, column * 128 : (column + 1) * 128]

            scores = [jnp.where(valid, nt_dot(queries[k], part(2 * k)), LOW) for k in heads]
            old = [top[k * 32 : (k + 1) * 32, :] for k in heads]
            new = [jnp.maximum(old[k], jnp.max(scores[k], axis=1, keepdims=True)) for k in heads]
            weights = [
                jnp.where(valid, jnp.exp2((scores[k] - new[k]) * EXP2_SCALE), 0.0) for k in heads
            ]
            products = [nn_dot(weights[k].astype(BF), part(2 * k + 1)) for k in heads]
            for k in heads:
                rows = slice(k * 32, (k + 1) * 32)
                fade = jnp.exp2((old[k] - new[k]) * EXP2_SCALE)
                top[rows, :] = new[k]
                total[rows, :] = total[rows, :] * fade + jnp.sum(weights[k], axis=1, keepdims=True)
                acc[rows, :] = acc[rows, :] * fade + products[k]
            return inner

        lax.fori_loop(first_chunk[r], first_chunk[r + 1], one_chunk, 0)
        some = total[...] > 0.0
        divisor = jnp.where(some, total[...], 1.0)
        result = (acc[...] * (1.0 / divisor)).astype(BF)
        level = jnp.where(some, top[...] * SCALE + jnp.log(divisor), LOW)
        for t in range(TP):
            out[t, pl.ds(at, 16), :] = result[t * 16 : (t + 1) * 16]
            lse[t, pl.ds(at, 16), :] = level[t * 16 : (t + 1) * 16]
        return carry

    lax.fori_loop(0, 16, one_row, 0)

    def one_target(t, carry):
        out[t, 256:272, :] = stat_block(lse[t])
        return carry

    lax.fori_loop(0, TP, one_target, 0)


def paged_attention(first_chunk, slot_page, slot_live, where, q, cache):
    return pl.pallas_call(
        paged_kernel,
        in_specs=[smem()] * 4 + [vmem(), hbm()],
        out_specs=vmem(),
        out_shape=jax.ShapeDtypeStruct((TP, 256 + STAT_ROWS, 128), BF),
        scratch_shapes=[
            pltpu.VMEM((32, 128, 2048), BF),
            pltpu.VMEM((256, 128), F32),
            pltpu.VMEM((256, 128), F32),
            pltpu.VMEM((256, 128), F32),
            pltpu.VMEM((TP, 256, 128), F32),
            pltpu.SemaphoreType.DMA((32,)),
        ],
        compiler_params=params(58),
        cost_estimate=pl.CostEstimate(
            flops=2 * 10**9, bytes_accessed=12 * 2**20, transcendentals=2**20
        ),
        name="paged_attention",
    )(first_chunk, slot_page, slot_live, where, q, cache)


def fresh_groups(group, start, q, keys, values, token_row, out):
    span = token_row.shape[1]
    for i in range(ROLE):
        rows = pl.ds(pl.multiple_of(start[i] * PAGE_TOKENS, PAGE_TOKENS), span)
        row = lax.broadcasted_iota(jnp.int32, (256, 1), 0) // 16
        valid = token_row[i : i + 1, :] == row
        scores = jnp.where(valid, nt_dot(q[i, :256, :], keys[rows, :]), LOW)
        top = jnp.maximum(jnp.max(scores, axis=1, keepdims=True), 0.5 * LOW)
        weights = jnp.exp2((scores - top) * EXP2_SCALE)
        total = jnp.sum(weights, axis=1, keepdims=True)
        acc = nn_dot(weights.astype(BF), values[rows, :])
        some = total > 0.0
        divisor = jnp.where(some, total, 1.0)
        target = group[i]
        out[target, :256, :] = (acc * (1.0 / divisor)).astype(BF)
        out[target, 256:272, :] = stat_block(
            jnp.where(some, top * SCALE + jnp.log(divisor), LOW)
        )


def prefill_kernel(q, keys, values, seg_row, out):
    rows = q.shape[0]
    for tile in range(rows // 256):
        high = (tile + 1) * 256
        low = max(0, (tile * 256 - 511) // 256 * 256)
        span = high - low
        seg_keys = seg_row[:, low:high]
        seg_queries = to_column(seg_row[:, tile * 256 : high])
        row = lax.broadcasted_iota(jnp.int32, (256, span), 0) + tile * 256
        column = lax.broadcasted_iota(jnp.int32, (256, span), 1) + low
        valid = (seg_keys == seg_queries) & (column <= row)
        for h in range(4):
            lanes = slice(h * 128, (h + 1) * 128)
            scores = nt_dot(q[tile * 256 : high, lanes], keys[low:high, :])
            scores = jnp.where(valid, scores, LOW)
            top = jnp.max(scores, axis=1, keepdims=True)
            weights = jnp.exp2((scores - top) * EXP2_SCALE)
            total = jnp.sum(weights, axis=1, keepdims=True)
            weights = (weights * (1.0 / total)).astype(BF)
            out[tile * 256 : high, lanes] = nn_dot(weights, values[low:high, :]).astype(BF)


def stat_columns(parts):
    rows = [stat_rows(parts[n, 256:272, :]) for n in range(parts.shape[0])]
    rows.append(jnp.zeros((128 - 2 * len(rows), 128), F32))
    columns = jnp.concatenate(rows, axis=0).T
    return [
        jnp.concatenate([columns[:, 2 * n : 2 * n + 1], columns[:, 2 * n + 1 : 2 * n + 2]], axis=0)
        for n in range(parts.shape[0])
    ]


def held_kernel(held, q, new_keys, new_values, out, top_out, total_out):
    row = lax.broadcasted_iota(jnp.int32, (256, 64), 0)
    key = lax.broadcasted_iota(jnp.int32, (256, 64), 1)
    valid = (row // 16 == key % 16) & (key // 16 <= row % 16 // 4)
    scores = jnp.where(valid, nt_dot(q[...], new_keys[...]) * SCALE, LOW)
    top = jnp.max(scores, axis=1, keepdims=True)
    levels = stat_columns(held)
    for level in levels:
        top = jnp.maximum(top, level)
    weights = jnp.where(valid, jnp.exp(scores - top), 0.0)
    total = jnp.sum(weights, axis=1, keepdims=True)
    acc = nn_dot(weights.astype(BF), new_values[...])
    for n, level in enumerate(levels):
        factor = jnp.exp(level - top)
        total = total + factor
        acc = acc + held[n, :256, :].astype(F32) * factor
    out[...] = acc
    top_out[...] = jnp.broadcast_to(top, top_out.shape)
    total_out[...] = jnp.broadcast_to(total, total_out.shape)


def merge_held(held, q, new_keys, new_values):
    state = jax.ShapeDtypeStruct((256, 128), F32)
    return pl.pallas_call(
        held_kernel,
        in_specs=[vmem()] * 4,
        out_specs=[vmem()] * 3,
        out_shape=[state] * 3,
        compiler_params=params(16),
        cost_estimate=pl.CostEstimate(
            flops=10**7, bytes_accessed=2 * 2**20, transcendentals=2**16
        ),
        name="merge_held_pages",
    )(held, q, new_keys, new_values)


def merge_kernel(fresh, held_acc, held_top, held_total, out):
    top = held_top[:, :1]
    levels = stat_columns(fresh)
    for level in levels:
        top = jnp.maximum(top, level)
    factor = jnp.exp(held_top[:, :1] - top)
    total = held_total[:, :1] * factor
    acc = held_acc[...] * factor
    for n, level in enumerate(levels):
        factor = jnp.exp(level - top)
        total = total + factor
        acc = acc + fresh[n, :256, :].astype(F32) * factor
    out[...] = (acc * (1.0 / total)).astype(BF)


def merge(fresh, state):
    return pl.pallas_call(
        merge_kernel,
        in_specs=[vmem()] * 4,
        out_specs=vmem(),
        out_shape=jax.ShapeDtypeStruct((256, 128), BF),
        compiler_params=params(16),
        cost_estimate=pl.CostEstimate(
            flops=10**7, bytes_accessed=2 * 2**20, transcendentals=2**16
        ),
        name="decode_merge",
    )(fresh, *state)


def find_kernel(table, length, pages, row_out, live_out):
    code = jnp.full(pages.shape, -1.0, F32)
    entry = lax.broadcasted_iota(jnp.int32, (128, 1), 0).astype(F32)
    for r in range(table.shape[0]):
        for n in range(table.shape[1] // 128):
            column = to_column(table[r : r + 1, n * 128 : (n + 1) * 128].astype(F32))
            found = jnp.where(column == pages[...], entry + (r * 256 + n * 128), -1.0)
            code = jnp.maximum(code, jnp.max(found, axis=0, keepdims=True))
    code = code.astype(jnp.int32)
    row = jnp.where(code >= 0, code // 256, -1)
    tokens = jnp.zeros(row.shape, jnp.int32)
    for r in range(table.shape[0]):
        tokens = jnp.where(row == r, length[r], tokens)
    row_out[...] = row
    live_out[...] = jnp.where(row >= 0, jnp.clip(tokens - code % 256 * PAGE_TOKENS, 0, PAGE_TOKENS), 0)


def find_pages(block_table, cache_len, pages):
    count = pages.shape[0]
    line = jax.ShapeDtypeStruct((1, count), jnp.int32)
    row, live = pl.pallas_call(
        find_kernel,
        in_specs=[vmem(), smem(), vmem()],
        out_specs=[vmem()] * 2,
        out_shape=[line] * 2,
        compiler_params=params(16),
        cost_estimate=pl.CostEstimate(flops=10**7, bytes_accessed=2**16, transcendentals=0),
        name="find_pages",
    )(block_table, cache_len, pages.astype(F32).reshape(1, count))
    return row[0], live[0]


def page_tables(row, live, replaced, rows):
    page_ids = jnp.arange(row.shape[0], dtype=jnp.int32)
    row = jnp.where(replaced | (row < 0), rows, row)
    onehot = row[:, None] == jnp.arange(rows, dtype=jnp.int32)[None, :]
    count = jnp.sum(onehot.astype(jnp.int32), axis=0)
    chunks = (count + 7) // 8
    ids17 = jnp.arange(rows + 1, dtype=jnp.int32)
    ids16 = jnp.arange(rows, dtype=jnp.int32)
    first_chunk = jnp.sum(
        jnp.where(ids16[None, :] < ids17[:, None], chunks[None, :], 0), axis=1
    )
    rank = jnp.sum(
        ((row[None, :] == row[:, None]) & (page_ids[None, :] < page_ids[:, None])).astype(jnp.int32),
        axis=1,
    )
    base = jnp.sum(jnp.where(onehot, first_chunk[None, :rows], 0), axis=1)
    slot = jnp.where(row < rows, base * 8 + rank, -1)
    hit = slot[None, :] == jnp.arange(256, dtype=jnp.int32)[:, None]
    slot_page = jnp.sum(jnp.where(hit, page_ids[None, :], 0), axis=1)
    slot_live = jnp.sum(jnp.where(hit, live[None, :], 0), axis=1)
    return first_chunk, slot_page, slot_live


def token_rows(row, live, ship_page, group):
    pages = ship_page.shape[0]
    window = pages // 2
    page_ids = jnp.arange(pages, dtype=jnp.int32)
    ours = (ship_page // 2048)[None, :] == group[:, None]
    start = jnp.min(jnp.where(ours, page_ids[None, :], window), axis=1)
    start = jnp.minimum(start, window)
    packed = jnp.where(ours & (live > 0), row * 32 + live, 0)
    place = start[:, None] + jnp.arange(window, dtype=jnp.int32)[None, :]
    hit = place[:, :, None] == page_ids[None, None, :]
    here = jnp.sum(jnp.where(hit, packed[:, None, :], 0), axis=2)
    token = jnp.arange(PAGE_TOKENS, dtype=jnp.int32)[None, None, :]
    token_row = jnp.where(token < (here % 32)[:, :, None], (here // 32)[:, :, None], -1)
    return start, token_row.reshape(ROLE, window * PAGE_TOKENS)


def phase(*arrays):
    return lax.optimization_barrier(arrays)


def per_device(
    text_embed,
    vision_rows,
    vision_group,
    vision_slot,
    request_blocks,
    ship_page,
    paged_cache,
    block_table,
    cache_len,
    step_embed,
    norm_gain,
    query_weight,
    keyvalue_weight,
):
    column = lax.axis_index("tp")
    role = lax.axis_index("role")
    core = column % 2
    group_rows, width = text_embed.shape
    steps, rows, _ = step_embed.shape

    role_id = role.reshape(1)

    def plus(a):
        return swap(a, "tp", CORE)

    other_weight = plus(keyvalue_weight)
    weights = (query_weight, keyvalue_weight, other_weight)
    (message,) = phase(pick_rows(vision_group, vision_slot, ship_page, vision_rows))
    arrived = lax.all_to_all(message, "role", split_axis=0, concat_axis=0, tiled=True)
    steps_y = doubling(step_embed.reshape(steps * rows, width), "tp", TP_MASKS[:2])
    arrived, steps_y = phase(arrived, steps_y)
    merged, squares = land_rows(role_id, arrived, text_embed)
    text_all = lax.all_gather(merged, "tp")

    first_page = (role * TP + column) * 128
    parts = arrived[:, 64 + 2 : 64 + 4, : ship_page.shape[0]].astype(jnp.int32)
    ships = parts[:, 0] * 128 + parts[:, 1]
    page_ids = first_page + jnp.arange(paged_cache.shape[0], dtype=jnp.int32)
    held_count = page_ids.shape[0]
    row_of, live_of = find_pages(
        block_table, cache_len, jnp.concatenate([page_ids, ships.reshape(-1)])
    )
    codes = jnp.concatenate(
        [
            row_of[held_count:].reshape(4, 128),
            live_of[held_count:].reshape(4, 128),
            jnp.zeros((8, 128), jnp.int32),
        ],
        axis=0,
    ).astype(BF)
    steps_all = more(more(steps_y, "tp", TP_MASKS[2]), "tp", CORE)
    step_q, step_a, step_b = step_project(
        (column // 4) ^ jnp.array([0, 1, 3, 2], jnp.int32),
        (column % 4).reshape(1),
        steps_all,
        norm_gain,
        *weights,
    )
    new_keys = jnp.where(core == 0, step_a, step_b)
    new_values = jnp.where(core == 0, step_b, step_a)
    own_queries = (
        step_q.reshape(steps, rows, 4, HEAD_SIZE).transpose(1, 0, 2, 3).reshape(rows * 16, HEAD_SIZE)
    )
    own_queries, squares, codes = phase(own_queries, squares, codes)

    query_all = doubling(jnp.concatenate([own_queries, squares], axis=0), "tp", TP_MASKS)
    replaced = jnp.any(ships.reshape(1, -1) == page_ids[:, None], axis=1)
    first_chunk, slot_page, slot_live = page_tables(
        row_of[:held_count], live_of[:held_count], replaced, rows
    )
    role_message = jnp.concatenate([own_queries, codes], axis=0)
    queries_role = doubling(role_message, "role", ROLE_MASKS[:1])
    difference = column ^ jnp.arange(TP, dtype=jnp.int32)
    far_bit = difference // 8
    near_bit = (difference // 4) % 2 ^ far_bit
    where = difference // 2 % 2 + 2 * near_bit + 4 * far_bit + 8 * (difference % 2)
    held = paged_attention(first_chunk, slot_page, slot_live, where, query_all, paged_cache)
    held, queries_role = phase(held, queries_role)

    held_parts = lax.all_to_all(held, "tp", split_axis=0, concat_axis=0, tiled=True)
    sums = jnp.sum(query_all[:, 256:280, :].astype(F32), axis=0)
    ssq = sums[0:8] + sums[8:16] + sums[16:24]
    queries_role = more(more(queries_role, "role", ROLE_MASKS[1]), "role", ROLE_MASKS[2])
    role_order = role ^ jnp.array(ROLE_OFFSETS, jnp.int32)
    info = queries_role[:, 256:264, :].reshape(ROLE, 2, ROLE * ship_page.shape[0])
    info = lax.dynamic_slice_in_dim(info, role * ship_page.shape[0], ship_page.shape[0], 2)
    info = info.astype(jnp.int32)
    start, token_row = token_rows(info[:, 0], info[:, 1], ship_page, role_order)
    text_all, start, token_row, queries_role, ssq = phase(
        text_all, start, token_row, queries_role, ssq
    )

    prefill_queries, keys, values, fresh = finish_keys(
        core.reshape(1),
        start,
        role_order,
        text_all,
        ssq,
        norm_gain,
        weights,
        queries_role,
        token_row,
    )
    fresh, held_parts = phase(fresh, held_parts)
    fresh_parts = lax.all_to_all(fresh, "role", split_axis=0, concat_axis=0, tiled=True)

    prefill_out = prefill_attention(request_blocks, prefill_queries, keys, values)
    state = merge_held(held_parts, own_queries, new_keys, new_values)

    decode = merge(fresh_parts, state)
    decode_out = (
        decode.reshape(rows, steps, 4, HEAD_SIZE).transpose(1, 0, 2, 3).reshape(steps, rows, 512)
    )
    return (prefill_out, decode_out)


def solution(mesh):
    in_specs = (
        P("role", "tp"),
        P("role", "tp"),
        P("role"),
        P("role"),
        P("role", None),
        P("role"),
        P(("role", "tp"), None, None),
        P("role", None),
        P("role"),
        P(None, "role", "tp"),
        P(),
        P(None, "tp"),
        P(None, "tp"),
    )
    out_specs = (P("role", "tp"), P(None, "role", "tp"))
    return jax.shard_map(
        per_device, mesh=mesh, in_specs=in_specs, out_specs=out_specs, check_vma=False
    )
```
